128 devices in a mesh: slab: 16 (over y, x), sub: 8 (over z, core).
Axes of the slice: x: 4, y: 4, z: 4, core: 2. Of those that a mesh axis runs over, the one named last changes fastest.
Arguments:
- atom_data: float32 [65536, 4, 128], P(('slab', 'sub')), as said below
- block_cell: int32 [65536], P(('slab', 'sub')), may hold values from 0 to 65535
- send_list: int32 [128, 128, 4], P(('slab', 'sub')), may hold values from 0 to 511, as said below
- send_count: int32 [128, 128], P(('slab', 'sub')), may hold values from 0 to 4, as said below
Outputs:
- potentials: float32 [65536, 128], P(('slab', 'sub'))
- grid_potential: float32 [256, 128, 128], P('slab', 'sub')
The draws below stay inside these ranges and needn't reach their ends.
Inputs may be any that keep to these rules, and one draw needn't show every extreme that they name: `atom_data`: positions inside the cell lie in [0, 4) grid spacings; the last component is the charge. `send_count`: number of blocks that each device sends to each device. In every draw one device receives exactly 4 blocks from every device. `send_list`: entries j below send_count[d, e] name distinct blocks of sender d whose cells belong to receiver e: c_x // 4 is e's slab index and c_y // 4 its sub index. Later entries are arbitrary block numbers of the sender.
All inputs are finite; a program needn't handle non-finite values.
Results may differ from the reference program's by a relative error of at most 0.0003.
Values sent between devices are 32-bit elements; how exact they have to be, the bound alone decides.
A program may use at most 64 MiB of HBM per device.

```python
import jax
import jax.numpy as jnp
from jax import lax

GX = 16
GY = 16
GZ = 128
SLOTS = 512
BLOCK = 128
CAP = 4
NX = 256
NY = 128
CELLS = 65536
ATOM_BLOCKS = 65536
N_SUB = 8
DEVICES = 128


def plan_blocks(key):
    streams = jax.random.split(key, 8)
    hottest = jax.random.randint(streams[0], (), 0, DEVICES)
    target = jnp.arange(DEVICES)
    counts = jax.random.randint(streams[1], (DEVICES, DEVICES), 0, CAP + 1)
    counts = jnp.where(target[None, :] == hottest, CAP, counts)
    counts = counts.at[0, DEVICES - 1].set(jnp.maximum(counts[0, DEVICES - 1], 1))
    orders = jax.vmap(lambda sub_key: jax.random.permutation(sub_key, SLOTS))(jax.random.split(streams[2], DEVICES))
    starts = jnp.cumsum(counts, axis=1) - counts
    slot_index = jnp.arange(CAP)
    position = starts[:, :, None] + slot_index[None, None, :]
    present = slot_index[None, None, :] < counts[:, :, None]
    clipped = jnp.minimum(position, SLOTS - 1).reshape(DEVICES, DEVICES * CAP)
    chosen = jnp.take_along_axis(orders, clipped, axis=1).reshape(DEVICES, DEVICES, CAP)
    spare = jax.random.randint(streams[3], (DEVICES, DEVICES, CAP), 0, SLOTS)
    listing = jnp.where(present, chosen, spare)
    cell_x = jax.random.randint(streams[4], (DEVICES, DEVICES, CAP), 0, GX // 4)
    cell_y = jax.random.randint(streams[5], (DEVICES, DEVICES, CAP), 0, GY // 4)
    cell_z = jax.random.randint(streams[6], (DEVICES, DEVICES, CAP), 0, GZ // 4)
    corner = (target == 0)[:, None, None] & (target == DEVICES - 1)[None, :, None] & (slot_index == 0)[None, None, :]
    cell_x = jnp.where(corner, GX // 4 - 1, cell_x)
    cell_y = jnp.where(corner, GY // 4 - 1, cell_y)
    cell_z = jnp.where(corner, GZ // 4 - 1, cell_z)
    slab_of = (target // N_SUB)[None, :, None]
    sub_of = (target % N_SUB)[None, :, None]
    global_cell = ((slab_of * (GX // 4) + cell_x) * (NY // 4) + sub_of * (GY // 4) + cell_y) * (GZ // 4) + cell_z
    background = jax.random.randint(streams[7], (DEVICES, SLOTS), 0, CELLS)
    senders = jnp.broadcast_to(target[:, None, None], listing.shape)
    cell_table = background.at[senders, jnp.where(present, listing, SLOTS)].set(global_cell, mode='drop')
    return (counts, listing, cell_table.reshape(DEVICES * SLOTS))


def draw_send_count(key, part):
    return plan_blocks(key)[0]


def draw_send_list(key, part):
    return plan_blocks(key)[1]


def draw_block_cell(key, part):
    return plan_blocks(key)[2]


def draw_atom_data(key, part):
    key = jax.random.fold_in(key, 17)
    key_place, key_charge = jax.random.split(key, 2)
    located = 4.0 * jax.random.uniform(key_place, (ATOM_BLOCKS, 3, BLOCK), jnp.float32)
    charge = 0.3 * jax.random.normal(key_charge, (ATOM_BLOCKS, 1, BLOCK), jnp.float32)
    return jnp.concatenate([located, charge], axis=1)


def setup_inputs(seed: int = 0) -> dict:
    key_of = jax.random.split(jax.random.key(seed), 5)
    return {
        "atom_data": draw_atom_data(jax.random.fold_in(key_of[4], 71), 0),
        "block_cell": draw_block_cell(jax.random.fold_in(key_of[4], 71), 0),
        "send_list": draw_send_list(jax.random.fold_in(key_of[4], 71), 0),
        "send_count": draw_send_count(jax.random.fold_in(key_of[4], 71), 0),
    }


PRECISE = lax.Precision.HIGHEST
RESTRICTION = (-0.0625, 0.0, 0.5625, 1.0, 0.5625, 0.0, -0.0625)

def spline(offset):
    magnitude = jnp.abs(offset)
    central = (1.0 - magnitude) * (1.0 + magnitude - 1.5 * magnitude * magnitude)
    flank = -0.5 * (magnitude - 1.0) * (2.0 - magnitude) * (2.0 - magnitude)
    return jnp.where(magnitude <= 1.0, central, jnp.where(magnitude < 2.0, flank, 0.0))

def soften(scaled):
    square = scaled * scaled
    central = (15.0 - 10.0 * square + 3.0 * square * square) / 8.0
    return jnp.where(scaled < 1.0, central, 1.0 / jnp.maximum(scaled, 1.0))

def split_kernel(distance):
    return soften(distance / 2.0) / 2.0 - soften(distance / 4.0) / 4.0

def block_weights(blocks):
    offsets = jnp.arange(7).astype(jnp.float32) - 1.0
    weights = spline(blocks[:, 0:3, :, None] - offsets)
    charged = blocks[:, 3, :, None] * weights[:, 0]
    across = weights[:, 1, :, :, None] * weights[:, 2, :, None, :]
    return (charged, across.reshape(blocks.shape[0], blocks.shape[2], 49), weights[:, 0])

def placement(cell_count, length):
    cell_index = jnp.arange(cell_count)[:, None, None]
    offset = jnp.arange(7)[None, :, None]
    points = jnp.arange(length)[None, None, :]
    return ((4 * cell_index + offset - 1) % length == points).astype(jnp.float32)

def deposit(patches, along_x, along_y, along_z):
    partial_value = jnp.einsum('abcijk,ckz->abijz', patches, along_z, precision=PRECISE)
    partial_value = jnp.einsum('abijz,bjy->aiyz', partial_value, along_y, precision=PRECISE)
    return jnp.einsum('aiyz,aix->xyz', partial_value, along_x, precision=PRECISE)

def collect(lattice, along_x, along_y, along_z):
    partial_value = jnp.einsum('xyz,ckz->xyck', lattice, along_z, precision=PRECISE)
    partial_value = jnp.einsum('xyck,bjy->xbjck', partial_value, along_y, precision=PRECISE)
    partial_value = jnp.einsum('xbjck,aix->aibjck', partial_value, along_x, precision=PRECISE)
    return partial_value.transpose(0, 2, 4, 1, 3, 5)

def short_range(lattice, scale):
    result = jnp.zeros_like(lattice)
    for i in range(-3, 4):
        for j in range(-3, 4):
            for k in range(-3, 4):
                weight = scale * split_kernel(jnp.sqrt(jnp.asarray(i * i + j * j + k * k).astype(jnp.float32)))
                result = result + weight * jnp.roll(lattice, (i, j, k), axis=(0, 1, 2))
    return result

def restrict(lattice):
    for dimension in range(3):
        summed = jnp.zeros_like(lattice)
        for m in (-3, -1, 0, 1, 3):
            summed = summed + RESTRICTION[m + 3] * jnp.roll(lattice, -m, dimension)
        lattice = lax.slice_in_dim(summed, 0, summed.shape[dimension], 2, dimension)
    return lattice

def prolong(lattice):
    for dimension in range(3):
        enlarged = list(lattice.shape)
        enlarged[dimension] = 2 * enlarged[dimension]
        stuffed = jnp.zeros(enlarged, lattice.dtype)
        selector = [slice(None)] * 3
        selector[dimension] = slice(0, None, 2)
        stuffed = stuffed.at[tuple(selector)].set(lattice)
        summed = jnp.zeros_like(stuffed)
        for m in (-3, -1, 0, 1, 3):
            summed = summed + RESTRICTION[m + 3] * jnp.roll(stuffed, m, dimension)
        lattice = summed
    return lattice

def coarsest(charges):
    squared = jnp.zeros(charges.shape, jnp.float32)
    for dimension in range(3):
        length = charges.shape[dimension]
        offsets = (jnp.arange(length) + length // 2) % length - length // 2
        enlarged = [1, 1, 1]
        enlarged[dimension] = length
        squared = squared + (offsets * offsets).astype(jnp.float32).reshape(enlarged)
    kernel = soften(jnp.sqrt(squared) / 2.0) / 8.0
    spectrum = jnp.fft.rfftn(charges) * jnp.fft.rfftn(kernel)
    return jnp.fft.irfftn(spectrum, s=charges.shape).astype(jnp.float32)

def reference(atom_data, block_cell, send_list, send_count):
    cells_x, cells_y, cells_z = (NX // 4, NY // 4, GZ // 4)
    slot_index = jnp.arange(CAP)
    first_rows = jnp.arange(DEVICES)[:, None] * SLOTS

    def receive(target):
        block_rows = (first_rows + send_list[:, target, :]).reshape(-1)
        present = (slot_index[None, :] < send_count[:, target][:, None]).reshape(-1)
        blocks = jnp.where(present[:, None, None], atom_data[block_rows], 0.0)
        return (blocks, block_cell[block_rows], present)

    def spread(accumulated, target):
        blocks, cell_ids, present = receive(target)
        charged, across, _ = block_weights(blocks)
        patches = jnp.einsum('sbp,sbk->spk', charged, across, precision=PRECISE).reshape(SLOTS, 343)
        return (accumulated + jax.ops.segment_sum(patches, cell_ids, num_segments=CELLS), None)
    cell_charge, _ = lax.scan(spread, jnp.zeros((CELLS, 343), jnp.float32), jnp.arange(DEVICES))
    along_x = placement(cells_x, NX)
    along_y = placement(cells_y, NY)
    along_z = placement(cells_z, GZ)
    fine_charge = deposit(cell_charge.reshape(cells_x, cells_y, cells_z, 7, 7, 7), along_x, along_y, along_z)
    middle_charge = restrict(fine_charge)
    top_charge = restrict(middle_charge)
    middle_potential = short_range(middle_charge, 0.5) + prolong(coarsest(top_charge))
    grid_potential = short_range(fine_charge, 1.0) + prolong(middle_potential)
    cell_potential = collect(grid_potential, along_x, along_y, along_z).reshape(CELLS, 7, 49)

    def interpolate(target):
        blocks, cell_ids, present = receive(target)
        _, across, along_first = block_weights(blocks)
        partial_value = jnp.einsum('sbp,spk->sbk', along_first, cell_potential[cell_ids], precision=PRECISE)
        return jnp.where(present[:, None], lax.optimization_barrier(jnp.sum(partial_value * across, axis=2)), 0.0)
    potentials = lax.map(interpolate, jnp.arange(DEVICES)).reshape(DEVICES * SLOTS, BLOCK)
    return (potentials, grid_potential)
```

```python
import functools
import math

import numpy as np
import jax
import jax.numpy as jnp
from jax import lax
from jax.experimental import pallas as pl
from jax.experimental.pallas import tpu as pltpu
from jax.sharding import PartitionSpec as P

BLOCK = 128
GROUP = 1
GROUP_BACK = 1
UNROLL = 32

GX = 16
GY = 16
GZ = 128
def spline_rows(row, offsets):
    far = jnp.maximum(2.0 - jnp.abs(row - offsets), 0.0)
    less = far - 1.0
    near = jnp.maximum(less, 0.0)
    return 0.5 * (far * far * less) + near * near * (1.0 - 2.0 * near)


def halves(values):
    high = values.astype(jnp.bfloat16)
    low = (values - high.astype(jnp.float32)).astype(jnp.bfloat16)
    return high, low


def block_rows(atoms, slot):
    offsets = lax.broadcasted_iota(jnp.int32, (8, BLOCK), 0).astype(jnp.float32) - 1.0
    return [spline_rows(atoms[pl.ds(4 * slot + d, 1), :], offsets) for d in range(3)]


def cross(first, second):
    return jnp.concatenate([first[i : i + 1, :] * second for i in range(8)], axis=0)


def spread_kernel(cells, atoms, place, out, patches):
    group = GROUP
    patches[...] = jnp.zeros_like(patches)

    def step(g, carry):
        results = []
        for h in range(UNROLL // group):
            left, right = [], []
            for t in range(group):
                slot = g * UNROLL + h * group + t
                wx, wy, wz = block_rows(atoms, slot)
                charge = atoms[pl.ds(4 * slot + 3, 1), :]
                across_high, across_low = halves(cross(wx * charge, wy))
                both = jnp.concatenate(halves(wz), axis=0)
                left.append(jnp.concatenate([both, both], axis=1))
                right.append(jnp.concatenate([across_high, across_low], axis=1))
            product = lax.dot_general(
                jnp.concatenate(left, axis=0),
                jnp.concatenate(right, axis=0),
                (((1,), (1,)), ((), ())),
                preferred_element_type=jnp.float32,
            )
            for t in range(group):
                part = product[16 * t : 16 * t + 8] + product[16 * t + 8 : 16 * t + 16]
                lane = 64 * t
                part = part[:, lane // 128 * 128 : lane // 128 * 128 + 128] if group > 1 else part
                if lane % 128:
                    part = pltpu.roll(part, 64, 1)
                results.append((g * UNROLL + h * group + t, part))
        for slot, part in results:
            cell = cells[slot // 4, lax.rem(slot, 4)]
            if part.shape[1] == 64:
                patches[cell, :, 0:64] += part
            else:
                patches[cell] += part
        return carry

    lax.fori_loop(0, cells.shape[0] * 4 // UNROLL, step, 0)
    out[...] = jnp.zeros_like(out)
    for a in range(4):
        for b in range(4):
            first = (a * 4 + b) * 32
            column = patches[first : first + 32].reshape(256, 128)
            high, low = halves(column.T)
            planes = jnp.dot(high, place[...], preferred_element_type=jnp.float32) + jnp.dot(
                low, place[...], preferred_element_type=jnp.float32
            )
            for i in range(7):
                out[4 * a + i, 4 * b : 4 * b + 8, :] += planes[8 * i : 8 * i + 8]


def gather_kernel(cells, atoms, lattice, place, out, table):
    group = GROUP_BACK
    place_back = place[...]
    for a in range(4):
        for b in range(4):
            rows = jnp.concatenate(
                [lattice[4 * a + i, 4 * b : 4 * b + 8, :] for i in range(7)] + [jnp.zeros((8, 128), jnp.float32)], axis=0
            )
            high, low = halves(rows)
            forms = (((1,), (1,)), ((), ()))
            column = lax.dot_general(place_back, high, forms, preferred_element_type=jnp.float32) + lax.dot_general(
                place_back, low, forms, preferred_element_type=jnp.float32
            )
            first = (a * 4 + b) * 32
            high, low = halves(column.reshape(32, 8, 64))
            pair = jnp.concatenate([high, low], axis=1)
            table[first : first + 32] = jnp.concatenate([pair, pair], axis=2)
    table[512] = jnp.zeros((16, 128), jnp.bfloat16)

    def step(g, carry):
        for h in range(UNROLL // group):
            left, right, along = [], [], []
            for t in range(group):
                slot = g * UNROLL + h * group + t
                wx, wy, wz = block_rows(atoms, slot)
                right.extend(halves(cross(wx, wy)))
                along.append(wz)
                pair = table[cells[slot // 4, lax.rem(slot, 4)]]
                zero = jnp.zeros_like(pair)
                left.append(jnp.concatenate([pair if n == t else zero for n in range(group)], axis=1))
            product = jnp.dot(
                jnp.concatenate(left, axis=0), jnp.concatenate(right, axis=0), preferred_element_type=jnp.float32
            )
            for t in range(group):
                part = product[16 * t : 16 * t + 8] + product[16 * t + 8 : 16 * t + 16]
                out[pl.ds(g * UNROLL + h * group + t, 1), :] = jnp.sum(part * along[t], axis=0, keepdims=True)
        return carry

    lax.fori_loop(0, cells.shape[0] * 4 // UNROLL, step, 0)

SMEM = pl.BlockSpec(memory_space=pltpu.SMEM)
VMEM = pl.BlockSpec(memory_space=pltpu.VMEM)
ANY = pl.BlockSpec(memory_space=pl.ANY)
MESH = pl.DeviceIdType.MESH


def exchange_kernel(devices, sub_count, chosen, counts, cells, atoms, out, out_cells, held, send, send_cells, *sems):
    load_sem, own_sem, own_cell_sem, sent, landed, sent_cells, landed_cells = sems
    me = lax.axis_index("slab") * sub_count + lax.axis_index("sub")
    load = pltpu.make_async_copy(atoms, held, load_sem)
    load.start()
    barrier = pltpu.get_barrier_semaphore()

    def place_of(step):
        peer = lax.rem(me + step, devices)
        return peer, (peer // sub_count, lax.rem(peer, sub_count))

    def greet(step, carry):
        pl.semaphore_signal(barrier, inc=1, device_id=place_of(step)[1], device_id_type=MESH)
        return carry

    lax.fori_loop(1, devices, greet, 0)
    load.wait()
    lane = lax.broadcasted_iota(jnp.int32, (1, BLOCK), 1)

    def pick(peer, carry):
        row = jnp.full((1, BLOCK), 512, jnp.int32)
        for j in range(4):
            index = chosen[peer, j]
            send[peer, pl.ds(4 * j, 4), :] = held[index]
            cell = cells[index]
            local = ((cell >> 10) & 3) * 128 + ((cell >> 5) & 3) * 32 + (cell & 31)
            row = jnp.where(lane == j, jnp.where(counts[0, peer] > j, local, 512), row)
        send_cells[peer] = row
        return carry

    lax.fori_loop(0, devices, pick, 0)
    pl.semaphore_wait(barrier, devices - 1)

    def start(step, carry):
        peer, target = place_of(step)
        pltpu.make_async_remote_copy(
            send_cells.at[peer], out_cells.at[me], sent_cells, landed_cells, device_id=target, device_id_type=MESH
        ).start()
        pltpu.make_async_remote_copy(
            send.at[peer], out.at[me], sent, landed, device_id=target, device_id_type=MESH
        ).start()
        return carry

    lax.fori_loop(1, devices, start, 0)
    own = pltpu.make_async_copy(send.at[me], out.at[me], own_sem)
    own.start()
    own_cells = pltpu.make_async_copy(send_cells.at[me], out_cells.at[me], own_cell_sem)
    own_cells.start()
    own.wait()
    own_cells.wait()
    others = pl.ds(0, devices - 1)
    for ref, sem in ((send, sent), (out, landed), (send_cells, sent_cells), (out_cells, landed_cells)):
        pltpu.make_async_copy(ref.at[others], ref.at[others], sem).wait()


def exchange(chosen, counts, cells, atoms, devices, sub_count):
    return pl.pallas_call(
        functools.partial(exchange_kernel, devices, sub_count),
        out_shape=(
            jax.ShapeDtypeStruct((devices, 16, BLOCK), jnp.float32),
            jax.ShapeDtypeStruct((devices, 1, BLOCK), jnp.int32),
        ),
        in_specs=[SMEM, SMEM, SMEM, ANY],
        out_specs=(ANY, ANY),
        scratch_shapes=[
            pltpu.VMEM(atoms.shape, jnp.float32),
            pltpu.VMEM((devices, 16, BLOCK), jnp.float32),
            pltpu.VMEM((devices, 1, BLOCK), jnp.int32),
        ]
        + [pltpu.SemaphoreType.DMA] * 7,
        compiler_params=pltpu.CompilerParams(collective_id=0, has_side_effects=True, vmem_limit_bytes=32 << 20),
        name="exchange",
    )(chosen, counts, cells, atoms)


def placement_table():
    table = np.zeros((256, GZ), np.float32)
    for c in range(32):
        for k in range(7):
            table[8 * c + k, (4 * c + k - 1) % GZ] = 1.0
    return jnp.asarray(table, jnp.bfloat16)


def spread(cells, atoms, place):
    return pl.pallas_call(
        spread_kernel,
        out_shape=jax.ShapeDtypeStruct((19, 24, GZ), jnp.float32),
        in_specs=[SMEM, VMEM, VMEM],
        out_specs=VMEM,
        scratch_shapes=[pltpu.VMEM((513, 8, 128), jnp.float32)],
        compiler_params=pltpu.CompilerParams(vmem_limit_bytes=32 << 20),
        name="spread",
    )(cells, atoms, place)


def interpolate(cells, atoms, lattice, place):
    return pl.pallas_call(
        gather_kernel,
        out_shape=jax.ShapeDtypeStruct((atoms.shape[0] // 4, BLOCK), jnp.float32),
        in_specs=[SMEM, VMEM, VMEM, VMEM],
        out_specs=VMEM,
        scratch_shapes=[pltpu.VMEM((513, 16, 128), jnp.bfloat16)],
        compiler_params=pltpu.CompilerParams(vmem_limit_bytes=32 << 20),
        name="interpolate",
    )(cells, atoms, lattice, place)

PRECISE = lax.Precision.HIGHEST


def padded(cells, sides, width):
    for axis, dim in sides:
        count = lax.axis_size(axis)
        head = lax.slice_in_dim(cells, 0, width, axis=dim)
        tail = lax.slice_in_dim(cells, cells.shape[dim] - width, cells.shape[dim], axis=dim)
        cells = jnp.concatenate(
            [
                lax.ppermute(tail, axis, [(i, (i + 1) % count) for i in range(count)]),
                cells,
                lax.ppermute(head, axis, [((i + 1) % count, i) for i in range(count)]),
            ],
            axis=dim,
        )
    return cells


def spline(offset):
    magnitude = jnp.abs(offset)
    central = (1.0 - magnitude) * (1.0 + magnitude - 1.5 * magnitude * magnitude)
    flank = -0.5 * (magnitude - 1.0) * (2.0 - magnitude) * (2.0 - magnitude)
    return jnp.where(magnitude <= 1.0, central, jnp.where(magnitude < 2.0, flank, 0.0))


def soften(scaled):
    square = scaled * scaled
    central = (15.0 - 10.0 * square + 3.0 * square * square) / 8.0
    return jnp.where(scaled < 1.0, central, 1.0 / jnp.maximum(scaled, 1.0))


def split_kernel(distance):
    return soften(distance / 2.0) / 2.0 - soften(distance / 4.0) / 4.0


def block_weights(blocks):
    offsets = jnp.arange(7).astype(jnp.float32) - 1.0
    weights = spline(blocks[:, 0:3, :, None] - offsets)
    charged = blocks[:, 3, :, None] * weights[:, 0]
    across = weights[:, 1, :, :, None] * weights[:, 2, :, None, :]
    return (charged, across.reshape(blocks.shape[0], blocks.shape[2], 49), weights[:, 0])


def restriction_weight(offset):
    magnitude = jnp.abs(offset)
    chosen = jnp.where(magnitude == 1, 0.5625, jnp.where(magnitude == 3, -0.0625, 0.0))
    return jnp.where(magnitude == 0, 1.0, chosen).astype(jnp.float32)


def wrapped(offset, length):
    return (offset + length // 2) % length - length // 2


def window_restrict(coarse_count, fine_count, margin):
    coarse_index = jnp.arange(coarse_count)[:, None]
    fine_index = jnp.arange(fine_count)[None, :]
    return restriction_weight(fine_index - 2 * coarse_index - margin)


def periodic_restrict(coarse_count, fine_count):
    coarse_index = jnp.arange(coarse_count)[:, None]
    fine_index = jnp.arange(fine_count)[None, :]
    return restriction_weight(wrapped(fine_index - 2 * coarse_index, fine_count))


def window_prolong(fine_count, coarse_count, shift):
    fine_index = jnp.arange(fine_count)[:, None]
    coarse_index = jnp.arange(coarse_count)[None, :]
    return restriction_weight(fine_index - 2 * coarse_index + shift)


def periodic_prolong(fine_count, coarse_count):
    return periodic_restrict(coarse_count, fine_count).T


def separable(lattice, along_x, along_y, along_z):
    partial_value = jnp.einsum("xyz,wz->xyw", lattice, along_z, precision=PRECISE)
    partial_value = jnp.einsum("xyw,vy->xvw", partial_value, along_y, precision=PRECISE)
    return jnp.einsum("xvw,ux->uvw", partial_value, along_x, precision=PRECISE)


def window_placement(cell_count, length):
    cell_index = jnp.arange(cell_count)[:, None, None]
    offset = jnp.arange(7)[None, :, None]
    points = jnp.arange(length)[None, None, :]
    return (4 * cell_index + offset + 1 == points).astype(jnp.float32)


def periodic_placement(cell_count, length):
    cell_index = jnp.arange(cell_count)[:, None, None]
    offset = jnp.arange(7)[None, :, None]
    points = jnp.arange(length)[None, None, :]
    return ((4 * cell_index + offset - 1) % length == points).astype(jnp.float32)


def deposit(patches, along_x, along_y, along_z):
    partial_value = jnp.einsum("abcijk,ckz->abijz", patches, along_z, precision=PRECISE)
    partial_value = jnp.einsum("abijz,bjy->aiyz", partial_value, along_y, precision=PRECISE)
    return jnp.einsum("aiyz,aix->xyz", partial_value, along_x, precision=PRECISE)


def collect(lattice, along_x, along_y, along_z):
    partial_value = jnp.einsum("xyz,ckz->xyck", lattice, along_z, precision=PRECISE)
    partial_value = jnp.einsum("xyck,bjy->xbjck", partial_value, along_y, precision=PRECISE)
    partial_value = jnp.einsum("xbjck,aix->aibjck", partial_value, along_x, precision=PRECISE)
    return partial_value.transpose(0, 2, 4, 1, 3, 5)


def stencil_tables(length, scale):
    source_z = jnp.arange(length)[:, None]
    target_z = jnp.arange(length)[None, :]
    shift_z = wrapped(target_z - source_z, length)
    nearby = jnp.abs(shift_z) <= 3
    planes = []
    for i in range(-3, 4):
        column = []
        for j in range(-3, 4):
            distance = jnp.sqrt((i * i + j * j + shift_z * shift_z).astype(jnp.float32))
            column.append(jnp.where(nearby, scale * split_kernel(distance), 0.0))
        planes.append(jnp.stack(column))
    return jnp.stack(planes)


def short_range(lattice, tables, rows_out, columns_out):
    result = 0.0
    for i in range(7):
        stacked = jnp.stack(
            [lattice[6 - i : 6 - i + rows_out, 6 - j : 6 - j + columns_out] for j in range(7)]
        )
        result = result + jnp.einsum("kxyz,kzw->xyw", stacked, tables[i], precision=PRECISE)
    return result


def pad_along(values, dimension, lower, upper):
    widths = [(0, 0)] * values.ndim
    widths[dimension] = (lower, upper)
    return jnp.pad(values, widths)


def fold_rims(extended, dimension, inner):
    lower_rim = lax.slice_in_dim(extended, 0, 7, axis=dimension)
    owned = lax.slice_in_dim(extended, 7, inner + 11, axis=dimension)
    upper_rim = lax.slice_in_dim(extended, inner + 11, inner + 18, axis=dimension)
    summed = pad_along(owned, dimension, 3, 3) + pad_along(lower_rim, dimension, 0, inner + 3)
    return summed + pad_along(upper_rim, dimension, inner + 3, 0)


def wave_tables(length):
    index = jnp.arange(length)
    angle = 2.0 * math.pi / length * (index[:, None] * index[None, :] % length).astype(jnp.float32)
    return (jnp.cos(angle), jnp.sin(angle))


def along_axis(values, table, dimension):
    forms = ("xyz,ax->ayz", "xyz,ay->xaz", "xyz,az->xya")
    return jnp.einsum(forms[dimension], values, table, precision=PRECISE)


def periodic_convolve(grid):
    extents = grid.shape
    squared = 0.0
    tables = []
    for dimension in range(3):
        length = extents[dimension]
        shape = [1, 1, 1]
        shape[dimension] = length
        offset = wrapped(jnp.arange(length), length).astype(jnp.float32)
        squared = squared + (offset * offset).reshape(shape)
        tables.append(wave_tables(length))
    spectrum = soften(jnp.sqrt(squared) / 2.0) / 8.0
    for dimension in range(3):
        spectrum = along_axis(spectrum, tables[dimension][0], dimension)
    real_part = grid
    imag_part = jnp.zeros_like(grid)
    for dimension in range(3):
        cosine, sine = tables[dimension]
        real_next = along_axis(real_part, cosine, dimension) + along_axis(
            imag_part, sine, dimension
        )
        imag_part = along_axis(imag_part, cosine, dimension) - along_axis(
            real_part, sine, dimension
        )
        real_part = real_next
    real_part = real_part * spectrum
    imag_part = imag_part * spectrum
    for dimension in range(3):
        cosine, sine = tables[dimension]
        real_next = along_axis(real_part, cosine, dimension) - along_axis(
            imag_part, sine, dimension
        )
        imag_part = along_axis(imag_part, cosine, dimension) + along_axis(
            real_part, sine, dimension
        )
        real_part = real_next
    return real_part / float(extents[0] * extents[1] * extents[2])


def body(atom_data, block_cell, send_list, send_count):
    slab_count = lax.axis_size("slab")
    sub_count = lax.axis_size("sub")
    slab_at = lax.axis_index("slab")
    sub_at = lax.axis_index("sub")
    place = placement_table()
    arrived, arrived_cells = exchange(
        send_list[0], send_count, block_cell, atom_data, slab_count * sub_count, sub_count
    )
    arrived = arrived.reshape(-1, BLOCK)
    arrived_cells = arrived_cells.reshape(-1, BLOCK)
    partial_charge = jnp.pad(spread(arrived_cells, arrived, place)[:, :19], ((1, 0), (1, 0), (0, 0)))
    extended = padded(partial_charge, (("slab", 0), ("sub", 1)), 7)
    fine_charge = fold_rims(fold_rims(extended, 0, GX), 1, GY)
    fine_short = short_range(fine_charge, stencil_tables(GZ, 1.0), GX + 4, GY + 4)
    middle_charge = separable(
        fine_charge,
        window_restrict(GX // 2, GX + 10, 5),
        window_restrict(GY // 2, GY + 10, 5),
        periodic_restrict(GZ // 2, GZ),
    )
    middle_wide = padded(middle_charge, (("slab", 0), ("sub", 1)), 6)
    top_charge = separable(
        middle_wide,
        window_restrict(GX // 4, GX // 2 + 12, 6),
        window_restrict(GY // 4, GY // 2 + 12, 6),
        periodic_restrict(GZ // 4, GZ // 2),
    )
    middle_short = short_range(middle_wide, stencil_tables(GZ // 2, 0.5), GX // 2 + 6, GY // 2 + 6)
    tile_x, tile_y, tile_z = (GX // 4, GY // 4, GZ // 4)
    per_shard = tile_x * tile_y * tile_z
    extent_x, extent_y = (tile_x * slab_count, tile_y * sub_count)
    flat_top = lax.all_gather(top_charge.reshape(per_shard), ("slab", "sub"), axis=0, tiled=True)
    whole_top = (
        flat_top.reshape(slab_count, sub_count, tile_x, tile_y, tile_z)
        .transpose(0, 2, 1, 3, 4)
        .reshape(extent_x, extent_y, tile_z)
    )
    everything = periodic_convolve(whole_top)
    rows_x = (slab_at * tile_x - 3 + jnp.arange(tile_x + 6)) % extent_x
    rows_y = (sub_at * tile_y - 3 + jnp.arange(tile_y + 6)) % extent_y
    top_potential = jnp.take(jnp.take(everything, rows_x, axis=0), rows_y, axis=1)
    middle_potential = middle_short + separable(
        top_potential,
        window_prolong(GX // 2 + 6, GX // 4 + 6, 3),
        window_prolong(GY // 2 + 6, GY // 4 + 6, 3),
        periodic_prolong(GZ // 2, GZ // 4),
    )
    grid_wide = fine_short + separable(
        middle_potential,
        window_prolong(GX + 4, GX // 2 + 6, 4),
        window_prolong(GY + 4, GY // 2 + 6, 4),
        periodic_prolong(GZ, GZ // 2),
    )
    potentials = interpolate(
        arrived_cells, arrived, jnp.pad(grid_wide[1:20, 1:20], ((0, 0), (0, 5), (0, 0))), place
    )
    return (potentials, grid_wide[2 : GX + 2, 2 : GY + 2])


def solution(mesh):
    placed = (
        P(("slab", "sub"), None, None),
        P(("slab", "sub")),
        P(("slab", "sub"), None, None),
        P(("slab", "sub"), None),
    )
    return jax.shard_map(
        body,
        mesh=mesh,
        in_specs=placed,
        out_specs=(P(("slab", "sub"), None), P("slab", "sub", None)),
        check_vma=False,
    )
```

```python
import functools
import ml_dtypes
import numpy as np
import jax
import jax.numpy as jnp
from jax import lax
from jax.experimental import pallas as pl
from jax.experimental.pallas import tpu as pltpu
from jax.sharding import PartitionSpec as P

BLOCK = 128
GROUP = 1
GROUP_BACK = 1
UNROLL = 32

GX = 16
GY = 16
GZ = 128
def spline_rows(row, offsets):
    far = jnp.maximum(2.0 - jnp.abs(row - offsets), 0.0)
    less = far - 1.0
    near = jnp.maximum(less, 0.0)
    return 0.5 * (far * far * less) + near * near * (1.0 - 2.0 * near)


def halves(values):
    high = values.astype(jnp.bfloat16)
    low = (values - high.astype(jnp.float32)).astype(jnp.bfloat16)
    return high, low


def block_rows(atoms, slot):
    offsets = lax.broadcasted_iota(jnp.int32, (8, BLOCK), 0).astype(jnp.float32) - 1.0
    return [spline_rows(atoms[pl.ds(4 * slot + d, 1), :], offsets) for d in range(3)]


def cross(first, second):
    return jnp.concatenate([first[i : i + 1, :] * second for i in range(8)], axis=0)


def spread_kernel(cells, atoms, place, out, patches):
    group = GROUP
    patches[...] = jnp.zeros_like(patches)

    def step(g, carry):
        results = []
        for h in range(UNROLL // group):
            left, right = [], []
            for t in range(group):
                slot = g * UNROLL + h * group + t
                wx, wy, wz = block_rows(atoms, slot)
                charge = atoms[pl.ds(4 * slot + 3, 1), :]
                across_high, across_low = halves(cross(wx * charge, wy))
                both = jnp.concatenate(halves(wz), axis=0)
                left.append(jnp.concatenate([both, both], axis=1))
                right.append(jnp.concatenate([across_high, across_low], axis=1))
            product = lax.dot_general(
                jnp.concatenate(left, axis=0),
                jnp.concatenate(right, axis=0),
                (((1,), (1,)), ((), ())),
                preferred_element_type=jnp.float32,
            )
            for t in range(group):
                part = product[16 * t : 16 * t + 8] + product[16 * t + 8 : 16 * t + 16]
                lane = 64 * t
                part = part[:, lane // 128 * 128 : lane // 128 * 128 + 128] if group > 1 else part
                if lane % 128:
                    part = pltpu.roll(part, 64, 1)
                results.append((g * UNROLL + h * group + t, part))
        for slot, part in results:
            cell = cells[slot // 4, lax.rem(slot, 4)]
            if part.shape[1] == 64:
                patches[cell, :, 0:64] += part
            else:
                patches[cell] += part
        return carry

    lax.fori_loop(0, cells.shape[0] * 4 // UNROLL, step, 0)
    out[...] = jnp.zeros_like(out)
    for a in range(4):
        for b in range(4):
            first = (a * 4 + b) * 32
            column = patches[first : first + 32].reshape(256, 128)
            high, low = halves(column.T)
            planes = jnp.dot(high, place[...], preferred_element_type=jnp.float32) + jnp.dot(
                low, place[...], preferred_element_type=jnp.float32
            )
            for i in range(7):
                out[4 * a + i, 4 * b : 4 * b + 8, :] += planes[8 * i : 8 * i + 8]


def gather_kernel(cells, atoms, lattice, place, out, grid, table):
    group = GROUP_BACK
    grid[...] = lattice[1:17, 1:17, :]
    place_back = place[...]
    for a in range(4):
        for b in range(4):
            rows = jnp.concatenate(
                [lattice[4 * a + i, 4 * b : 4 * b + 8, :] for i in range(7)] + [jnp.zeros((8, 128), jnp.float32)], axis=0
            )
            high, low = halves(rows)
            forms = (((1,), (1,)), ((), ()))
            column = lax.dot_general(place_back, high, forms, preferred_element_type=jnp.float32) + lax.dot_general(
                place_back, low, forms, preferred_element_type=jnp.float32
            )
            first = (a * 4 + b) * 32
            high, low = halves(column.reshape(32, 8, 64))
            pair = jnp.concatenate([high, low], axis=1)
            table[first : first + 32] = jnp.concatenate([pair, pair], axis=2)
    table[512] = jnp.zeros((16, 128), jnp.bfloat16)

    def step(g, carry):
        for h in range(UNROLL // group):
            left, right, along = [], [], []
            for t in range(group):
                slot = g * UNROLL + h * group + t
                wx, wy, wz = block_rows(atoms, slot)
                right.extend(halves(cross(wx, wy)))
                along.append(wz)
                pair = table[cells[slot // 4, lax.rem(slot, 4)]]
                zero = jnp.zeros_like(pair)
                left.append(jnp.concatenate([pair if n == t else zero for n in range(group)], axis=1))
            product = jnp.dot(
                jnp.concatenate(left, axis=0), jnp.concatenate(right, axis=0), preferred_element_type=jnp.float32
            )
            for t in range(group):
                part = product[16 * t : 16 * t + 8] + product[16 * t + 8 : 16 * t + 16]
                out[pl.ds(g * UNROLL + h * group + t, 1), :] = jnp.sum(part * along[t], axis=0, keepdims=True)
        return carry

    lax.fori_loop(0, cells.shape[0] * 4 // UNROLL, step, 0)

SMEM = pl.BlockSpec(memory_space=pltpu.SMEM)
VMEM = pl.BlockSpec(memory_space=pltpu.VMEM)
ANY = pl.BlockSpec(memory_space=pl.ANY)
MESH = pl.DeviceIdType.MESH


def exchange_kernel(devices, sub_count, chosen, counts, cells, atoms, out, out_cells, held, send, send_cells, *sems):
    load_sem, own_sem, own_cell_sem, sent, landed, sent_cells, landed_cells = sems
    me = lax.axis_index("slab") * sub_count + lax.axis_index("sub")
    load = pltpu.make_async_copy(atoms, held, load_sem)
    load.start()
    barrier = pltpu.get_barrier_semaphore()

    def place_of(step):
        peer = lax.rem(me + step, devices)
        return peer, (peer // sub_count, lax.rem(peer, sub_count))

    def greet(step, carry):
        pl.semaphore_signal(barrier, inc=1, device_id=place_of(step)[1], device_id_type=MESH)
        return carry

    lax.fori_loop(1, devices, greet, 0)
    load.wait()
    lane = lax.broadcasted_iota(jnp.int32, (1, BLOCK), 1)

    def pick(peer, carry):
        row = jnp.full((1, BLOCK), 512, jnp.int32)
        for j in range(4):
            index = chosen[peer, j]
            send[peer, pl.ds(4 * j, 4), :] = held[index]
            cell = cells[index]
            local = ((cell >> 10) & 3) * 128 + ((cell >> 5) & 3) * 32 + (cell & 31)
            row = jnp.where(lane == j, jnp.where(counts[0, peer] > j, local, 512), row)
        send_cells[peer] = row
        return carry

    lax.fori_loop(0, devices, pick, 0)
    pl.semaphore_wait(barrier, devices - 1)

    def start(step, carry):
        peer, target = place_of(step)
        pltpu.make_async_remote_copy(
            send_cells.at[peer], out_cells.at[me], sent_cells, landed_cells, device_id=target, device_id_type=MESH
        ).start()
        pltpu.make_async_remote_copy(
            send.at[peer], out.at[me], sent, landed, device_id=target, device_id_type=MESH
        ).start()
        return carry

    lax.fori_loop(1, devices, start, 0)
    own = pltpu.make_async_copy(send.at[me], out.at[me], own_sem)
    own.start()
    own_cells = pltpu.make_async_copy(send_cells.at[me], out_cells.at[me], own_cell_sem)
    own_cells.start()
    own.wait()
    own_cells.wait()
    others = pl.ds(0, devices - 1)
    for ref, sem in ((send, sent), (out, landed), (send_cells, sent_cells), (out_cells, landed_cells)):
        pltpu.make_async_copy(ref.at[others], ref.at[others], sem).wait()


def exchange(chosen, counts, cells, atoms, devices, sub_count):
    return pl.pallas_call(
        functools.partial(exchange_kernel, devices, sub_count),
        out_shape=(
            jax.ShapeDtypeStruct((devices, 16, BLOCK), jnp.float32),
            jax.ShapeDtypeStruct((devices, 1, BLOCK), jnp.int32),
        ),
        in_specs=[SMEM, SMEM, SMEM, ANY],
        out_specs=(ANY, ANY),
        scratch_shapes=[
            pltpu.VMEM(atoms.shape, jnp.float32),
            pltpu.VMEM((devices, 16, BLOCK), jnp.float32),
            pltpu.VMEM((devices, 1, BLOCK), jnp.int32),
        ]
        + [pltpu.SemaphoreType.DMA] * 7,
        compiler_params=pltpu.CompilerParams(collective_id=0, has_side_effects=True, vmem_limit_bytes=60 << 20),
        name="exchange",
    )(chosen, counts, cells, atoms)


def placement_table():
    table = np.zeros((256, GZ), np.float32)
    for c in range(32):
        for k in range(7):
            table[8 * c + k, (4 * c + k - 1) % GZ] = 1.0
    return jnp.asarray(table, jnp.bfloat16)


def spread(cells, atoms, place):
    return pl.pallas_call(
        spread_kernel,
        out_shape=jax.ShapeDtypeStruct((19, 24, GZ), jnp.float32),
        in_specs=[SMEM, VMEM, VMEM],
        out_specs=VMEM,
        scratch_shapes=[pltpu.VMEM((513, 8, 128), jnp.float32)],
        compiler_params=pltpu.CompilerParams(vmem_limit_bytes=32 << 20),
        name="spread",
    )(cells, atoms, place)


def interpolate(cells, atoms, lattice, place):
    return pl.pallas_call(
        gather_kernel,
        out_shape=(
            jax.ShapeDtypeStruct((atoms.shape[0] // 4, BLOCK), jnp.float32),
            jax.ShapeDtypeStruct((GX, GY, GZ), jnp.float32),
        ),
        in_specs=[SMEM, VMEM, VMEM, VMEM],
        out_specs=(VMEM, VMEM),
        scratch_shapes=[pltpu.VMEM((513, 16, 128), jnp.bfloat16)],
        compiler_params=pltpu.CompilerParams(vmem_limit_bytes=32 << 20),
        name="interpolate",
    )(cells, atoms, lattice, place)

def two_parts(table):
    high = table.astype(ml_dtypes.bfloat16)
    low = (table - high.astype(np.float64)).astype(ml_dtypes.bfloat16)
    return np.stack([high, low])


def stencil(offset):
    size = np.abs(offset)
    return np.where(size == 0, 1.0, np.where(size == 1, 0.5625, np.where(size == 3, -0.0625, 0.0)))


def wrapped(offset, length):
    return (offset + length // 2) % length - length // 2


def halve(coarse, fine, coarse_first, fine_first, coarse_rows, fine_rows):
    table = np.zeros((coarse_rows, fine_rows))
    k = coarse_first + np.arange(coarse)[:, None]
    table[:coarse, :fine] = stencil(fine_first + np.arange(fine)[None, :] - 2 * k)
    return table


def halve_ring(coarse):
    return stencil(wrapped(np.arange(2 * coarse)[None, :] - 2 * np.arange(coarse)[:, None], 2 * coarse))


def soften(scaled):
    square = scaled * scaled
    return np.where(scaled < 1.0, (15.0 - 10.0 * square + 3.0 * square * square) / 8.0, 1.0 / np.maximum(scaled, 1.0))


def split_kernel(distance):
    return soften(distance / 2.0) / 2.0 - soften(distance / 4.0) / 4.0


def modes(length):
    angle = 2.0 * np.pi / length * (np.arange(length)[:, None] * np.arange(length)[None, :] % length)
    return (np.cos(angle) + np.sin(angle)) / np.sqrt(length)


RINGS = [(a, b) for a in range(4) for b in range(a, 4)]


def ring_tables(length, scale):
    shift = wrapped(np.arange(length)[:, None] - np.arange(length)[None, :], length)
    out = np.zeros((len(RINGS), GZ, GZ))
    for n, (a, b) in enumerate(RINGS):
        values = scale * split_kernel(np.sqrt(a * a + b * b + shift * shift))
        out[n, :length, :length] = np.where(np.abs(shift) <= 3, values, 0.0)
    return out.reshape(len(RINGS) * GZ, GZ)


def level_tables(slabs, subs):
    exact = lambda table: table.astype(ml_dtypes.bfloat16)
    down = np.kron(halve(13, 19, -2, -1, 13, 19), halve(13, 19, -2, -1, 16, 24))
    down_z = np.zeros((GZ, GZ))
    down_z[:, :64] = halve_ring(64).T
    top_x = halve(9, 13, -2, -2, 16, 13)
    top_y = halve(9, 13, -2, -2, 9, 16)
    wave_x, wave_y, wave_z = modes(4 * slabs), modes(4 * subs), modes(32)
    reach = np.arange(9) - 2
    enter = []
    for sub in range(subs):
        rows = 4 * ((sub + np.arange(subs)[None, :]) % subs) + np.arange(4)[:, None]
        along = wave_y[rows][:, :, (4 * sub + reach) % (4 * subs)] @ top_y
        enter.append(np.einsum("jrm,xn->jrxnm", along, top_x).reshape(4 * subs * 16, 13 * 16))
    enter = np.stack(enter)
    enter_z = np.kron(np.eye(4), (wave_z @ halve_ring(32)).T)
    mode_x = np.zeros((4 * slabs, slabs, 16))
    for r in range(slabs):
        mode_x[:, r, :9] = wave_x[:, (4 * r + reach) % (4 * slabs)]
    back_x = np.zeros((16, 4 * slabs))
    back_x[:9] = wave_x[:, reach % (4 * slabs)].T
    squared = 0.0
    for dimension, length in enumerate((4 * slabs, 4 * subs, 32)):
        shape = [1, 1, 1]
        shape[dimension] = length
        squared = squared + (wrapped(np.arange(length), length) ** 2).reshape(shape)
    spectrum = np.fft.fftn(soften(np.sqrt(squared) / 2.0) / 8.0).real
    spectrum = spectrum.reshape(4 * slabs, subs, 128).transpose(1, 0, 2).astype(np.float32)
    return (
        exact(down),
        exact(down.T),
        exact(down_z),
        exact(down_z.T),
        two_parts(enter).transpose(1, 0, 2, 3),
        two_parts(enter.transpose(0, 2, 1)).transpose(1, 0, 2, 3),
        two_parts(enter_z),
        two_parts(enter_z.T),
        two_parts(mode_x.reshape(4 * slabs, slabs * 16)),
        two_parts(back_x),
        spectrum,
        two_parts(ring_tables(GZ, 1.0)),
        two_parts(ring_tables(GZ // 2, 0.5)),
    )


PER_SUB = (4, 5, 10)


def dot(a, b):
    return jnp.dot(a, b, preferred_element_type=jnp.float32)


def dot_right(values, table):
    high, low = halves(values)
    if len(table.shape) == 2:
        return dot(high, table[...]) + dot(low, table[...])
    return dot(high, table[0]) + dot(low, table[0]) + dot(high, table[1])


def dot_left(table, values):
    high, low = halves(values)
    if len(table.shape) == 2:
        return dot(table[...], high) + dot(table[...], low)
    return dot(table[0], high) + dot(table[0], low) + dot(table[1], high)


def fold_columns(lattice, columns, planes, rows):
    columns[0] = lattice[:, 3 : 3 + rows, :]
    for b in range(1, 4):
        columns[b] = lattice[:, 3 - b : 3 - b + rows, :] + lattice[:, 3 + b : 3 + b + rows, :]


def short_range(columns, table, planes, rows):
    def sides(a, b):
        if a == 0:
            return columns[b, 3 : 3 + planes]
        return columns[b, 3 - a : 3 - a + planes] + columns[b, 3 + a : 3 + a + planes]

    total = None
    for n in range(0, len(RINGS), 2):
        parts = []
        for a, b in RINGS[n : n + 2]:
            part = sides(a, b) if a == b else sides(a, b) + sides(b, a)
            parts.append(halves(part.reshape(planes * rows, GZ)))
        high, low = (jnp.concatenate([part[m] for part in parts], axis=1) for m in range(2))
        span = pl.ds(n * GZ, 2 * GZ)
        here = dot(high, table[0, span, :]) + dot(low, table[0, span, :]) + dot(high, table[1, span, :])
        total = here if total is None else total + here
    return total


SIDES = [(1, 0), (-1, 0), (0, 1), (0, -1), (1, 1), (1, -1), (-1, 1), (-1, -1)]


def levels_kernel(slabs, subs, *refs):
    partial, *tables = refs[:14]
    out = refs[14]
    rest = list(refs[15:])
    held = [rest.pop(0) for _ in range(13)]
    fine_in = [rest.pop(0) for _ in range(8)]
    middle_in = [rest.pop(0) for _ in range(8)]
    edge, middle_edge, middle, fine, middle_wide, columns, middle_columns = (rest.pop(0) for _ in range(7))
    modes_out, modes_in, line_out, line_in, back_out, back_in = (rest.pop(0) for _ in range(6))
    load_sem, fine_sent, fine_got, middle_sent, middle_got, in_sent, in_got, line_sent, line_got, back_sent, back_got = rest
    slab = lax.axis_index("slab")
    sub = lax.axis_index("sub")

    def beside(dx, dy):
        return (lax.rem(slab + dx + slabs, slabs), lax.rem(sub + dy + subs, subs))

    barrier = pltpu.get_barrier_semaphore()
    partners = [beside(r, 0) for r in range(1, slabs)] + [beside(0, r) for r in range(1, subs)]
    partners += [beside(dx, dy) for dx, dy in SIDES[4:]]
    for target in partners:
        pl.semaphore_signal(barrier, inc=1, device_id=target, device_id_type=MESH)
    loads = [
        pltpu.make_async_copy(table.at[sub] if n in PER_SUB else table, held[n], load_sem.at[n])
        for n, table in enumerate(tables)
    ]
    for load in loads:
        load.start()
    down, up, down_z, up_z, enter, leave, enter_z, leave_z, mode_x, back_x, spectrum, near, near_middle = held

    def send(source, target_ref, sent, got, target):
        copy = pltpu.make_async_remote_copy(source, target_ref, sent, got, device_id=target, device_id_type=MESH)
        copy.start()
        return copy

    edge[...] = partial[:, 13:21, :]
    pl.semaphore_wait(barrier, len(partners))

    low, high = pl.ds(0, 6), pl.ds(13, 6)
    near_rows = pl.ds(0, 8)
    sources = [
        partial.at[high], partial.at[low], edge, partial.at[:, near_rows, :],
        edge.at[high], partial.at[high, near_rows, :], edge.at[low], partial.at[low, near_rows, :],
    ]
    fine_copies = [
        send(source, fine_in[n], fine_sent.at[n], fine_got.at[n], beside(*SIDES[n])) for n, source in enumerate(sources)
    ]

    for n in (0, 2):
        loads[n].wait()
    middle_part = dot_left(down, dot_right(partial[...].reshape(19 * 24, GZ), down_z))
    middle[...] = middle_part.reshape(13, 16, GZ)

    for n in (4, 6):
        loads[n].wait()
    rows = 16 * subs
    spread_modes = dot_left(enter, middle_part)
    packed = jnp.concatenate(
        [
            spread_modes[0:rows] + pltpu.roll(spread_modes[rows : 2 * rows], 64, 1),
            spread_modes[2 * rows : 3 * rows] + pltpu.roll(spread_modes[3 * rows : 4 * rows], 64, 1),
        ],
        axis=1,
    )
    modes_out[...] = dot_right(packed, enter_z).reshape(subs, 16, GZ)
    mode_copies = [
        send(modes_out.at[r], modes_in.at[subs - r], in_sent.at[r], in_got.at[subs - r], beside(0, r))
        for r in range(1, subs)
    ]

    middle_edge[...] = middle[:, 5:13, :]
    low, high = pl.ds(0, 8), pl.ds(5, 8)
    sources = [
        middle.at[high], middle.at[low], middle_edge, middle.at[:, near_rows, :],
        middle_edge.at[high], middle.at[high, near_rows, :], middle_edge.at[low], middle.at[low, near_rows, :],
    ]
    middle_copies = [
        send(source, middle_in[n], middle_sent.at[n], middle_got.at[n], beside(*SIDES[n]))
        for n, source in enumerate(sources)
    ]

    fine[...] = jnp.zeros_like(fine)
    fine[3:22, 3:27, :] = partial[...]
    for n, (dx, dy) in enumerate(SIDES):
        fine_copies[n].wait_recv()
        first = {1: 0, -1: 19, 0: 3}
        size = fine_in[n].shape
        x, y = first[dx], first[dy]
        fine[x : x + size[0], y : y + size[1], :] += fine_in[n][...]

    for copy in mode_copies:
        copy.wait_recv()
    total = modes_out[0]
    for r in range(1, subs):
        total = total + modes_in[r]
    line_out[...] = total
    line_copies = [
        send(line_out, line_in.at[slabs - r], line_sent.at[r], line_got.at[slabs - r], beside(r, 0))
        for r in range(1, slabs)
    ]
    line_in[0] = total

    fold_columns(fine, columns, 19, 24)
    loads[11].wait()
    fine_short = short_range(columns, near, 19, 24)

    for n in (8, 9, 10):
        loads[n].wait()
    for copy in line_copies:
        copy.wait_recv()
    in_modes = dot_left(mode_x, line_in[...].reshape(slabs * 16, GZ)) * spectrum[...]
    back_out[...] = dot_left(back_x, in_modes)
    back_copies = [
        send(back_out, back_in.at[subs - r], back_sent.at[r], back_got.at[subs - r], beside(0, r))
        for r in range(1, subs)
    ]
    back_in[0] = back_out[...]

    middle_wide[...] = jnp.zeros_like(middle_wide)
    middle_wide[3:16, 3:19, :] = middle[...]
    for n, (dx, dy) in enumerate(SIDES):
        middle_copies[n].wait_recv()
        first = {1: 0, -1: 11, 0: 3}
        size = middle_in[n].shape
        x, y = first[dx], first[dy]
        middle_wide[x : x + size[0], y : y + size[1], :] += middle_in[n][...]
    fold_columns(middle_wide, middle_columns, 13, 16)
    loads[12].wait()
    middle_short = short_range(middle_columns, near_middle, 13, 16)

    for n in (1, 3, 5, 7):
        loads[n].wait()
    for copy in back_copies:
        copy.wait_recv()
    wide = dot_right(back_in[...].reshape(rows, GZ), leave_z)
    stacked = jnp.concatenate(
        [wide[:, :GZ], pltpu.roll(wide[:, :GZ], 64, 1), wide[:, GZ:], pltpu.roll(wide[:, GZ:], 64, 1)], axis=0
    )
    middle_potential = middle_short + dot_left(leave, stacked)
    grid = fine_short + dot_right(dot_left(up, middle_potential), up_z)
    out[...] = grid.reshape(19, 24, GZ)
    for copy in fine_copies + middle_copies + mode_copies + line_copies + back_copies:
        copy.wait_send()


def levels(partial, slabs, subs):
    tables = [jnp.asarray(table) for table in level_tables(slabs, subs)]
    held = [
        pltpu.VMEM(table.shape[1:] if n in PER_SUB else table.shape, table.dtype) for n, table in enumerate(tables)
    ]
    f32 = lambda *shape: pltpu.VMEM(shape, jnp.float32)
    fine_in = [(6, 24), (6, 24), (19, 8), (19, 8)] + [(6, 8)] * 4
    middle_in = [(8, 16), (8, 16), (13, 8), (13, 8)] + [(8, 8)] * 4
    dma = lambda count: pltpu.SemaphoreType.DMA((count,))
    return pl.pallas_call(
        functools.partial(levels_kernel, slabs, subs),
        out_shape=jax.ShapeDtypeStruct((19, 24, GZ), jnp.float32),
        in_specs=[VMEM] + [ANY] * len(tables),
        out_specs=VMEM,
        scratch_shapes=held
        + [f32(*shape, GZ) for shape in fine_in + middle_in]
        + [
            f32(19, 8, GZ),
            f32(13, 8, GZ),
            f32(13, 16, GZ),
            f32(25, 32, GZ),
            f32(19, 24, GZ),
            f32(4, 25, 24, GZ),
            f32(4, 19, 16, GZ),
            f32(subs, 16, GZ),
            f32(subs, 16, GZ),
            f32(16, GZ),
            f32(slabs, 16, GZ),
            f32(16, GZ),
            f32(subs, 16, GZ),
        ]
        + [dma(len(tables)), dma(8), dma(8), dma(8), dma(8), dma(subs), dma(subs), dma(slabs), dma(slabs), dma(subs), dma(subs)],
        compiler_params=pltpu.CompilerParams(collective_id=1, has_side_effects=True, vmem_limit_bytes=60 << 20),
        name="levels",
    )(partial, *tables)


def body(atom_data, block_cell, send_list, send_count):
    slab_count = lax.axis_size("slab")
    sub_count = lax.axis_size("sub")
    place = placement_table()
    arrived, arrived_cells = exchange(
        send_list[0], send_count, block_cell, atom_data, slab_count * sub_count, sub_count
    )
    arrived = arrived.reshape(-1, BLOCK)
    arrived_cells = arrived_cells.reshape(-1, BLOCK)
    partial_charge = spread(arrived_cells, arrived, place)
    lattice = levels(partial_charge, slab_count, sub_count)
    return tuple(interpolate(arrived_cells, arrived, lattice, place))


def solution(mesh):
    placed = (
        P(("slab", "sub"), None, None),
        P(("slab", "sub")),
        P(("slab", "sub"), None, None),
        P(("slab", "sub"), None),
    )
    return jax.shard_map(
        body,
        mesh=mesh,
        in_specs=placed,
        out_specs=(P(("slab", "sub"), None), P("slab", "sub", None)),
        check_vma=False,
    )
```

```python
import functools
import ml_dtypes
import numpy as np
import jax
import jax.numpy as jnp
from jax import lax
from jax.experimental import pallas as pl
from jax.experimental.pallas import tpu as pltpu
from jax.sharding import PartitionSpec as P

BLOCK = 128
SENDERS = 8

GX = 16
GY = 16
GZ = 128
SMEM = pl.BlockSpec(memory_space=pltpu.SMEM)
VMEM = pl.BlockSpec(memory_space=pltpu.VMEM)
ANY = pl.BlockSpec(memory_space=pl.ANY)
MESH = pl.DeviceIdType.MESH


def spline_rows(row, offsets):
    far = jnp.maximum(2.0 - jnp.abs(row - offsets), 0.0)
    less = far - 1.0
    near = jnp.maximum(less, 0.0)
    return 0.5 * (far * far * less) + near * near * (1.0 - 2.0 * near)


def halves(values):
    high = values.astype(jnp.bfloat16)
    low = (values - high.astype(jnp.float32)).astype(jnp.bfloat16)
    return high, low


def cross(first, second):
    return jnp.concatenate([first[i : i + 1, :] * second for i in range(8)], axis=0)


def placement_tables():
    table = np.zeros((32, 8, GZ))
    for c in range(32):
        for k in range(7):
            table[c, k, (4 * c + k - 1) % GZ] = 1.0
    exact = table.astype(ml_dtypes.bfloat16)
    return exact.transpose(1, 0, 2).reshape(256, GZ), exact.reshape(256, GZ)


def two_parts(table):
    high = table.astype(ml_dtypes.bfloat16)
    low = (table - high.astype(np.float64)).astype(ml_dtypes.bfloat16)
    return np.stack([high, low])


def stencil(offset):
    size = np.abs(offset)
    return np.where(size == 0, 1.0, np.where(size == 1, 0.5625, np.where(size == 3, -0.0625, 0.0)))


def wrapped(offset, length):
    return (offset + length // 2) % length - length // 2


def halve(coarse, fine, coarse_first, fine_first, coarse_rows, fine_rows):
    table = np.zeros((coarse_rows, fine_rows))
    k = coarse_first + np.arange(coarse)[:, None]
    table[:coarse, :fine] = stencil(fine_first + np.arange(fine)[None, :] - 2 * k)
    return table


def halve_ring(coarse):
    return stencil(wrapped(np.arange(2 * coarse)[None, :] - 2 * np.arange(coarse)[:, None], 2 * coarse))


def soften(scaled):
    square = scaled * scaled
    return np.where(scaled < 1.0, (15.0 - 10.0 * square + 3.0 * square * square) / 8.0, 1.0 / np.maximum(scaled, 1.0))


def split_kernel(distance):
    return soften(distance / 2.0) / 2.0 - soften(distance / 4.0) / 4.0


def modes(length):
    angle = 2.0 * np.pi / length * (np.arange(length)[:, None] * np.arange(length)[None, :] % length)
    return (np.cos(angle) + np.sin(angle)) / np.sqrt(length)


RINGS = [(a, b) for a in range(4) for b in range(a, 4)]


def ring_tables(length, scale):
    shift = wrapped(np.arange(length)[:, None] - np.arange(length)[None, :], length)
    out = np.zeros((len(RINGS), GZ, GZ))
    for n, (a, b) in enumerate(RINGS):
        values = scale * split_kernel(np.sqrt(a * a + b * b + shift * shift))
        out[n, :length, :length] = np.where(np.abs(shift) <= 3, values, 0.0)
    return out.reshape(len(RINGS) * GZ, GZ)


def level_tables(slabs, subs):
    exact = lambda table: table.astype(ml_dtypes.bfloat16)
    down = np.kron(halve(13, 19, -2, -1, 13, 19), halve(13, 19, -2, -1, 16, 24))
    down_z = np.zeros((GZ, GZ))
    down_z[:, :64] = halve_ring(64).T
    top_x = halve(9, 13, -2, -2, 16, 13)
    top_y = halve(9, 13, -2, -2, 9, 16)
    wave_x, wave_y, wave_z = modes(4 * slabs), modes(4 * subs), modes(32)
    reach = np.arange(9) - 2
    enter = []
    for sub in range(subs):
        rows = 4 * ((sub + np.arange(subs)[None, :]) % subs) + np.arange(4)[:, None]
        along = wave_y[rows][:, :, (4 * sub + reach) % (4 * subs)] @ top_y
        enter.append(np.einsum("jrm,xn->jrxnm", along, top_x).reshape(4 * subs * 16, 13 * 16))
    enter = np.stack(enter)
    enter_z = np.kron(np.eye(4), (wave_z @ halve_ring(32)).T)
    mode_x = np.zeros((4 * slabs, slabs, 16))
    for r in range(slabs):
        mode_x[:, r, :9] = wave_x[:, (4 * r + reach) % (4 * slabs)]
    back_x = np.zeros((16, 4 * slabs))
    back_x[:9] = wave_x[:, reach % (4 * slabs)].T
    squared = 0.0
    for dimension, length in enumerate((4 * slabs, 4 * subs, 32)):
        shape = [1, 1, 1]
        shape[dimension] = length
        squared = squared + (wrapped(np.arange(length), length) ** 2).reshape(shape)
    spectrum = np.fft.fftn(soften(np.sqrt(squared) / 2.0) / 8.0).real
    spectrum = spectrum.reshape(4 * slabs, subs, 128).transpose(1, 0, 2).astype(np.float32)
    return placement_tables() + (
        exact(down),
        exact(down.T),
        exact(down_z),
        exact(down_z.T),
        two_parts(enter).transpose(1, 0, 2, 3),
        two_parts(enter.transpose(0, 2, 1)).transpose(1, 0, 2, 3),
        two_parts(enter_z),
        two_parts(enter_z.T),
        two_parts(mode_x.reshape(4 * slabs, slabs * 16)),
        two_parts(back_x),
        spectrum,
        two_parts(ring_tables(GZ, 1.0)),
        two_parts(ring_tables(GZ // 2, 0.5)),
    )


PER_SUB = (6, 7, 12)


def dot(a, b):
    return jnp.dot(a, b, preferred_element_type=jnp.float32)


def dot_right(values, table):
    high, low = halves(values)
    if len(table.shape) == 2:
        return dot(high, table[...]) + dot(low, table[...])
    return dot(high, table[0]) + dot(low, table[0]) + dot(high, table[1])


def dot_left(table, values):
    high, low = halves(values)
    if len(table.shape) == 2:
        return dot(table[...], high) + dot(table[...], low)
    return dot(table[0], high) + dot(table[0], low) + dot(table[1], high)


def fold_columns(lattice, columns, planes, rows):
    columns[0] = lattice[:, 3 : 3 + rows, :]
    for b in range(1, 4):
        columns[b] = lattice[:, 3 - b : 3 - b + rows, :] + lattice[:, 3 + b : 3 + b + rows, :]


def short_range(columns, table, planes, rows):
    def sides(a, b):
        if a == 0:
            return columns[b, 3 : 3 + planes]
        return columns[b, 3 - a : 3 - a + planes] + columns[b, 3 + a : 3 + a + planes]

    total = None
    for n in range(0, len(RINGS), 2):
        parts = []
        for a, b in RINGS[n : n + 2]:
            part = sides(a, b) if a == b else sides(a, b) + sides(b, a)
            parts.append(halves(part.reshape(planes * rows, GZ)))
        high, low = (jnp.concatenate([part[m] for part in parts], axis=1) for m in range(2))
        span = pl.ds(n * GZ, 2 * GZ)
        here = dot(high, table[0, span, :]) + dot(low, table[0, span, :]) + dot(high, table[1, span, :])
        total = here if total is None else total + here
    return total


SIDES = [(1, 0), (-1, 0), (0, 1), (0, -1), (1, 1), (1, -1), (-1, 1), (-1, -1)]


def whole_kernel(slabs, subs, chosen, counts, cells, atoms, *refs):
    tables = refs[:15]
    potentials, grid_out = refs[15:17]
    rest = list(refs[17:])
    take = lambda count: [rest.pop(0) for _ in range(count)]
    held = take(15)
    atoms_held, outgoing, incoming, cell_rows, cell_line, cell_pack, cell_all, cell_block, cell_scalars = take(9)
    across, along, patches, cell_sums, partial, table = take(6)
    fine_in, middle_in = take(8), take(8)
    edge, middle_edge, middle, fine, middle_wide, columns, middle_columns = take(7)
    modes_out, modes_in, line_out, line_in, back_out, back_in = take(6)
    load_sem, atoms_sem, sent, got, cell_sent, cell_got, relay_sent, relay_got, scalar_sem = take(9)
    fine_sent, fine_got, middle_sent, middle_got, in_sent, in_got, line_sent, line_got, back_sent, back_got = rest
    devices = slabs * subs
    slab = lax.axis_index("slab")
    sub = lax.axis_index("sub")
    me = slab * subs + sub

    def beside(dx, dy):
        return (lax.rem(slab + dx + slabs, slabs), lax.rem(sub + dy + subs, subs))

    def send(source, target_ref, sent, got, target):
        copy = pltpu.make_async_remote_copy(source, target_ref, sent, got, device_id=target, device_id_type=MESH)
        copy.start()
        return copy

    atoms_load = pltpu.make_async_copy(atoms, atoms_held, atoms_sem)
    atoms_load.start()
    barrier = pltpu.get_barrier_semaphore()

    def peer_of(step):
        peer = lax.rem(me + step, devices)
        return peer, (peer // subs, lax.rem(peer, subs))

    def greet(step, carry):
        pl.semaphore_signal(barrier, inc=1, device_id=peer_of(step)[1], device_id_type=MESH)
        return carry

    lax.fori_loop(1, devices, greet, 0)
    loads = [
        pltpu.make_async_copy(table_ref.at[sub] if n in PER_SUB else table_ref, held[n], load_sem.at[n])
        for n, table_ref in enumerate(tables)
    ]
    for load in loads:
        load.start()
    place_in, place_back = held[:2]
    loads_of_levels = loads[2:]

    atoms_load.wait()
    lane = lax.broadcasted_iota(jnp.int32, (1, BLOCK), 1)

    def pick(row, carry):
        line = jnp.full((1, BLOCK), 512, jnp.int32)
        for n in range(subs):
            peer = row * subs + n
            for j in range(4):
                index = chosen[j, peer]
                outgoing[peer, pl.ds(4 * j, 4), :] = atoms_held[index]
                cell = cells[index]
                local = ((cell >> 10) & 3) * 128 + ((cell >> 5) & 3) * 32 + (cell & 31)
                line = jnp.where(lane == 4 * n + j, jnp.where(counts[0, peer] > j, local, 512), line)
        cell_rows[row] = line
        return carry

    lax.fori_loop(0, slabs, pick, 0)
    pl.semaphore_wait(barrier, devices - 1)

    def start(step, carry):
        peer, target = peer_of(step)
        send(outgoing.at[peer], incoming.at[step], sent, got.at[step], target)
        return carry

    lax.fori_loop(1, devices, start, 0)
    own = pltpu.make_async_copy(outgoing.at[me], incoming.at[0], got.at[0])
    own.start()
    cell_copies = [
        send(cell_rows.at[lax.rem(slab + r, slabs)], cell_line.at[slab], cell_sent.at[r], cell_got.at[slabs - r], beside(r, 0))
        for r in range(1, slabs)
    ]
    cell_line[slab] = cell_rows[slab]

    offsets = lax.broadcasted_iota(jnp.int32, (8, BLOCK), 0).astype(jnp.float32) - 1.0

    def sender_of(step):
        sender = lax.rem(me - step + devices, devices)
        return sender, lax.rem(sender, subs) * slabs + sender // subs

    def spread(group, carry):
        for n in range(SENDERS):
            step = group * SENDERS + n
            pltpu.make_async_copy(incoming.at[step], incoming.at[step], got.at[step]).wait()
        parts = []
        for n in range(SENDERS):
            step = group * SENDERS + n
            for j in range(4):
                wx, wy, wz = (spline_rows(incoming[step, pl.ds(4 * j + d, 1), :], offsets) for d in range(3))
                charge = incoming[step, pl.ds(4 * j + 3, 1), :]
                high, low = halves(cross(wx, wy))
                slot = step * 4 + j
                across[slot, 0:64, :] = high
                across[slot, 64:128, :] = low
                along[slot] = wz
                both = jnp.concatenate(halves(wz * charge), axis=0)
                product = lax.dot_general(
                    jnp.concatenate([both, both], axis=1),
                    jnp.concatenate([high, low], axis=1),
                    (((1,), (1,)), ((), ())),
                    preferred_element_type=jnp.float32,
                )
                parts.append((step, j, product[0:8] + product[8:16]))
        for step, j, part in parts:
            patches[j * devices + sender_of(step)[1], :, 0:64] = part
        return carry

    groups = devices // SENDERS
    lax.fori_loop(0, groups // 2, spread, 0)
    for copy in cell_copies:
        copy.wait_recv()
    cell_pack[...] = cell_line[:, 0, :]
    relay_copies = [
        send(cell_pack, cell_all.at[sub], relay_sent.at[r], relay_got.at[subs - r], beside(0, r)) for r in range(1, subs)
    ]
    cell_all[sub] = cell_pack[...]
    lax.fori_loop(groups // 2, groups, spread, 0)
    for copy in relay_copies:
        copy.wait_recv()
    cell_block[...] = pltpu.roll(cell_all[...].reshape(devices, BLOCK), lax.rem(BLOCK - 4 * sub, BLOCK), 1)
    scalars = pltpu.make_async_copy(cell_block, cell_scalars, scalar_sem)
    scalars.start()

    slots_across = cell_block[...].T
    cell_number = lax.broadcasted_iota(jnp.int32, (512, devices), 0)
    member = jnp.concatenate(
        [(cell_number == slots_across[j : j + 1, :]).astype(jnp.float32).astype(jnp.bfloat16) for j in range(4)], axis=1
    )
    for k in range(8):
        sums = dot(member, jnp.concatenate(halves(patches[:, k, :]), axis=1))
        cell_sums[k] = sums[:, :128] + sums[:, 128:]
    partial[...] = jnp.zeros_like(partial)
    loads[0].wait()
    loads[1].wait()
    for a in range(4):
        for b in range(4):
            first = (a * 4 + b) * 32
            column = cell_sums[:, first : first + 32, :].reshape(256, 128)
            planes = dot_right(column.T, place_in)
            for i in range(7):
                partial[4 * a + i, 4 * b : 4 * b + 8, :] += planes[8 * i : 8 * i + 8]

    loads = loads_of_levels
    down, up, down_z, up_z, enter, leave, enter_z, leave_z, mode_x, back_x, spectrum, near, near_middle = held[2:]

    edge[...] = partial[:, 13:21, :]

    low, high = pl.ds(0, 6), pl.ds(13, 6)
    near_rows = pl.ds(0, 8)
    sources = [
        partial.at[high], partial.at[low], edge, partial.at[:, near_rows, :],
        edge.at[high], partial.at[high, near_rows, :], edge.at[low], partial.at[low, near_rows, :],
    ]
    fine_copies = [
        send(source, fine_in[n], fine_sent.at[n], fine_got.at[n], beside(*SIDES[n])) for n, source in enumerate(sources)
    ]

    for n in (0, 2):
        loads[n].wait()
    middle_part = dot_left(down, dot_right(partial[...].reshape(19 * 24, GZ), down_z))
    middle[...] = middle_part.reshape(13, 16, GZ)

    for n in (4, 6):
        loads[n].wait()
    rows = 16 * subs
    spread_modes = dot_left(enter, middle_part)
    packed = jnp.concatenate(
        [
            spread_modes[0:rows] + pltpu.roll(spread_modes[rows : 2 * rows], 64, 1),
            spread_modes[2 * rows : 3 * rows] + pltpu.roll(spread_modes[3 * rows : 4 * rows], 64, 1),
        ],
        axis=1,
    )
    modes_out[...] = dot_right(packed, enter_z).reshape(subs, 16, GZ)
    mode_copies = [
        send(modes_out.at[r], modes_in.at[subs - r], in_sent.at[r], in_got.at[subs - r], beside(0, r))
        for r in range(1, subs)
    ]

    middle_edge[...] = middle[:, 5:13, :]
    low, high = pl.ds(0, 8), pl.ds(5, 8)
    sources = [
        middle.at[high], middle.at[low], middle_edge, middle.at[:, near_rows, :],
        middle_edge.at[high], middle.at[high, near_rows, :], middle_edge.at[low], middle.at[low, near_rows, :],
    ]
    middle_copies = [
        send(source, middle_in[n], middle_sent.at[n], middle_got.at[n], beside(*SIDES[n]))
        for n, source in enumerate(sources)
    ]

    fine[...] = jnp.zeros_like(fine)
    fine[3:22, 3:27, :] = partial[...]
    for n, (dx, dy) in enumerate(SIDES):
        fine_copies[n].wait_recv()
        first = {1: 0, -1: 19, 0: 3}
        size = fine_in[n].shape
        x, y = first[dx], first[dy]
        fine[x : x + size[0], y : y + size[1], :] += fine_in[n][...]

    for copy in mode_copies:
        copy.wait_recv()
    total = modes_out[0]
    for r in range(1, subs):
        total = total + modes_in[r]
    line_out[...] = total
    line_copies = [
        send(line_out, line_in.at[slabs - r], line_sent.at[r], line_got.at[slabs - r], beside(r, 0))
        for r in range(1, slabs)
    ]
    line_in[0] = total

    fold_columns(fine, columns, 19, 24)
    loads[11].wait()
    fine_short = short_range(columns, near, 19, 24)

    for n in (8, 9, 10):
        loads[n].wait()
    for copy in line_copies:
        copy.wait_recv()
    in_modes = dot_left(mode_x, line_in[...].reshape(slabs * 16, GZ)) * spectrum[...]
    back_out[...] = dot_left(back_x, in_modes)
    back_copies = [
        send(back_out, back_in.at[subs - r], back_sent.at[r], back_got.at[subs - r], beside(0, r))
        for r in range(1, subs)
    ]
    back_in[0] = back_out[...]

    middle_wide[...] = jnp.zeros_like(middle_wide)
    middle_wide[3:16, 3:19, :] = middle[...]
    for n, (dx, dy) in enumerate(SIDES):
        middle_copies[n].wait_recv()
        first = {1: 0, -1: 11, 0: 3}
        size = middle_in[n].shape
        x, y = first[dx], first[dy]
        middle_wide[x : x + size[0], y : y + size[1], :] += middle_in[n][...]
    fold_columns(middle_wide, middle_columns, 13, 16)
    loads[12].wait()
    middle_short = short_range(middle_columns, near_middle, 13, 16)

    for n in (1, 3, 5, 7):
        loads[n].wait()
    for copy in back_copies:
        copy.wait_recv()
    wide = dot_right(back_in[...].reshape(rows, GZ), leave_z)
    stacked = jnp.concatenate(
        [wide[:, :GZ], pltpu.roll(wide[:, :GZ], 64, 1), wide[:, GZ:], pltpu.roll(wide[:, GZ:], 64, 1)], axis=0
    )
    middle_potential = middle_short + dot_left(leave, stacked)
    grid = fine_short + dot_right(dot_left(up, middle_potential), up_z)
    for copy in fine_copies:
        copy.wait_send()
    lattice = partial
    lattice[...] = grid.reshape(19, 24, GZ)
    grid_out[...] = lattice[1:17, 1:17, :]

    scalars.wait()
    forms = (((1,), (1,)), ((), ()))
    for a in range(4):
        for b in range(4):
            rows_of = [lattice[4 * a + i, 4 * b : 4 * b + 8, :] for i in range(7)] + [jnp.zeros((8, 128), jnp.float32)]
            high, low = halves(jnp.concatenate(rows_of, axis=0))
            column = lax.dot_general(place_back[...], high, forms, preferred_element_type=jnp.float32)
            column = column + lax.dot_general(place_back[...], low, forms, preferred_element_type=jnp.float32)
            first = (a * 4 + b) * 32
            pair = jnp.concatenate(halves(column.reshape(32, 8, 64)), axis=1)
            table[first : first + 32] = jnp.concatenate([pair, pair], axis=2)
    table[512] = jnp.zeros((16, 128), jnp.bfloat16)

    def interpolate(group, carry):
        for n in range(SENDERS):
            step = group * SENDERS + n
            sender, order = sender_of(step)
            for j in range(4):
                slot = step * 4 + j
                product = dot(table[cell_scalars[order, j]], across[slot])
                part = (product[0:8] + product[8:16]) * along[slot]
                potentials[pl.ds(sender * 4 + j, 1), :] = jnp.sum(part, axis=0, keepdims=True)
        return carry

    lax.fori_loop(0, groups, interpolate, 0)
    others = pl.ds(0, devices - 1)
    pltpu.make_async_copy(outgoing.at[others], outgoing.at[others], sent).wait()
    for copy in middle_copies + mode_copies + line_copies + back_copies + cell_copies + relay_copies:
        copy.wait_send()


def whole(chosen, counts, cells, atoms, slabs, subs):
    tables = [jnp.asarray(table) for table in level_tables(slabs, subs)]
    devices = slabs * subs
    held = [
        pltpu.VMEM(table.shape[1:] if n in PER_SUB else table.shape, table.dtype) for n, table in enumerate(tables)
    ]
    f32 = lambda *shape: pltpu.VMEM(shape, jnp.float32)
    i32 = lambda *shape: pltpu.VMEM(shape, jnp.int32)
    fine_in = [(6, 24), (6, 24), (19, 8), (19, 8)] + [(6, 8)] * 4
    middle_in = [(8, 16), (8, 16), (13, 8), (13, 8)] + [(8, 8)] * 4
    dma = lambda count: pltpu.SemaphoreType.DMA((count,))
    return pl.pallas_call(
        functools.partial(whole_kernel, slabs, subs),
        out_shape=(
            jax.ShapeDtypeStruct((devices * 4, BLOCK), jnp.float32),
            jax.ShapeDtypeStruct((GX, GY, GZ), jnp.float32),
        ),
        in_specs=[SMEM, SMEM, SMEM] + [ANY] * (1 + len(tables)),
        out_specs=(VMEM, VMEM),
        scratch_shapes=held
        + [
            f32(*atoms.shape),
            f32(devices, 16, BLOCK),
            f32(devices, 16, BLOCK),
            i32(slabs, 1, BLOCK),
            i32(slabs, 1, BLOCK),
            i32(slabs, BLOCK),
            i32(subs, slabs, BLOCK),
            i32(devices, BLOCK),
            pltpu.SMEM((devices, BLOCK), jnp.int32),
            pltpu.VMEM((devices * 4, 128, BLOCK), jnp.bfloat16),
            f32(devices * 4, 8, BLOCK),
            f32(devices * 4, 8, 128),
            f32(8, 512, 128),
            f32(19, 24, GZ),
            pltpu.VMEM((513, 16, 128), jnp.bfloat16),
        ]
        + [f32(*shape, GZ) for shape in fine_in + middle_in]
        + [
            f32(19, 8, GZ),
            f32(13, 8, GZ),
            f32(13, 16, GZ),
            f32(25, 32, GZ),
            f32(19, 24, GZ),
            f32(4, 25, 24, GZ),
            f32(4, 19, 16, GZ),
            f32(subs, 16, GZ),
            f32(subs, 16, GZ),
            f32(16, GZ),
            f32(slabs, 16, GZ),
            f32(16, GZ),
            f32(subs, 16, GZ),
        ]
        + [dma(len(tables)), pltpu.SemaphoreType.DMA, pltpu.SemaphoreType.DMA, dma(devices)]
        + [dma(slabs), dma(slabs), dma(subs), dma(subs), pltpu.SemaphoreType.DMA]
        + [dma(8), dma(8), dma(8), dma(8)]
        + [dma(subs), dma(subs), dma(slabs), dma(slabs), dma(subs), dma(subs)],
        compiler_params=pltpu.CompilerParams(collective_id=0, has_side_effects=True, vmem_limit_bytes=60 << 20),
        name="multilevel",
    )(chosen, counts, cells, atoms, *tables)


def body(atom_data, block_cell, send_list, send_count):
    slabs, subs = lax.axis_size("slab"), lax.axis_size("sub")
    return tuple(whole(send_list[0].T, send_count, block_cell, atom_data, slabs, subs))


def solution(mesh):
    placed = (
        P(("slab", "sub"), None, None),
        P(("slab", "sub")),
        P(("slab", "sub"), None, None),
        P(("slab", "sub"), None),
    )
    return jax.shard_map(
        body,
        mesh=mesh,
        in_specs=placed,
        out_specs=(P(("slab", "sub"), None), P("slab", "sub", None)),
        check_vma=False,
    )
```

```python
import functools
import ml_dtypes
import numpy as np
import jax
import jax.numpy as jnp
from jax import lax
from jax.experimental import pallas as pl
from jax.experimental.pallas import tpu as pltpu
from jax.sharding import PartitionSpec as P

BLOCK = 128
SENDERS = 8

GX = 16
GY = 16
GZ = 128
SMEM = pl.BlockSpec(memory_space=pltpu.SMEM)
VMEM = pl.BlockSpec(memory_space=pltpu.VMEM)
ANY = pl.BlockSpec(memory_space=pl.ANY)
MESH = pl.DeviceIdType.MESH


def spline_rows(row, offsets):
    far = jnp.maximum(2.0 - jnp.abs(row - offsets), 0.0)
    less = far - 1.0
    near = jnp.maximum(less, 0.0)
    return 0.5 * (far * far * less) + near * near * (1.0 - 2.0 * near)


def halves(values):
    high = values.astype(jnp.bfloat16)
    low = (values - high.astype(jnp.float32)).astype(jnp.bfloat16)
    return high, low


def cross(first, second):
    return jnp.concatenate([first[i : i + 1, :] * second for i in range(8)], axis=0)


def placement_tables():
    table = np.zeros((32, 8, GZ))
    for c in range(32):
        for k in range(7):
            table[c, k, (4 * c + k - 1) % GZ] = 1.0
    exact = table.astype(ml_dtypes.bfloat16)
    return exact.transpose(1, 0, 2).reshape(256, GZ).T, exact.reshape(256, GZ)


def two_parts(table):
    high = table.astype(ml_dtypes.bfloat16)
    low = (table - high.astype(np.float64)).astype(ml_dtypes.bfloat16)
    return np.stack([high, low])


def stencil(offset):
    size = np.abs(offset)
    return np.where(size == 0, 1.0, np.where(size == 1, 0.5625, np.where(size == 3, -0.0625, 0.0)))


def wrapped(offset, length):
    return (offset + length // 2) % length - length // 2


def halve(coarse, fine, coarse_first, fine_first, coarse_rows, fine_rows):
    table = np.zeros((coarse_rows, fine_rows))
    k = coarse_first + np.arange(coarse)[:, None]
    table[:coarse, :fine] = stencil(fine_first + np.arange(fine)[None, :] - 2 * k)
    return table


def halve_ring(coarse):
    return stencil(wrapped(np.arange(2 * coarse)[None, :] - 2 * np.arange(coarse)[:, None], 2 * coarse))


def soften(scaled):
    square = scaled * scaled
    return np.where(scaled < 1.0, (15.0 - 10.0 * square + 3.0 * square * square) / 8.0, 1.0 / np.maximum(scaled, 1.0))


def split_kernel(distance):
    return soften(distance / 2.0) / 2.0 - soften(distance / 4.0) / 4.0


def modes(length):
    angle = 2.0 * np.pi / length * (np.arange(length)[:, None] * np.arange(length)[None, :] % length)
    return (np.cos(angle) + np.sin(angle)) / np.sqrt(length)


RINGS = [(a, b) for a in range(4) for b in range(a, 4)]


def ring_tables(length, scale):
    shift = wrapped(np.arange(length)[:, None] - np.arange(length)[None, :], length)
    out = np.zeros((len(RINGS), GZ, GZ))
    for n, (a, b) in enumerate(RINGS):
        values = scale * split_kernel(np.sqrt(a * a + b * b + shift * shift))
        out[n, :length, :length] = np.where(np.abs(shift) <= 3, values, 0.0)
    return out.reshape(len(RINGS) * GZ, GZ)


def level_tables(slabs, subs):
    exact = lambda table: table.astype(ml_dtypes.bfloat16)
    down = np.kron(halve(13, 19, -2, -1, 13, 19), halve(13, 19, -2, -1, 16, 24))
    down_z = np.zeros((GZ, GZ))
    down_z[:, :64] = halve_ring(64).T
    top_x = halve(9, 13, -2, -2, 16, 13) @ halve(13, 19, -2, -1, 13, 19)
    top_y = halve(9, 13, -2, -2, 9, 16) @ halve(13, 19, -2, -1, 16, 24)
    top_z = halve_ring(32) @ halve_ring(64)
    wave_x, wave_y, wave_z = modes(4 * slabs), modes(4 * subs), modes(32)
    reach = np.arange(9) - 2
    enter = []
    for sub in range(subs):
        rows = 4 * ((sub + np.arange(subs)[None, :]) % subs) + np.arange(4)[:, None]
        along = wave_y[rows][:, :, (4 * sub + reach) % (4 * subs)] @ top_y
        enter.append(np.einsum("jrm,xn->jrxnm", along, top_x).reshape(4 * subs * 16, 19 * 24))
    enter = np.stack(enter)
    enter_z = np.tile((wave_z @ top_z).T, (1, 4))
    leave_z = np.kron(np.eye(4), wave_z @ top_z)
    mode_x = np.zeros((4 * slabs, slabs, 16))
    for r in range(slabs):
        mode_x[:, r, :9] = wave_x[:, (4 * r + reach) % (4 * slabs)]
    back_x = np.zeros((16, 4 * slabs))
    back_x[:9] = wave_x[:, reach % (4 * slabs)].T
    squared = 0.0
    for dimension, length in enumerate((4 * slabs, 4 * subs, 32)):
        shape = [1, 1, 1]
        shape[dimension] = length
        squared = squared + (wrapped(np.arange(length), length) ** 2).reshape(shape)
    spectrum = np.fft.fftn(soften(np.sqrt(squared) / 2.0) / 8.0).real
    spectrum = spectrum.reshape(4 * slabs, subs, 128).transpose(1, 0, 2).astype(np.float32)
    return placement_tables() + (
        exact(down),
        exact(down.T),
        exact(down_z),
        exact(down_z.T),
        two_parts(enter).transpose(1, 0, 2, 3),
        two_parts(enter.transpose(0, 2, 1)).transpose(1, 0, 2, 3),
        two_parts(enter_z),
        two_parts(leave_z),
        two_parts(mode_x.reshape(4 * slabs, slabs * 16)),
        two_parts(back_x),
        spectrum,
        two_parts(ring_tables(GZ, 1.0)),
        two_parts(ring_tables(GZ // 2, 0.5)),
    )


PER_SUB = (6, 7, 12)


def dot(a, b):
    return jnp.dot(a, b, preferred_element_type=jnp.float32)


def dot_right(values, table):
    high, low = halves(values)
    if len(table.shape) == 2:
        return dot(high, table[...]) + dot(low, table[...])
    return dot(high, table[0]) + dot(low, table[0]) + dot(high, table[1])


def dot_left(table, values):
    high, low = halves(values)
    if len(table.shape) == 2:
        return dot(table[...], high) + dot(table[...], low)
    return dot(table[0], high) + dot(table[0], low) + dot(table[1], high)


def fold_columns(lattice, columns, planes, rows):
    columns[0] = lattice[:, 3 : 3 + rows, :]
    for b in range(1, 4):
        columns[b] = lattice[:, 3 - b : 3 - b + rows, :] + lattice[:, 3 + b : 3 + b + rows, :]


def short_range(columns, table, planes, rows):
    def sides(a, b):
        if a == 0:
            return columns[b, 3 : 3 + planes]
        return columns[b, 3 - a : 3 - a + planes] + columns[b, 3 + a : 3 + a + planes]

    total = None
    for n in range(0, len(RINGS), 2):
        parts = []
        for a, b in RINGS[n : n + 2]:
            part = sides(a, b) if a == b else sides(a, b) + sides(b, a)
            parts.append(halves(part.reshape(planes * rows, GZ)))
        high, low = (jnp.concatenate([part[m] for part in parts], axis=1) for m in range(2))
        span = pl.ds(n * GZ, 2 * GZ)
        here = dot(high, table[0, span, :]) + dot(low, table[0, span, :]) + dot(high, table[1, span, :])
        total = here if total is None else total + here
    return total


SIDES = [(1, 0), (-1, 0), (0, 1), (0, -1), (1, 1), (1, -1), (-1, 1), (-1, -1)]


def whole_kernel(slabs, subs, chosen, counts, cells, atoms, *refs):
    tables = refs[:15]
    potentials, grid_out = refs[15:17]
    rest = list(refs[17:])
    take = lambda count: [rest.pop(0) for _ in range(count)]
    held = take(15)
    atoms_held, outgoing, incoming, cells_out, cells_in, cell_block, cell_scalars = take(7)
    across, along, patches, cell_sums, partial, table = take(6)
    fine_in, middle_in = take(8), take(8)
    edge, middle_edge, middle, fine, middle_wide, columns, middle_columns = take(7)
    modes_out, modes_in, line_out, line_in, back_out, back_in = take(6)
    load_sem, atoms_sem, sent, got, cell_sent, cell_got, scalar_sem = take(7)
    fine_sent, fine_got, middle_sent, middle_got, in_sent, in_got, line_sent, line_got, back_sent, back_got = rest
    devices = slabs * subs
    slab = lax.axis_index("slab")
    sub = lax.axis_index("sub")
    me = slab * subs + sub

    def beside(dx, dy):
        return (lax.rem(slab + dx + slabs, slabs), lax.rem(sub + dy + subs, subs))

    def send(source, target_ref, sent, got, target):
        copy = pltpu.make_async_remote_copy(source, target_ref, sent, got, device_id=target, device_id_type=MESH)
        copy.start()
        return copy

    atoms_load = pltpu.make_async_copy(atoms, atoms_held, atoms_sem)
    atoms_load.start()
    barrier = pltpu.get_barrier_semaphore()

    def peer_of(step):
        peer = lax.rem(me + step, devices)
        return peer, (peer // subs, lax.rem(peer, subs))

    def greet(step, carry):
        pl.semaphore_signal(barrier, inc=1, device_id=peer_of(step)[1], device_id_type=MESH)
        return carry

    lax.fori_loop(1, devices, greet, 0)
    loads = [
        pltpu.make_async_copy(table_ref.at[sub] if n in PER_SUB else table_ref, held[n], load_sem.at[n])
        for n, table_ref in enumerate(tables)
    ]
    for load in loads:
        load.start()
    place_in, place_back = held[:2]
    loads_of_levels = loads[2:]

    atoms_load.wait()
    lane = lax.broadcasted_iota(jnp.int32, (1, BLOCK), 1)

    def pick(row, carry):
        for n in range(subs):
            peer = row * subs + n
            line = jnp.full((1, BLOCK), 512, jnp.int32)
            for j in range(4):
                index = chosen[j, peer]
                outgoing[peer, pl.ds(4 * j, 4), :] = atoms_held[index]
                cell = cells[index]
                local = ((cell >> 10) & 3) * 128 + ((cell >> 5) & 3) * 32 + (cell & 31)
                line = jnp.where(lane == j, jnp.where(counts[0, peer] > j, local, 512), line)
            cells_out[peer] = line
        return carry

    lax.fori_loop(0, slabs, pick, 0)
    pl.semaphore_wait(barrier, devices - 1)

    def start(step, carry):
        peer, target = peer_of(step)
        send(cells_out.at[peer], cells_in.at[step], cell_sent, cell_got, target)
        send(outgoing.at[peer], incoming.at[step], sent, got.at[step], target)
        return carry

    lax.fori_loop(1, devices, start, 0)
    own = pltpu.make_async_copy(outgoing.at[me], incoming.at[0], got.at[0])
    own.start()
    cells_in[0] = cells_out[me]

    offsets = lax.broadcasted_iota(jnp.int32, (8, BLOCK), 0).astype(jnp.float32) - 1.0

    def spread(group, carry):
        for n in range(SENDERS):
            step = group * SENDERS + n
            pltpu.make_async_copy(incoming.at[step], incoming.at[step], got.at[step]).wait()
        parts = []
        for n in range(SENDERS):
            step = group * SENDERS + n
            for j in range(4):
                wx, wy, wz = (spline_rows(incoming[step, pl.ds(4 * j + d, 1), :], offsets) for d in range(3))
                charge = incoming[step, pl.ds(4 * j + 3, 1), :]
                high, low = halves(cross(wx, wy))
                slot = step * 4 + j
                across[slot, 0:64, :] = high
                across[slot, 64:128, :] = low
                along[slot] = wz
                both = jnp.concatenate(halves(wz * charge), axis=0)
                product = lax.dot_general(
                    jnp.concatenate([both, both], axis=1),
                    jnp.concatenate([high, low], axis=1),
                    (((1,), (1,)), ((), ())),
                    preferred_element_type=jnp.float32,
                )
                parts.append((step, j, product[0:8] + product[8:16]))
        for step, j, part in parts:
            patches[pl.ds(pl.multiple_of((j * devices + step) * 8, 8), 8), 0:64] = part
        return carry

    groups = devices // SENDERS
    lax.fori_loop(0, groups, spread, 0)
    others = pl.ds(1, devices - 1)
    pltpu.make_async_copy(cells_in.at[others], cells_in.at[others], cell_got).wait()
    cell_block[...] = cells_in[:, 0, :]
    scalars = pltpu.make_async_copy(cell_block, cell_scalars, scalar_sem)
    scalars.start()

    slots_across = cell_block[...].T
    cell_number = lax.broadcasted_iota(jnp.int32, (512, devices), 0)
    member = jnp.concatenate(
        [(cell_number == slots_across[j : j + 1, :]).astype(jnp.float32).astype(jnp.bfloat16) for j in range(4)], axis=1
    )
    for k in range(8):
        sums = dot(member, jnp.concatenate(halves(patches[pl.ds(k, devices * 4, stride=8), :]), axis=1))
        cell_sums[k] = sums[:, :128] + sums[:, 128:]
    partial[...] = jnp.zeros_like(partial)
    loads[0].wait()
    loads[1].wait()
    for a in range(4):
        for b in range(4):
            first = (a * 4 + b) * 32
            column = cell_sums[:, first : first + 32, :].reshape(256, 128)
            planes = dot_left(place_in, column).T
            for i in range(7):
                partial[4 * a + i, 4 * b : 4 * b + 8, :] += planes[8 * i : 8 * i + 8]

    loads = loads_of_levels
    down, up, down_z, up_z, enter, leave, enter_z, leave_z, mode_x, back_x, spectrum, near, near_middle = held[2:]

    for n in (4, 6):
        loads[n].wait()
    rows = 16 * subs
    spread_modes = dot_left(enter, dot_right(partial[...].reshape(19 * 24, GZ), enter_z))
    group_of_lane = lax.broadcasted_iota(jnp.int32, (rows, GZ), 1) // 32
    packed = spread_modes[0:rows]
    for j in range(1, 4):
        packed = jnp.where(group_of_lane == j, spread_modes[j * rows : (j + 1) * rows], packed)
    modes_out[...] = packed.reshape(subs, 16, GZ)
    mode_copies = [
        send(modes_out.at[r], modes_in.at[subs - r], in_sent.at[r], in_got.at[subs - r], beside(0, r))
        for r in range(1, subs)
    ]

    edge[...] = partial[:, 13:21, :]

    low, high = pl.ds(0, 6), pl.ds(13, 6)
    near_rows = pl.ds(0, 8)
    sources = [
        partial.at[high], partial.at[low], edge, partial.at[:, near_rows, :],
        edge.at[high], partial.at[high, near_rows, :], edge.at[low], partial.at[low, near_rows, :],
    ]
    fine_copies = [
        send(source, fine_in[n], fine_sent.at[n], fine_got.at[n], beside(*SIDES[n])) for n, source in enumerate(sources)
    ]

    for copy in mode_copies:
        copy.wait_recv()
    total = modes_out[0]
    for r in range(1, subs):
        total = total + modes_in[r]
    line_out[...] = total
    line_copies = [
        send(line_out, line_in.at[slabs - r], line_sent.at[r], line_got.at[slabs - r], beside(r, 0))
        for r in range(1, slabs)
    ]
    line_in[0] = total

    for n in (0, 2):
        loads[n].wait()
    middle[...] = dot_left(down, dot_right(partial[...].reshape(19 * 24, GZ), down_z)).reshape(13, 16, GZ)

    middle_edge[...] = middle[:, 5:13, :]
    low, high = pl.ds(0, 8), pl.ds(5, 8)
    sources = [
        middle.at[high], middle.at[low], middle_edge, middle.at[:, near_rows, :],
        middle_edge.at[high], middle.at[high, near_rows, :], middle_edge.at[low], middle.at[low, near_rows, :],
    ]
    middle_copies = [
        send(source, middle_in[n], middle_sent.at[n], middle_got.at[n], beside(*SIDES[n]))
        for n, source in enumerate(sources)
    ]

    for n in (8, 9, 10):
        loads[n].wait()
    for copy in line_copies:
        copy.wait_recv()
    in_modes = dot_left(mode_x, line_in[...].reshape(slabs * 16, GZ)) * spectrum[...]
    back_out[...] = dot_left(back_x, in_modes)
    back_copies = [
        send(back_out, back_in.at[subs - r], back_sent.at[r], back_got.at[subs - r], beside(0, r))
        for r in range(1, subs)
    ]
    back_in[0] = back_out[...]

    fine[...] = jnp.zeros_like(fine)
    fine[3:22, 3:27, :] = partial[...]
    for n, (dx, dy) in enumerate(SIDES):
        fine_copies[n].wait_recv()
        first = {1: 0, -1: 19, 0: 3}
        size = fine_in[n].shape
        x, y = first[dx], first[dy]
        fine[x : x + size[0], y : y + size[1], :] += fine_in[n][...]

    fold_columns(fine, columns, 19, 24)
    loads[11].wait()
    fine_short = short_range(columns, near, 19, 24)

    middle_wide[...] = jnp.zeros_like(middle_wide)
    middle_wide[3:16, 3:19, :] = middle[...]
    for n, (dx, dy) in enumerate(SIDES):
        middle_copies[n].wait_recv()
        first = {1: 0, -1: 11, 0: 3}
        size = middle_in[n].shape
        x, y = first[dx], first[dy]
        middle_wide[x : x + size[0], y : y + size[1], :] += middle_in[n][...]
    fold_columns(middle_wide, middle_columns, 13, 16)
    loads[12].wait()
    middle_short = short_range(middle_columns, near_middle, 13, 16)

    for n in (1, 3):
        loads[n].wait()
    grid = fine_short + dot_right(dot_left(up, middle_short), up_z)
    for n in (5, 7):
        loads[n].wait()
    for copy in back_copies:
        copy.wait_recv()
    wide = dot_right(back_in[...].reshape(rows, GZ), leave_z)
    grid = grid + dot_left(leave, jnp.concatenate([wide[:, j * GZ : (j + 1) * GZ] for j in range(4)], axis=0))
    for copy in fine_copies:
        copy.wait_send()
    lattice = partial
    lattice[...] = grid.reshape(19, 24, GZ)
    grid_out[...] = lattice[1:17, 1:17, :]

    scalars.wait()
    forms = (((1,), (1,)), ((), ()))
    for a in range(4):
        for b in range(4):
            rows_of = [lattice[4 * a + i, 4 * b : 4 * b + 8, :] for i in range(7)] + [jnp.zeros((8, 128), jnp.float32)]
            high, low = halves(jnp.concatenate(rows_of, axis=0))
            column = lax.dot_general(place_back[...], high, forms, preferred_element_type=jnp.float32)
            column = column + lax.dot_general(place_back[...], low, forms, preferred_element_type=jnp.float32)
            first = (a * 4 + b) * 32
            pair = jnp.concatenate(halves(column.reshape(32, 8, 64)), axis=1)
            table[first : first + 32] = jnp.concatenate([pair, pair], axis=2)
    table[512] = jnp.zeros((16, 128), jnp.bfloat16)

    def interpolate(group, carry):
        for n in range(2 * SENDERS):
            step = group * 2 * SENDERS + n
            sender = lax.rem(me - step + devices, devices)
            for j in range(0, 4, 2):
                slot = step * 4 + j
                first, second = (table[cell_scalars[step, j + m]] for m in range(2))
                none = jnp.zeros_like(first)
                product = dot(
                    jnp.concatenate(
                        [jnp.concatenate([first, none], axis=1), jnp.concatenate([none, second], axis=1)], axis=0
                    ),
                    across[pl.ds(slot, 2)].reshape(256, BLOCK),
                )
                for m in range(2):
                    part = (product[16 * m : 16 * m + 8] + product[16 * m + 8 : 16 * m + 16]) * along[slot + m]
                    potentials[pl.ds(sender * 4 + j + m, 1), :] = jnp.sum(part, axis=0, keepdims=True)
        return carry

    lax.fori_loop(0, groups // 2, interpolate, 0)
    pltpu.make_async_copy(outgoing.at[others], outgoing.at[others], sent).wait()
    pltpu.make_async_copy(cells_out.at[others], cells_out.at[others], cell_sent).wait()
    for copy in middle_copies + mode_copies + line_copies + back_copies:
        copy.wait_send()


def whole(chosen, counts, cells, atoms, slabs, subs):
    tables = [jnp.asarray(table) for table in level_tables(slabs, subs)]
    devices = slabs * subs
    held = [
        pltpu.VMEM(table.shape[1:] if n in PER_SUB else table.shape, table.dtype) for n, table in enumerate(tables)
    ]
    f32 = lambda *shape: pltpu.VMEM(shape, jnp.float32)
    i32 = lambda *shape: pltpu.VMEM(shape, jnp.int32)
    fine_in = [(6, 24), (6, 24), (19, 8), (19, 8)] + [(6, 8)] * 4
    middle_in = [(8, 16), (8, 16), (13, 8), (13, 8)] + [(8, 8)] * 4
    dma = lambda count: pltpu.SemaphoreType.DMA((count,))
    return pl.pallas_call(
        functools.partial(whole_kernel, slabs, subs),
        out_shape=(
            jax.ShapeDtypeStruct((devices * 4, BLOCK), jnp.float32),
            jax.ShapeDtypeStruct((GX, GY, GZ), jnp.float32),
        ),
        in_specs=[SMEM, SMEM, SMEM] + [ANY] * (1 + len(tables)),
        out_specs=(VMEM, VMEM),
        scratch_shapes=held
        + [
            f32(*atoms.shape),
            f32(devices, 16, BLOCK),
            f32(devices, 16, BLOCK),
            i32(devices, 1, BLOCK),
            i32(devices, 1, BLOCK),
            i32(devices, BLOCK),
            pltpu.SMEM((devices, BLOCK), jnp.int32),
            pltpu.VMEM((devices * 4, 128, BLOCK), jnp.bfloat16),
            f32(devices * 4, 8, BLOCK),
            f32(devices * 4 * 8, 128),
            f32(8, 512, 128),
            f32(19, 24, GZ),
            pltpu.VMEM((513, 16, 128), jnp.bfloat16),
        ]
        + [f32(*shape, GZ) for shape in fine_in + middle_in]
        + [
            f32(19, 8, GZ),
            f32(13, 8, GZ),
            f32(13, 16, GZ),
            f32(25, 32, GZ),
            f32(19, 24, GZ),
            f32(4, 25, 24, GZ),
            f32(4, 19, 16, GZ),
            f32(subs, 16, GZ),
            f32(subs, 16, GZ),
            f32(16, GZ),
            f32(slabs, 16, GZ),
            f32(16, GZ),
            f32(subs, 16, GZ),
        ]
        + [dma(len(tables)), pltpu.SemaphoreType.DMA, pltpu.SemaphoreType.DMA, dma(devices)]
        + [pltpu.SemaphoreType.DMA] * 3
        + [dma(8), dma(8), dma(8), dma(8)]
        + [dma(subs), dma(subs), dma(slabs), dma(slabs), dma(subs), dma(subs)],
        compiler_params=pltpu.CompilerParams(collective_id=0, has_side_effects=True, vmem_limit_bytes=60 << 20),
        name="multilevel",
    )(chosen, counts, cells, atoms, *tables)


def finish_kernel(potentials, grid, potentials_out, grid_out, *rest):
    values, sems = rest[:2], rest[2]
    loads = [pltpu.make_async_copy(ref, values[n], sems.at[n]) for n, ref in enumerate((potentials, grid))]
    stores = [pltpu.make_async_copy(values[n], ref, sems.at[n]) for n, ref in enumerate((potentials_out, grid_out))]
    for load in loads:
        load.start()
    for load, store in zip(loads, stores):
        load.wait()
        store.start()
    for store in stores:
        store.wait()


def finish(potentials, grid):
    return pl.pallas_call(
        finish_kernel,
        out_shape=tuple(jax.ShapeDtypeStruct(value.shape, value.dtype) for value in (potentials, grid)),
        in_specs=[ANY, ANY],
        out_specs=(ANY, ANY),
        scratch_shapes=[pltpu.VMEM(value.shape, value.dtype) for value in (potentials, grid)]
        + [pltpu.SemaphoreType.DMA((2,))],
        compiler_params=pltpu.CompilerParams(vmem_limit_bytes=60 << 20),
        name="finish",
    )(potentials, grid)


def body(atom_data, block_cell, send_list, send_count):
    slabs, subs = lax.axis_size("slab"), lax.axis_size("sub")
    return finish(*whole(send_list[0].T, send_count, block_cell, atom_data, slabs, subs))


def solution(mesh):
    placed = (
        P(("slab", "sub"), None, None),
        P(("slab", "sub")),
        P(("slab", "sub"), None, None),
        P(("slab", "sub"), None),
    )
    return jax.shard_map(
        body,
        mesh=mesh,
        in_specs=placed,
        out_specs=(P(("slab", "sub"), None), P("slab", "sub", None)),
        check_vma=False,
    )
```

```python
import functools
import ml_dtypes
import numpy as np
import jax
import jax.numpy as jnp
from jax import lax
from jax.experimental import pallas as pl
from jax.experimental.pallas import tpu as pltpu
from jax.sharding import PartitionSpec as P

BLOCK = 128
SENDERS = 16
ISSUE = 8

GX = 16
GY = 16
GZ = 128
SMEM = pl.BlockSpec(memory_space=pltpu.SMEM)
VMEM = pl.BlockSpec(memory_space=pltpu.VMEM)
ANY = pl.BlockSpec(memory_space=pl.ANY)
MESH = pl.DeviceIdType.MESH


def spline_rows(row, offsets):
    left = jnp.maximum(1.0 - jnp.abs(row - offsets), -1.0)
    inner = left > 0.0
    return left * (0.5 + left * (jnp.where(inner, 2.0, 1.0) + left * jnp.where(inner, -1.5, 0.5)))


def halves(values):
    high = values.astype(jnp.bfloat16)
    low = (values - high.astype(jnp.float32)).astype(jnp.bfloat16)
    return high, low


def cross(first, second):
    rows = [first[i : i + 1, :] * second for i in range(7)]
    return jnp.concatenate(rows + [jnp.zeros_like(second)], axis=0)


def placement_tables():
    table = np.zeros((32, 8, GZ))
    for c in range(32):
        for k in range(7):
            table[c, k, (4 * c + k - 1) % GZ] = 1.0
    exact = table.astype(ml_dtypes.bfloat16)
    return exact.transpose(1, 0, 2).reshape(256, GZ).T, exact.reshape(256, GZ)


def two_parts(table):
    high = table.astype(ml_dtypes.bfloat16)
    low = (table - high.astype(np.float64)).astype(ml_dtypes.bfloat16)
    return np.stack([high, low])


def stencil(offset):
    size = np.abs(offset)
    return np.where(size == 0, 1.0, np.where(size == 1, 0.5625, np.where(size == 3, -0.0625, 0.0)))


def wrapped(offset, length):
    return (offset + length // 2) % length - length // 2


def halve(coarse, fine, coarse_first, fine_first, coarse_rows, fine_rows):
    table = np.zeros((coarse_rows, fine_rows))
    k = coarse_first + np.arange(coarse)[:, None]
    table[:coarse, :fine] = stencil(fine_first + np.arange(fine)[None, :] - 2 * k)
    return table


def halve_ring(coarse):
    return stencil(wrapped(np.arange(2 * coarse)[None, :] - 2 * np.arange(coarse)[:, None], 2 * coarse))


def soften(scaled):
    square = scaled * scaled
    return np.where(scaled < 1.0, (15.0 - 10.0 * square + 3.0 * square * square) / 8.0, 1.0 / np.maximum(scaled, 1.0))


def split_kernel(distance):
    return soften(distance / 2.0) / 2.0 - soften(distance / 4.0) / 4.0


def modes(length):
    angle = 2.0 * np.pi / length * (np.arange(length)[:, None] * np.arange(length)[None, :] % length)
    return (np.cos(angle) + np.sin(angle)) / np.sqrt(length)


RINGS = [(a, b) for a in range(4) for b in range(a, 4)]


def ring_tables(length, scale):
    shift = wrapped(np.arange(length)[:, None] - np.arange(length)[None, :], length)
    out = np.zeros((len(RINGS), GZ, GZ))
    for n, (a, b) in enumerate(RINGS):
        values = scale * split_kernel(np.sqrt(a * a + b * b + shift * shift))
        out[n, :length, :length] = np.where(np.abs(shift) <= 3, values, 0.0)
    return out.reshape(len(RINGS) * GZ, GZ)


def level_tables(slabs, subs):
    exact = lambda table: table.astype(ml_dtypes.bfloat16)
    down = np.kron(halve(13, 19, -2, -1, 13, 19), halve(13, 19, -2, -1, 16, 24))
    down_z = np.zeros((GZ, GZ))
    down_z[:, :64] = halve_ring(64).T
    top_x = halve(9, 13, -2, -2, 16, 13) @ halve(13, 19, -2, -1, 13, 19)
    top_y = halve(9, 13, -2, -2, 9, 16) @ halve(13, 19, -2, -1, 16, 24)
    top_z = halve_ring(32) @ halve_ring(64)
    wave_x, wave_y, wave_z = modes(4 * slabs), modes(4 * subs), modes(32)
    reach = np.arange(9) - 2
    enter = []
    for sub in range(subs):
        rows = 4 * ((sub + np.arange(subs)[None, :]) % subs) + np.arange(4)[:, None]
        along = wave_y[rows][:, :, (4 * sub + reach) % (4 * subs)] @ top_y
        enter.append(np.einsum("jrm,xn->jrxnm", along, top_x).reshape(4 * subs * 16, 19 * 24))
    enter = np.stack(enter)
    enter_z = np.tile((wave_z @ top_z).T, (1, 4))
    leave_z = np.kron(np.eye(4), wave_z @ top_z)
    mode_x = np.zeros((4 * slabs, slabs, 16))
    for r in range(slabs):
        mode_x[:, r, :9] = wave_x[:, (4 * r + reach) % (4 * slabs)]
    back_x = np.zeros((16, 4 * slabs))
    back_x[:9] = wave_x[:, reach % (4 * slabs)].T
    squared = 0.0
    for dimension, length in enumerate((4 * slabs, 4 * subs, 32)):
        shape = [1, 1, 1]
        shape[dimension] = length
        squared = squared + (wrapped(np.arange(length), length) ** 2).reshape(shape)
    spectrum = np.fft.fftn(soften(np.sqrt(squared) / 2.0) / 8.0).real
    spectrum = spectrum.reshape(4 * slabs, subs, 128).transpose(1, 0, 2).astype(np.float32)
    return placement_tables() + (
        exact(down),
        exact(down.T),
        exact(down_z),
        exact(down_z.T),
        two_parts(enter).transpose(1, 0, 2, 3),
        two_parts(enter.transpose(0, 2, 1)).transpose(1, 0, 2, 3),
        two_parts(enter_z),
        two_parts(leave_z),
        two_parts(mode_x.reshape(4 * slabs, slabs * 16)),
        two_parts(back_x),
        spectrum,
        two_parts(ring_tables(GZ, 1.0)),
        two_parts(ring_tables(GZ // 2, 0.5)),
    )


PER_SUB = (6, 7, 12)


def dot(a, b):
    return jnp.dot(a, b, preferred_element_type=jnp.float32)


def dot_right(values, table):
    high, low = halves(values)
    if len(table.shape) == 2:
        return dot(high, table[...]) + dot(low, table[...])
    return dot(high, table[0]) + dot(low, table[0]) + dot(high, table[1])


def dot_left(table, values):
    high, low = halves(values)
    if len(table.shape) == 2:
        return dot(table[...], high) + dot(table[...], low)
    return dot(table[0], high) + dot(table[0], low) + dot(table[1], high)


def fold_columns(lattice, columns, planes, rows):
    columns[0] = lattice[:, 3 : 3 + rows, :]
    for b in range(1, 4):
        columns[b] = lattice[:, 3 - b : 3 - b + rows, :] + lattice[:, 3 + b : 3 + b + rows, :]


def short_range(columns, table, planes, rows):
    def sides(a, b):
        if a == 0:
            return columns[b, 3 : 3 + planes]
        return columns[b, 3 - a : 3 - a + planes] + columns[b, 3 + a : 3 + a + planes]

    total = None
    for n in range(0, len(RINGS), 2):
        parts = []
        for a, b in RINGS[n : n + 2]:
            part = sides(a, b) if a == b else sides(a, b) + sides(b, a)
            parts.append(halves(part.reshape(planes * rows, GZ)))
        high, low = (jnp.concatenate([part[m] for part in parts], axis=1) for m in range(2))
        span = pl.ds(n * GZ, 2 * GZ)
        here = dot(high, table[0, span, :]) + dot(low, table[0, span, :]) + dot(high, table[1, span, :])
        total = here if total is None else total + here
    return total


SIDES = [(1, 0), (-1, 0), (0, 1), (0, -1), (1, 1), (1, -1), (-1, 1), (-1, -1)]


def whole_kernel(slabs, subs, chosen, counts, cells, atoms, *refs):
    tables = refs[:15]
    potentials, grid_out = refs[15:17]
    rest = list(refs[17:])
    take = lambda count: [rest.pop(0) for _ in range(count)]
    held = take(15)
    atoms_held, outgoing, incoming, cells_out, cells_in, cell_block, cell_scalars = take(7)
    across, along, patches, cell_sums, partial, table = take(6)
    fine_in, middle_in = take(8), take(8)
    edge, middle, fine, middle_wide, columns, middle_columns, rim_x, rim_y, rim_corner = take(9)
    modes_out, modes_in, line_out, line_in, back_out, back_in = take(6)
    load_sem, atoms_sem, sent, got, cell_sent, cell_got, scalar_sem = take(7)
    fine_sent, fine_got, middle_sent, middle_got, in_sent, in_got, line_sent, line_got, back_sent, back_got = rest
    devices = slabs * subs
    slab = lax.axis_index("slab")
    sub = lax.axis_index("sub")
    me = slab * subs + sub

    def beside(dx, dy):
        return (lax.rem(slab + dx + slabs, slabs), lax.rem(sub + dy + subs, subs))

    def send(source, target_ref, sent, got, target):
        copy = pltpu.make_async_remote_copy(source, target_ref, sent, got, device_id=target, device_id_type=MESH)
        copy.start()
        return copy

    atoms_load = pltpu.make_async_copy(atoms, atoms_held, atoms_sem)
    atoms_load.start()
    barrier = pltpu.get_barrier_semaphore()

    def peer_of(step):
        peer = lax.rem(me + step, devices)
        return peer, (peer // subs, lax.rem(peer, subs))

    def in_groups(act):
        def several(group, carry):
            for n in range(ISSUE):
                act(group * ISSUE + n)
            return carry

        for step in range(1, ISSUE):
            act(step)
        lax.fori_loop(1, devices // ISSUE, several, 0)

    def greet(step):
        pl.semaphore_signal(barrier, inc=1, device_id=peer_of(step)[1], device_id_type=MESH)

    in_groups(greet)
    loads = [
        pltpu.make_async_copy(table_ref.at[sub] if n in PER_SUB else table_ref, held[n], load_sem.at[n])
        for n, table_ref in enumerate(tables)
    ]
    for load in loads:
        load.start()
    place_in, place_back = held[:2]
    loads_of_levels = loads[2:]

    atoms_load.wait()
    lane = lax.broadcasted_iota(jnp.int32, (1, BLOCK), 1)

    def pick(row, carry):
        for n in range(subs):
            peer = row * subs + n
            line = jnp.full((1, BLOCK), 512, jnp.int32)
            for j in range(4):
                index = chosen[j, peer]
                outgoing[peer, pl.ds(4 * j, 4), :] = atoms_held[index]
                cell = cells[index]
                local = ((cell >> 10) & 3) * 128 + ((cell >> 5) & 3) * 32 + (cell & 31)
                line = jnp.where(lane == j, jnp.where(counts[0, peer] > j, local, 512), line)
            cells_out[peer] = line
        return carry

    lax.fori_loop(0, slabs, pick, 0)
    pl.semaphore_wait(barrier, devices - 1)

    def start(step):
        peer, target = peer_of(step)
        send(cells_out.at[peer], cells_in.at[step], cell_sent, cell_got, target)
        send(outgoing.at[peer], incoming.at[step], sent, got.at[step], target)

    in_groups(start)
    own = pltpu.make_async_copy(outgoing.at[me], incoming.at[0], got.at[0])
    own.start()
    cells_in[0] = cells_out[me]

    offsets = lax.broadcasted_iota(jnp.int32, (8, BLOCK), 0).astype(jnp.float32) - 1.0

    def spread(group, carry):
        for n in range(SENDERS):
            step = group * SENDERS + n
            pltpu.make_async_copy(incoming.at[step], incoming.at[step], got.at[step]).wait()
        parts = []
        for n in range(SENDERS):
            step = group * SENDERS + n
            for j in range(4):
                wx, wy, wz = (spline_rows(incoming[step, pl.ds(4 * j + d, 1), :], offsets) for d in range(3))
                charge = incoming[step, pl.ds(4 * j + 3, 1), :]
                high, low = halves(cross(wx, wy))
                slot = step * 4 + j
                across[slot, 0:64, :] = high
                across[slot, 64:128, :] = low
                along[slot] = wz
                both = jnp.concatenate(halves(wz * charge), axis=0)
                product = lax.dot_general(
                    jnp.concatenate([both, both], axis=1),
                    jnp.concatenate([high, low], axis=1),
                    (((1,), (1,)), ((), ())),
                    preferred_element_type=jnp.float32,
                )
                parts.append((step, j, product[0:8] + product[8:16]))
        for step, j, part in parts:
            patches[pl.ds(pl.multiple_of((j * devices + step) * 8, 8), 8), 0:64] = part
        return carry

    groups = devices // SENDERS
    lax.fori_loop(0, groups, spread, 0)
    others = pl.ds(1, devices - 1)
    pltpu.make_async_copy(cells_in.at[others], cells_in.at[others], cell_got).wait()
    cell_block[...] = cells_in[:, 0, :]
    scalars = pltpu.make_async_copy(cell_block, cell_scalars, scalar_sem)
    scalars.start()

    slots_across = cell_block[...].T
    cell_number = lax.broadcasted_iota(jnp.int32, (512, devices), 0)
    member = jnp.concatenate(
        [(cell_number == slots_across[j : j + 1, :]).astype(jnp.float32).astype(jnp.bfloat16) for j in range(4)], axis=1
    )
    for k in range(8):
        sums = dot(member, jnp.concatenate(halves(patches[pl.ds(k, devices * 4, stride=8), :]), axis=1))
        cell_sums[k] = sums[:, :128] + sums[:, 128:]
    partial[...] = jnp.zeros_like(partial)
    loads[0].wait()
    loads[1].wait()
    for a in range(4):
        for b in range(4):
            first = (a * 4 + b) * 32
            column = cell_sums[:, first : first + 32, :].reshape(256, 128)
            planes = dot_left(place_in, column).T
            for i in range(7):
                partial[4 * a + i, 4 * b : 4 * b + 8, :] += planes[8 * i : 8 * i + 8]

    loads = loads_of_levels
    down, up, down_z, up_z, enter, leave, enter_z, leave_z, mode_x, back_x, spectrum, near, near_middle = held[2:]

    for n in (4, 6):
        loads[n].wait()
    rows = 16 * subs
    spread_modes = dot_left(enter, dot_right(partial[...].reshape(19 * 24, GZ), enter_z))
    group_of_lane = lax.broadcasted_iota(jnp.int32, (rows, GZ), 1) // 32
    packed = spread_modes[0:rows]
    for j in range(1, 4):
        packed = jnp.where(group_of_lane == j, spread_modes[j * rows : (j + 1) * rows], packed)
    modes_out[...] = packed.reshape(subs, 16, GZ)
    mode_copies = [
        send(modes_out.at[r], modes_in.at[subs - r], in_sent.at[r], in_got.at[subs - r], beside(0, r))
        for r in range(1, subs)
    ]

    edge[...] = partial[:, 13:21, :]

    low, high = pl.ds(0, 6), pl.ds(13, 6)
    near_rows = pl.ds(0, 8)
    sources = [
        partial.at[high], partial.at[low], edge, partial.at[:, near_rows, :],
        edge.at[high], partial.at[high, near_rows, :], edge.at[low], partial.at[low, near_rows, :],
    ]
    fine_copies = [
        send(source, fine_in[n], fine_sent.at[n], fine_got.at[n], beside(*SIDES[n])) for n, source in enumerate(sources)
    ]

    for n in (0, 2):
        loads[n].wait()
    middle[...] = dot_left(down, dot_right(partial[...].reshape(19 * 24, GZ), down_z)).reshape(13, 16, GZ)

    def pair_planes(values, count):
        return values[:count] + pltpu.roll(values[count:], 64, 2)

    high_x = pair_planes(middle[5:13], 4)
    low_x = pair_planes(middle[0:8], 4)
    rim_x[0] = high_x
    rim_x[1] = low_x
    rim_y[0, 0:7] = middle[0:7, 5:13, :]
    rim_y[0, 0:6] += pltpu.roll(middle[7:13, 5:13, :], 64, 2)
    rim_y[1, 0:7] = middle[0:7, 0:8, :]
    rim_y[1, 0:6] += pltpu.roll(middle[7:13, 0:8, :], 64, 2)
    rim_corner[0] = high_x[:, 5:13, :]
    rim_corner[1] = low_x[:, 5:13, :]
    sources = [
        rim_x.at[0], rim_x.at[1], rim_y.at[0], rim_y.at[1],
        rim_corner.at[0], rim_x.at[0, :, near_rows, :], rim_corner.at[1], rim_x.at[1, :, near_rows, :],
    ]
    middle_copies = [
        send(source, middle_in[n], middle_sent.at[n], middle_got.at[n], beside(*SIDES[n]))
        for n, source in enumerate(sources)
    ]

    for copy in mode_copies:
        copy.wait_recv()
    total = modes_out[0]
    for r in range(1, subs):
        total = total + modes_in[r]
    line_out[...] = total
    line_copies = [
        send(line_out, line_in.at[slabs - r], line_sent.at[r], line_got.at[slabs - r], beside(r, 0))
        for r in range(1, slabs)
    ]
    line_in[0] = total

    fine[...] = jnp.zeros_like(fine)
    fine[3:22, 3:27, :] = partial[...]
    for n, (dx, dy) in enumerate(SIDES):
        fine_copies[n].wait_recv()
        first = {1: 0, -1: 19, 0: 3}
        size = fine_in[n].shape
        x, y = first[dx], first[dy]
        fine[x : x + size[0], y : y + size[1], :] += fine_in[n][...]

    fold_columns(fine, columns, 19, 24)
    loads[11].wait()
    fine_short = short_range(columns, near, 19, 24)

    for n in (8, 9, 10):
        loads[n].wait()
    for copy in line_copies:
        copy.wait_recv()
    in_modes = dot_left(mode_x, line_in[...].reshape(slabs * 16, GZ)) * spectrum[...]
    back_out[...] = dot_left(back_x, in_modes)
    back_copies = [
        send(back_out, back_in.at[subs - r], back_sent.at[r], back_got.at[subs - r], beside(0, r))
        for r in range(1, subs)
    ]
    back_in[0] = back_out[...]

    middle_wide[...] = jnp.zeros_like(middle_wide)
    middle_wide[3:16, 3:19, :] = middle[...]
    for n, (dx, dy) in enumerate(SIDES):
        middle_copies[n].wait_recv()
        first = {1: 0, -1: 11, 0: 3}
        size = middle_in[n].shape
        x, y, span = first[dx], first[dy], size[0] if dx else 6
        middle_wide[x : x + size[0], y : y + size[1], :] += middle_in[n][...]
        x = x + size[0]
        middle_wide[x : x + span, y : y + size[1], :] += pltpu.roll(middle_in[n][0:span], 64, 2)
    fold_columns(middle_wide, middle_columns, 13, 16)
    loads[12].wait()
    middle_short = short_range(middle_columns, near_middle, 13, 16)

    for n in (1, 3):
        loads[n].wait()
    grid = fine_short + dot_right(dot_left(up, middle_short), up_z)
    for n in (5, 7):
        loads[n].wait()
    for copy in back_copies:
        copy.wait_recv()
    wide = dot_right(back_in[...].reshape(rows, GZ), leave_z)
    grid = grid + dot_left(leave, jnp.concatenate([wide[:, j * GZ : (j + 1) * GZ] for j in range(4)], axis=0))
    for copy in fine_copies:
        copy.wait_send()
    lattice = partial
    lattice[...] = grid.reshape(19, 24, GZ)
    grid_out[...] = lattice[1:17, 1:17, :]

    scalars.wait()
    forms = (((1,), (1,)), ((), ()))
    for a in range(4):
        for b in range(4):
            rows_of = [lattice[4 * a + i, 4 * b : 4 * b + 8, :] for i in range(7)] + [jnp.zeros((8, 128), jnp.float32)]
            high, low = halves(jnp.concatenate(rows_of, axis=0))
            column = lax.dot_general(place_back[...], high, forms, preferred_element_type=jnp.float32)
            column = column + lax.dot_general(place_back[...], low, forms, preferred_element_type=jnp.float32)
            first = (a * 4 + b) * 32
            pair = jnp.concatenate(halves(column.reshape(32, 8, 64)), axis=1)
            table[first : first + 32] = jnp.concatenate([pair, pair], axis=2)
    table[512] = jnp.zeros((16, 128), jnp.bfloat16)

    def interpolate(group, carry):
        for n in range(SENDERS):
            step = group * SENDERS + n
            sender = lax.rem(me - step + devices, devices)
            for j in range(0, 4, 2):
                slot = step * 4 + j
                first, second = (table[cell_scalars[step, j + m]] for m in range(2))
                none = jnp.zeros_like(first)
                product = dot(
                    jnp.concatenate(
                        [jnp.concatenate([first, none], axis=1), jnp.concatenate([none, second], axis=1)], axis=0
                    ),
                    across[pl.ds(slot, 2)].reshape(256, BLOCK),
                )
                for m in range(2):
                    part = (product[16 * m : 16 * m + 8] + product[16 * m + 8 : 16 * m + 16]) * along[slot + m]
                    potentials[pl.ds(sender * 4 + j + m, 1), :] = jnp.sum(part, axis=0, keepdims=True)
        return carry

    lax.fori_loop(0, groups, interpolate, 0)
    pltpu.make_async_copy(outgoing.at[others], outgoing.at[others], sent).wait()
    pltpu.make_async_copy(cells_out.at[others], cells_out.at[others], cell_sent).wait()
    for copy in middle_copies + mode_copies + line_copies + back_copies:
        copy.wait_send()


def whole(chosen, counts, cells, atoms, slabs, subs):
    tables = [jnp.asarray(table) for table in level_tables(slabs, subs)]
    devices = slabs * subs
    held = [
        pltpu.VMEM(table.shape[1:] if n in PER_SUB else table.shape, table.dtype) for n, table in enumerate(tables)
    ]
    f32 = lambda *shape: pltpu.VMEM(shape, jnp.float32)
    i32 = lambda *shape: pltpu.VMEM(shape, jnp.int32)
    fine_in = [(6, 24), (6, 24), (19, 8), (19, 8)] + [(6, 8)] * 4
    middle_in = [(4, 16), (4, 16), (7, 8), (7, 8)] + [(4, 8)] * 4
    dma = lambda count: pltpu.SemaphoreType.DMA((count,))
    return pl.pallas_call(
        functools.partial(whole_kernel, slabs, subs),
        out_shape=(
            jax.ShapeDtypeStruct((devices * 4, BLOCK), jnp.float32),
            jax.ShapeDtypeStruct((GX, GY, GZ), jnp.float32),
        ),
        in_specs=[SMEM, SMEM, SMEM] + [ANY] * (1 + len(tables)),
        out_specs=(VMEM, VMEM),
        scratch_shapes=held
        + [
            f32(*atoms.shape),
            f32(devices, 16, BLOCK),
            f32(devices, 16, BLOCK),
            i32(devices, 1, BLOCK),
            i32(devices, 1, BLOCK),
            i32(devices, BLOCK),
            pltpu.SMEM((devices, BLOCK), jnp.int32),
            pltpu.VMEM((devices * 4, 128, BLOCK), jnp.bfloat16),
            f32(devices * 4, 8, BLOCK),
            f32(devices * 4 * 8, 128),
            f32(8, 512, 128),
            f32(19, 24, GZ),
            pltpu.VMEM((513, 16, 128), jnp.bfloat16),
        ]
        + [f32(*shape, GZ) for shape in fine_in + middle_in]
        + [
            f32(19, 8, GZ),
            f32(13, 16, GZ),
            f32(25, 32, GZ),
            f32(19, 24, GZ),
            f32(4, 25, 24, GZ),
            f32(4, 19, 16, GZ),
            f32(2, 4, 16, GZ),
            f32(2, 7, 8, GZ),
            f32(2, 4, 8, GZ),
            f32(subs, 16, GZ),
            f32(subs, 16, GZ),
            f32(16, GZ),
            f32(slabs, 16, GZ),
            f32(16, GZ),
            f32(subs, 16, GZ),
        ]
        + [dma(len(tables)), pltpu.SemaphoreType.DMA, pltpu.SemaphoreType.DMA, dma(devices)]
        + [pltpu.SemaphoreType.DMA] * 3
        + [dma(8), dma(8), dma(8), dma(8)]
        + [dma(subs), dma(subs), dma(slabs), dma(slabs), dma(subs), dma(subs)],
        compiler_params=pltpu.CompilerParams(collective_id=0, has_side_effects=True, vmem_limit_bytes=60 << 20),
        name="multilevel",
    )(chosen, counts, cells, atoms, *tables)


def finish_kernel(potentials, grid, potentials_out, grid_out, *rest):
    values, sems = rest[:2], rest[2]
    loads = [pltpu.make_async_copy(ref, values[n], sems.at[n]) for n, ref in enumerate((potentials, grid))]
    stores = [pltpu.make_async_copy(values[n], ref, sems.at[n]) for n, ref in enumerate((potentials_out, grid_out))]
    for load in loads:
        load.start()
    for load, store in zip(loads, stores):
        load.wait()
        store.start()
    for store in stores:
        store.wait()


def finish(potentials, grid):
    return pl.pallas_call(
        finish_kernel,
        out_shape=tuple(jax.ShapeDtypeStruct(value.shape, value.dtype) for value in (potentials, grid)),
        in_specs=[ANY, ANY],
        out_specs=(ANY, ANY),
        scratch_shapes=[pltpu.VMEM(value.shape, value.dtype) for value in (potentials, grid)]
        + [pltpu.SemaphoreType.DMA((2,))],
        compiler_params=pltpu.CompilerParams(vmem_limit_bytes=60 << 20),
        name="finish",
    )(potentials, grid)


def body(atom_data, block_cell, send_list, send_count):
    slabs, subs = lax.axis_size("slab"), lax.axis_size("sub")
    return finish(*whole(send_list[0].T, send_count, block_cell, atom_data, slabs, subs))


def solution(mesh):
    placed = (
        P(("slab", "sub"), None, None),
        P(("slab", "sub")),
        P(("slab", "sub"), None, None),
        P(("slab", "sub"), None),
    )
    return jax.shard_map(
        body,
        mesh=mesh,
        in_specs=placed,
        out_specs=(P(("slab", "sub"), None), P("slab", "sub", None)),
        check_vma=False,
    )
```

```python
import functools
import ml_dtypes
import numpy as np
import jax
import jax.numpy as jnp
from jax import lax
from jax.experimental import pallas as pl
from jax.experimental.pallas import tpu as pltpu
from jax.sharding import PartitionSpec as P

BLOCK = 128
SENDERS = 16
ISSUE = 8
STRIDE = 77

GX = 16
GY = 16
GZ = 128
SMEM = pl.BlockSpec(memory_space=pltpu.SMEM)
VMEM = pl.BlockSpec(memory_space=pltpu.VMEM)
ANY = pl.BlockSpec(memory_space=pl.ANY)
MESH = pl.DeviceIdType.MESH


def spline_rows(row, offsets):
    left = jnp.maximum(1.0 - jnp.abs(row - offsets), -1.0)
    inner = left > 0.0
    return left * (0.5 + left * (jnp.where(inner, 2.0, 1.0) + left * jnp.where(inner, -1.5, 0.5)))


def halves(values):
    high = values.astype(jnp.bfloat16)
    low = (values - high.astype(jnp.float32)).astype(jnp.bfloat16)
    return high, low


def cross(first, second):
    rows = [first[i : i + 1, :] * second for i in range(7)]
    return jnp.concatenate(rows + [jnp.zeros_like(second)], axis=0)


def placement_tables():
    table = np.zeros((32, 8, GZ))
    for c in range(32):
        for k in range(7):
            table[c, k, (4 * c + k - 1) % GZ] = 1.0
    exact = table.astype(ml_dtypes.bfloat16)
    return exact.transpose(1, 0, 2).reshape(256, GZ).T, exact.reshape(256, GZ)


def two_parts(table):
    high = table.astype(ml_dtypes.bfloat16)
    low = (table - high.astype(np.float64)).astype(ml_dtypes.bfloat16)
    return np.stack([high, low])


def stencil(offset):
    size = np.abs(offset)
    return np.where(size == 0, 1.0, np.where(size == 1, 0.5625, np.where(size == 3, -0.0625, 0.0)))


def wrapped(offset, length):
    return (offset + length // 2) % length - length // 2


def halve(coarse, fine, coarse_first, fine_first, coarse_rows, fine_rows):
    table = np.zeros((coarse_rows, fine_rows))
    k = coarse_first + np.arange(coarse)[:, None]
    table[:coarse, :fine] = stencil(fine_first + np.arange(fine)[None, :] - 2 * k)
    return table


def halve_ring(coarse):
    return stencil(wrapped(np.arange(2 * coarse)[None, :] - 2 * np.arange(coarse)[:, None], 2 * coarse))


def soften(scaled):
    square = scaled * scaled
    return np.where(scaled < 1.0, (15.0 - 10.0 * square + 3.0 * square * square) / 8.0, 1.0 / np.maximum(scaled, 1.0))


def split_kernel(distance):
    return soften(distance / 2.0) / 2.0 - soften(distance / 4.0) / 4.0


def modes(length):
    angle = 2.0 * np.pi / length * (np.arange(length)[:, None] * np.arange(length)[None, :] % length)
    return (np.cos(angle) + np.sin(angle)) / np.sqrt(length)


RINGS = [(a, b) for a in range(4) for b in range(a, 4)]


def ring_tables(length, scale):
    shift = wrapped(np.arange(length)[:, None] - np.arange(length)[None, :], length)
    out = np.zeros((len(RINGS), GZ, GZ))
    for n, (a, b) in enumerate(RINGS):
        values = scale * split_kernel(np.sqrt(a * a + b * b + shift * shift))
        out[n, :length, :length] = np.where(np.abs(shift) <= 3, values, 0.0)
    return out.reshape(len(RINGS) * GZ, GZ)


def level_tables(slabs, subs):
    exact = lambda table: table.astype(ml_dtypes.bfloat16)
    down = np.kron(halve(13, 19, -2, -1, 13, 19), halve(13, 19, -2, -1, 16, 24))
    down_z = np.zeros((GZ, GZ))
    down_z[:, :64] = halve_ring(64).T
    top_x = halve(9, 13, -2, -2, 16, 13) @ halve(13, 19, -2, -1, 13, 19)
    top_y = halve(9, 13, -2, -2, 9, 16) @ halve(13, 19, -2, -1, 16, 24)
    top_z = halve_ring(32) @ halve_ring(64)
    wave_x, wave_y, wave_z = modes(4 * slabs), modes(4 * subs), modes(32)
    reach = np.arange(9) - 2
    enter = []
    for sub in range(subs):
        rows = 4 * ((sub + np.arange(subs)[None, :]) % subs) + np.arange(4)[:, None]
        along = wave_y[rows][:, :, (4 * sub + reach) % (4 * subs)] @ top_y
        enter.append(np.einsum("jrm,xn->jrxnm", along, top_x).reshape(4 * subs * 16, 19 * 24))
    enter = np.stack(enter)
    enter_z = np.tile((wave_z @ top_z).T, (1, 4))
    leave_z = np.kron(np.eye(4), wave_z @ top_z)
    mode_x = np.zeros((4 * slabs, slabs, 16))
    for r in range(slabs):
        mode_x[:, r, :9] = wave_x[:, (4 * r + reach) % (4 * slabs)]
    back_x = np.zeros((16, 4 * slabs))
    back_x[:9] = wave_x[:, reach % (4 * slabs)].T
    squared = 0.0
    for dimension, length in enumerate((4 * slabs, 4 * subs, 32)):
        shape = [1, 1, 1]
        shape[dimension] = length
        squared = squared + (wrapped(np.arange(length), length) ** 2).reshape(shape)
    spectrum = np.fft.fftn(soften(np.sqrt(squared) / 2.0) / 8.0).real
    spectrum = spectrum.reshape(4 * slabs, subs, 128).transpose(1, 0, 2).astype(np.float32)
    return placement_tables() + (
        exact(down),
        exact(down.T),
        exact(down_z),
        exact(down_z.T),
        two_parts(enter).transpose(1, 0, 2, 3),
        two_parts(enter.transpose(0, 2, 1)).transpose(1, 0, 2, 3),
        two_parts(enter_z),
        two_parts(leave_z),
        two_parts(mode_x.reshape(4 * slabs, slabs * 16)),
        two_parts(back_x),
        spectrum,
        two_parts(ring_tables(GZ, 1.0)),
        two_parts(ring_tables(GZ // 2, 0.5)),
    )


PER_SUB = (6, 7, 12)


def dot(a, b):
    return jnp.dot(a, b, preferred_element_type=jnp.float32)


def dot_right(values, table):
    high, low = halves(values)
    if len(table.shape) == 2:
        return dot(high, table[...]) + dot(low, table[...])
    return dot(high, table[0]) + dot(low, table[0]) + dot(high, table[1])


def dot_left(table, values):
    high, low = halves(values)
    if len(table.shape) == 2:
        return dot(table[...], high) + dot(table[...], low)
    return dot(table[0], high) + dot(table[0], low) + dot(table[1], high)


def fold_columns(lattice, columns, planes, rows):
    columns[0] = lattice[:, 3 : 3 + rows, :]
    for b in range(1, 4):
        columns[b] = lattice[:, 3 - b : 3 - b + rows, :] + lattice[:, 3 + b : 3 + b + rows, :]


def short_range(columns, table, planes, rows):
    def sides(a, b):
        if a == 0:
            return columns[b, 3 : 3 + planes]
        return columns[b, 3 - a : 3 - a + planes] + columns[b, 3 + a : 3 + a + planes]

    total = None
    for n in range(0, len(RINGS), 2):
        parts = []
        for a, b in RINGS[n : n + 2]:
            part = sides(a, b) if a == b else sides(a, b) + sides(b, a)
            parts.append(halves(part.reshape(planes * rows, GZ)))
        high, low = (jnp.concatenate([part[m] for part in parts], axis=1) for m in range(2))
        span = pl.ds(n * GZ, 2 * GZ)
        here = dot(high, table[0, span, :]) + dot(low, table[0, span, :]) + dot(high, table[1, span, :])
        total = here if total is None else total + here
    return total


SIDES = [(1, 0), (-1, 0), (0, 1), (0, -1), (1, 1), (1, -1), (-1, 1), (-1, -1)]


def whole_kernel(slabs, subs, chosen, counts, cells, atoms, *refs):
    tables = refs[:15]
    potentials, grid_out = refs[15:17]
    rest = list(refs[17:])
    take = lambda count: [rest.pop(0) for _ in range(count)]
    held = take(15)
    atoms_held, outgoing, incoming, cells_out, cells_in, cell_block, cell_scalars = take(7)
    across, along, patches, cell_sums, partial, table = take(6)
    fine_in, middle_in = take(8), take(8)
    edge, middle, fine, middle_wide, columns, middle_columns, rim_x, rim_y, rim_corner = take(9)
    modes_out, modes_in, line_out, line_in, back_out, back_in = take(6)
    ready, load_sem, atoms_sem, sent, got, cell_sent, cell_got, scalar_sem = take(8)
    fine_sent, fine_got, middle_sent, middle_got, in_sent, in_got, line_sent, line_got, back_sent, back_got = rest
    devices = slabs * subs
    slab = lax.axis_index("slab")
    sub = lax.axis_index("sub")
    me = slab * subs + sub

    def beside(dx, dy):
        return (lax.rem(slab + dx + slabs, slabs), lax.rem(sub + dy + subs, subs))

    def send(source, target_ref, sent, got, target):
        copy = pltpu.make_async_remote_copy(source, target_ref, sent, got, device_id=target, device_id_type=MESH)
        copy.start()
        return copy

    atoms_load = pltpu.make_async_copy(atoms, atoms_held, atoms_sem)
    atoms_load.start()
    barrier = pltpu.get_barrier_semaphore()

    def peer_of(step):
        peer = lax.rem(me + step * STRIDE, devices)
        return peer, (peer // subs, lax.rem(peer, subs))

    def in_groups(act):
        def several(group, carry):
            for n in range(ISSUE):
                act(group * ISSUE + n)
            return carry

        for step in range(1, ISSUE):
            act(step)
        lax.fori_loop(1, devices // ISSUE, several, 0)

    lines = [beside(r, 0) for r in range(1, slabs)] + [beside(0, r) for r in range(1, subs)]
    for target in lines:
        pl.semaphore_signal(barrier, inc=1, device_id=target, device_id_type=MESH)
    loads = [
        pltpu.make_async_copy(table_ref.at[sub] if n in PER_SUB else table_ref, held[n], load_sem.at[n])
        for n, table_ref in enumerate(tables)
    ]
    for load in loads:
        load.start()
    place_in, place_back = held[:2]
    loads_of_levels = loads[2:]

    atoms_load.wait()
    lane = lax.broadcasted_iota(jnp.int32, (1, BLOCK), 1)

    def pick(row, carry):
        for n in range(subs):
            peer = row * subs + n
            line = jnp.full((1, BLOCK), 512, jnp.int32)
            for j in range(4):
                index = chosen[j, peer]
                outgoing[peer, pl.ds(4 * j, 4), :] = atoms_held[index]
                cell = cells[index]
                local = ((cell >> 10) & 3) * 128 + ((cell >> 5) & 3) * 32 + (cell & 31)
                line = jnp.where(lane == j, jnp.where(counts[0, peer] > j, local, 512), line)
            cells_out[peer] = line
        return carry

    pl.semaphore_wait(barrier, len(lines))
    for r in range(1, subs):
        pl.semaphore_signal(ready, inc=1, device_id=beside(0, r), device_id_type=MESH)
    lax.fori_loop(0, slabs, pick, 0)
    pl.semaphore_wait(ready, subs - 1)

    def start(step):
        peer, target = peer_of(step)
        send(outgoing.at[peer], incoming.at[step], sent, got.at[step], target)
        send(cells_out.at[peer], cells_in.at[step], cell_sent, cell_got, target)

    in_groups(start)
    own = pltpu.make_async_copy(outgoing.at[me], incoming.at[0], got.at[0])
    own.start()
    cells_in[0] = cells_out[me]

    offsets = lax.broadcasted_iota(jnp.int32, (8, BLOCK), 0).astype(jnp.float32) - 1.0

    def spread(group, carry):
        for n in range(SENDERS):
            step = group * SENDERS + n
            pltpu.make_async_copy(incoming.at[step], incoming.at[step], got.at[step]).wait()
        parts = []
        for n in range(SENDERS):
            step = group * SENDERS + n
            for j in range(4):
                wx, wy, wz = (spline_rows(incoming[step, pl.ds(4 * j + d, 1), :], offsets) for d in range(3))
                charge = incoming[step, pl.ds(4 * j + 3, 1), :]
                high, low = halves(cross(wx, wy))
                slot = step * 4 + j
                across[slot, 0:64, :] = high
                across[slot, 64:128, :] = low
                along[slot] = wz
                both = jnp.concatenate(halves(wz * charge), axis=0)
                product = lax.dot_general(
                    jnp.concatenate([both, both], axis=1),
                    jnp.concatenate([high, low], axis=1),
                    (((1,), (1,)), ((), ())),
                    preferred_element_type=jnp.float32,
                )
                parts.append((step, j, product[0:8] + product[8:16]))
        for step, j, part in parts:
            patches[pl.ds(pl.multiple_of((j * devices + step) * 8, 8), 8), 0:64] = part
        return carry

    groups = devices // SENDERS
    lax.fori_loop(0, groups, spread, 0)
    others = pl.ds(1, devices - 1)
    pltpu.make_async_copy(cells_in.at[others], cells_in.at[others], cell_got).wait()
    cell_block[...] = cells_in[:, 0, :]
    scalars = pltpu.make_async_copy(cell_block, cell_scalars, scalar_sem)
    scalars.start()

    slots_across = cell_block[...].T
    cell_number = lax.broadcasted_iota(jnp.int32, (512, devices), 0)
    member = jnp.concatenate(
        [(cell_number == slots_across[j : j + 1, :]).astype(jnp.float32).astype(jnp.bfloat16) for j in range(4)], axis=1
    )
    for k in range(8):
        sums = dot(member, jnp.concatenate(halves(patches[pl.ds(k, devices * 4, stride=8), :]), axis=1))
        cell_sums[k] = sums[:, :128] + sums[:, 128:]
    partial[...] = jnp.zeros_like(partial)
    loads[0].wait()
    loads[1].wait()
    for a in range(4):
        for b in range(4):
            first = (a * 4 + b) * 32
            column = cell_sums[:, first : first + 32, :].reshape(256, 128)
            planes = dot_left(place_in, column).T
            for i in range(7):
                partial[4 * a + i, 4 * b : 4 * b + 8, :] += planes[8 * i : 8 * i + 8]

    loads = loads_of_levels
    down, up, down_z, up_z, enter, leave, enter_z, leave_z, mode_x, back_x, spectrum, near, near_middle = held[2:]

    for n in (4, 6):
        loads[n].wait()
    rows = 16 * subs
    spread_modes = dot_left(enter, dot_right(partial[...].reshape(19 * 24, GZ), enter_z))
    group_of_lane = lax.broadcasted_iota(jnp.int32, (rows, GZ), 1) // 32
    packed = spread_modes[0:rows]
    for j in range(1, 4):
        packed = jnp.where(group_of_lane == j, spread_modes[j * rows : (j + 1) * rows], packed)
    modes_out[...] = packed.reshape(subs, 16, GZ)
    mode_copies = [
        send(modes_out.at[r], modes_in.at[subs - r], in_sent.at[r], in_got.at[subs - r], beside(0, r))
        for r in range(1, subs)
    ]

    edge[...] = partial[:, 13:21, :]

    low, high = pl.ds(0, 6), pl.ds(13, 6)
    near_rows = pl.ds(0, 8)
    sources = [
        partial.at[high], partial.at[low], edge, partial.at[:, near_rows, :],
        edge.at[high], partial.at[high, near_rows, :], edge.at[low], partial.at[low, near_rows, :],
    ]
    fine_copies = [
        send(source, fine_in[n], fine_sent.at[n], fine_got.at[n], beside(*SIDES[n])) for n, source in enumerate(sources)
    ]

    for n in (0, 2):
        loads[n].wait()
    middle[...] = dot_left(down, dot_right(partial[...].reshape(19 * 24, GZ), down_z)).reshape(13, 16, GZ)

    def pair_planes(values, count):
        return values[:count] + pltpu.roll(values[count:], 64, 2)

    high_x = pair_planes(middle[5:13], 4)
    low_x = pair_planes(middle[0:8], 4)
    rim_x[0] = high_x
    rim_x[1] = low_x
    rim_y[0, 0:7] = middle[0:7, 5:13, :]
    rim_y[0, 0:6] += pltpu.roll(middle[7:13, 5:13, :], 64, 2)
    rim_y[1, 0:7] = middle[0:7, 0:8, :]
    rim_y[1, 0:6] += pltpu.roll(middle[7:13, 0:8, :], 64, 2)
    rim_corner[0] = high_x[:, 5:13, :]
    rim_corner[1] = low_x[:, 5:13, :]
    sources = [
        rim_x.at[0], rim_x.at[1], rim_y.at[0], rim_y.at[1],
        rim_corner.at[0], rim_x.at[0, :, near_rows, :], rim_corner.at[1], rim_x.at[1, :, near_rows, :],
    ]
    middle_copies = [
        send(source, middle_in[n], middle_sent.at[n], middle_got.at[n], beside(*SIDES[n]))
        for n, source in enumerate(sources)
    ]

    for copy in mode_copies:
        copy.wait_recv()
    total = modes_out[0]
    for r in range(1, subs):
        total = total + modes_in[r]
    line_out[...] = total
    line_copies = [
        send(line_out, line_in.at[slabs - r], line_sent.at[r], line_got.at[slabs - r], beside(r, 0))
        for r in range(1, slabs)
    ]
    line_in[0] = total

    fine[...] = jnp.zeros_like(fine)
    fine[3:22, 3:27, :] = partial[...]
    for n, (dx, dy) in enumerate(SIDES):
        fine_copies[n].wait_recv()
        first = {1: 0, -1: 19, 0: 3}
        size = fine_in[n].shape
        x, y = first[dx], first[dy]
        fine[x : x + size[0], y : y + size[1], :] += fine_in[n][...]

    fold_columns(fine, columns, 19, 24)
    loads[11].wait()
    fine_short = short_range(columns, near, 19, 24)

    for n in (8, 9, 10):
        loads[n].wait()
    for copy in line_copies:
        copy.wait_recv()
    in_modes = dot_left(mode_x, line_in[...].reshape(slabs * 16, GZ)) * spectrum[...]
    back_out[...] = dot_left(back_x, in_modes)
    back_copies = [
        send(back_out, back_in.at[subs - r], back_sent.at[r], back_got.at[subs - r], beside(0, r))
        for r in range(1, subs)
    ]
    back_in[0] = back_out[...]

    middle_wide[...] = jnp.zeros_like(middle_wide)
    middle_wide[3:16, 3:19, :] = middle[...]
    for n, (dx, dy) in enumerate(SIDES):
        middle_copies[n].wait_recv()
        first = {1: 0, -1: 11, 0: 3}
        size = middle_in[n].shape
        x, y, span = first[dx], first[dy], size[0] if dx else 6
        middle_wide[x : x + size[0], y : y + size[1], :] += middle_in[n][...]
        x = x + size[0]
        middle_wide[x : x + span, y : y + size[1], :] += pltpu.roll(middle_in[n][0:span], 64, 2)
    fold_columns(middle_wide, middle_columns, 13, 16)
    loads[12].wait()
    middle_short = short_range(middle_columns, near_middle, 13, 16)

    for n in (1, 3):
        loads[n].wait()
    grid = fine_short + dot_right(dot_left(up, middle_short), up_z)
    for n in (5, 7):
        loads[n].wait()
    for copy in back_copies:
        copy.wait_recv()
    wide = dot_right(back_in[...].reshape(rows, GZ), leave_z)
    grid = grid + dot_left(leave, jnp.concatenate([wide[:, j * GZ : (j + 1) * GZ] for j in range(4)], axis=0))
    for copy in fine_copies:
        copy.wait_send()
    lattice = partial
    lattice[...] = grid.reshape(19, 24, GZ)
    grid_out[...] = lattice[1:17, 1:17, :]

    scalars.wait()
    forms = (((1,), (1,)), ((), ()))
    for a in range(4):
        for b in range(4):
            rows_of = [lattice[4 * a + i, 4 * b : 4 * b + 8, :] for i in range(7)] + [jnp.zeros((8, 128), jnp.float32)]
            high, low = halves(jnp.concatenate(rows_of, axis=0))
            column = lax.dot_general(place_back[...], high, forms, preferred_element_type=jnp.float32)
            column = column + lax.dot_general(place_back[...], low, forms, preferred_element_type=jnp.float32)
            first = (a * 4 + b) * 32
            pair = jnp.concatenate(halves(column.reshape(32, 8, 64)), axis=1)
            table[first : first + 32] = jnp.concatenate([pair, pair], axis=2)
    table[512] = jnp.zeros((16, 128), jnp.bfloat16)

    def interpolate(group, carry):
        for n in range(SENDERS):
            step = group * SENDERS + n
            sender = lax.rem(me + devices - lax.rem(step * STRIDE, devices), devices)
            for j in range(0, 4, 2):
                slot = step * 4 + j
                first, second = (table[cell_scalars[step, j + m]] for m in range(2))
                none = jnp.zeros_like(first)
                product = dot(
                    jnp.concatenate(
                        [jnp.concatenate([first, none], axis=1), jnp.concatenate([none, second], axis=1)], axis=0
                    ),
                    across[pl.ds(slot, 2)].reshape(256, BLOCK),
                )
                for m in range(2):
                    part = (product[16 * m : 16 * m + 8] + product[16 * m + 8 : 16 * m + 16]) * along[slot + m]
                    potentials[pl.ds(sender * 4 + j + m, 1), :] = jnp.sum(part, axis=0, keepdims=True)
        return carry

    lax.fori_loop(0, groups, interpolate, 0)
    pltpu.make_async_copy(outgoing.at[others], outgoing.at[others], sent).wait()
    pltpu.make_async_copy(cells_out.at[others], cells_out.at[others], cell_sent).wait()
    for copy in middle_copies + mode_copies + line_copies + back_copies:
        copy.wait_send()


def whole(chosen, counts, cells, atoms, slabs, subs):
    tables = [jnp.asarray(table) for table in level_tables(slabs, subs)]
    devices = slabs * subs
    held = [
        pltpu.VMEM(table.shape[1:] if n in PER_SUB else table.shape, table.dtype) for n, table in enumerate(tables)
    ]
    f32 = lambda *shape: pltpu.VMEM(shape, jnp.float32)
    i32 = lambda *shape: pltpu.VMEM(shape, jnp.int32)
    fine_in = [(6, 24), (6, 24), (19, 8), (19, 8)] + [(6, 8)] * 4
    middle_in = [(4, 16), (4, 16), (7, 8), (7, 8)] + [(4, 8)] * 4
    dma = lambda count: pltpu.SemaphoreType.DMA((count,))
    return pl.pallas_call(
        functools.partial(whole_kernel, slabs, subs),
        out_shape=(
            jax.ShapeDtypeStruct((devices * 4, BLOCK), jnp.float32),
            jax.ShapeDtypeStruct((GX, GY, GZ), jnp.float32),
        ),
        in_specs=[SMEM, SMEM, SMEM] + [ANY] * (1 + len(tables)),
        out_specs=(VMEM, VMEM),
        scratch_shapes=held
        + [
            f32(*atoms.shape),
            f32(devices, 16, BLOCK),
            f32(devices, 16, BLOCK),
            i32(devices, 1, BLOCK),
            i32(devices, 1, BLOCK),
            i32(devices, BLOCK),
            pltpu.SMEM((devices, BLOCK), jnp.int32),
            pltpu.VMEM((devices * 4, 128, BLOCK), jnp.bfloat16),
            f32(devices * 4, 8, BLOCK),
            f32(devices * 4 * 8, 128),
            f32(8, 512, 128),
            f32(19, 24, GZ),
            pltpu.VMEM((513, 16, 128), jnp.bfloat16),
        ]
        + [f32(*shape, GZ) for shape in fine_in + middle_in]
        + [
            f32(19, 8, GZ),
            f32(13, 16, GZ),
            f32(25, 32, GZ),
            f32(19, 24, GZ),
            f32(4, 25, 24, GZ),
            f32(4, 19, 16, GZ),
            f32(2, 4, 16, GZ),
            f32(2, 7, 8, GZ),
            f32(2, 4, 8, GZ),
            f32(subs, 16, GZ),
            f32(subs, 16, GZ),
            f32(16, GZ),
            f32(slabs, 16, GZ),
            f32(16, GZ),
            f32(subs, 16, GZ),
        ]
        + [pltpu.SemaphoreType.REGULAR, dma(len(tables)), pltpu.SemaphoreType.DMA, pltpu.SemaphoreType.DMA, dma(devices)]
        + [pltpu.SemaphoreType.DMA] * 3
        + [dma(8), dma(8), dma(8), dma(8)]
        + [dma(subs), dma(subs), dma(slabs), dma(slabs), dma(subs), dma(subs)],
        compiler_params=pltpu.CompilerParams(collective_id=0, has_side_effects=True, vmem_limit_bytes=60 << 20),
        name="multilevel",
    )(chosen, counts, cells, atoms, *tables)


def finish_kernel(potentials, grid, potentials_out, grid_out, *rest):
    values, sems = rest[:2], rest[2]
    loads = [pltpu.make_async_copy(ref, values[n], sems.at[n]) for n, ref in enumerate((potentials, grid))]
    stores = [pltpu.make_async_copy(values[n], ref, sems.at[n]) for n, ref in enumerate((potentials_out, grid_out))]
    for load in loads:
        load.start()
    for load, store in zip(loads, stores):
        load.wait()
        store.start()
    for store in stores:
        store.wait()


def finish(potentials, grid):
    return pl.pallas_call(
        finish_kernel,
        out_shape=tuple(jax.ShapeDtypeStruct(value.shape, value.dtype) for value in (potentials, grid)),
        in_specs=[ANY, ANY],
        out_specs=(ANY, ANY),
        scratch_shapes=[pltpu.VMEM(value.shape, value.dtype) for value in (potentials, grid)]
        + [pltpu.SemaphoreType.DMA((2,))],
        compiler_params=pltpu.CompilerParams(vmem_limit_bytes=60 << 20),
        name="finish",
    )(potentials, grid)


def body(atom_data, block_cell, send_list, send_count):
    slabs, subs = lax.axis_size("slab"), lax.axis_size("sub")
    return finish(*whole(send_list[0].T, send_count, block_cell, atom_data, slabs, subs))


def solution(mesh):
    placed = (
        P(("slab", "sub"), None, None),
        P(("slab", "sub")),
        P(("slab", "sub"), None, None),
        P(("slab", "sub"), None),
    )
    return jax.shard_map(
        body,
        mesh=mesh,
        in_specs=placed,
        out_specs=(P(("slab", "sub"), None), P("slab", "sub", None)),
        check_vma=False,
    )
```

```python
import functools
import ml_dtypes
import numpy as np
import jax
import jax.numpy as jnp
from jax import lax
from jax.experimental import pallas as pl
from jax.experimental.pallas import tpu as pltpu
from jax.sharding import PartitionSpec as P

BLOCK = 128
SENDERS = 16
ISSUE = 8
STRIDE = 77

GX = 16
GY = 16
GZ = 128
SMEM = pl.BlockSpec(memory_space=pltpu.SMEM)
VMEM = pl.BlockSpec(memory_space=pltpu.VMEM)
ANY = pl.BlockSpec(memory_space=pl.ANY)
MESH = pl.DeviceIdType.MESH


def spline_rows(row, offsets):
    left = jnp.maximum(1.0 - jnp.abs(row - offsets), -1.0)
    inner = left > 0.0
    return left * (0.5 + left * (jnp.where(inner, 2.0, 1.0) + left * jnp.where(inner, -1.5, 0.5)))


def halves(values):
    high = values.astype(jnp.bfloat16)
    low = (values - high.astype(jnp.float32)).astype(jnp.bfloat16)
    return high, low


def cross(first, second):
    rows = [first[i : i + 1, :] * second for i in range(7)]
    return jnp.concatenate(rows + [jnp.zeros_like(second)], axis=0)


def placement_tables():
    table = np.zeros((32, 8, GZ))
    for c in range(32):
        for k in range(7):
            table[c, k, (4 * c + k - 1) % GZ] = 1.0
    exact = table.astype(ml_dtypes.bfloat16)
    return exact.transpose(1, 0, 2).reshape(256, GZ).T, exact.reshape(256, GZ)


def two_parts(table):
    high = table.astype(ml_dtypes.bfloat16)
    low = (table - high.astype(np.float64)).astype(ml_dtypes.bfloat16)
    return np.stack([high, low])


def stencil(offset):
    size = np.abs(offset)
    return np.where(size == 0, 1.0, np.where(size == 1, 0.5625, np.where(size == 3, -0.0625, 0.0)))


def wrapped(offset, length):
    return (offset + length // 2) % length - length // 2


def halve(coarse, fine, coarse_first, fine_first, coarse_rows, fine_rows):
    table = np.zeros((coarse_rows, fine_rows))
    k = coarse_first + np.arange(coarse)[:, None]
    table[:coarse, :fine] = stencil(fine_first + np.arange(fine)[None, :] - 2 * k)
    return table


def halve_ring(coarse):
    return stencil(wrapped(np.arange(2 * coarse)[None, :] - 2 * np.arange(coarse)[:, None], 2 * coarse))


def soften(scaled):
    square = scaled * scaled
    return np.where(scaled < 1.0, (15.0 - 10.0 * square + 3.0 * square * square) / 8.0, 1.0 / np.maximum(scaled, 1.0))


def split_kernel(distance):
    return soften(distance / 2.0) / 2.0 - soften(distance / 4.0) / 4.0


def modes(length):
    angle = 2.0 * np.pi / length * (np.arange(length)[:, None] * np.arange(length)[None, :] % length)
    return (np.cos(angle) + np.sin(angle)) / np.sqrt(length)


RINGS = [(a, b) for a in range(4) for b in range(a, 4)]


def ring_tables(length, scale):
    shift = wrapped(np.arange(length)[:, None] - np.arange(length)[None, :], length)
    out = np.zeros((len(RINGS), GZ, GZ))
    for n, (a, b) in enumerate(RINGS):
        values = scale * split_kernel(np.sqrt(a * a + b * b + shift * shift))
        out[n, :length, :length] = np.where(np.abs(shift) <= 3, values, 0.0)
    return out.reshape(len(RINGS) * GZ, GZ)


def level_tables(slabs, subs):
    exact = lambda table: table.astype(ml_dtypes.bfloat16)
    down = np.kron(halve(13, 19, -2, -1, 13, 19), halve(13, 19, -2, -1, 16, 24))
    down_z = np.zeros((GZ, GZ))
    down_z[:, :64] = halve_ring(64).T
    top_x = halve(9, 13, -2, -2, 16, 13) @ halve(13, 19, -2, -1, 13, 19)
    top_y = halve(9, 13, -2, -2, 9, 16) @ halve(13, 19, -2, -1, 16, 24)
    top_z = halve_ring(32) @ halve_ring(64)
    wave_x, wave_y, wave_z = modes(4 * slabs), modes(4 * subs), modes(32)
    reach = np.arange(9) - 2
    enter = []
    for sub in range(subs):
        rows = 4 * ((sub + np.arange(subs)[None, :]) % subs) + np.arange(4)[:, None]
        along = wave_y[rows][:, :, (4 * sub + reach) % (4 * subs)] @ top_y
        enter.append(np.einsum("jrm,xn->jrxnm", along, top_x).reshape(4 * subs * 16, 19 * 24))
    enter = np.stack(enter)
    enter_z = np.tile((wave_z @ top_z).T, (1, 4))
    leave_z = np.kron(np.eye(4), wave_z @ top_z)
    mode_x = np.zeros((4 * slabs, slabs, 16))
    for r in range(slabs):
        mode_x[:, r, :9] = wave_x[:, (4 * r + reach) % (4 * slabs)]
    back_x = np.zeros((16, 4 * slabs))
    back_x[:9] = wave_x[:, reach % (4 * slabs)].T
    squared = 0.0
    for dimension, length in enumerate((4 * slabs, 4 * subs, 32)):
        shape = [1, 1, 1]
        shape[dimension] = length
        squared = squared + (wrapped(np.arange(length), length) ** 2).reshape(shape)
    spectrum = np.fft.fftn(soften(np.sqrt(squared) / 2.0) / 8.0).real
    spectrum = spectrum.reshape(4 * slabs, subs, 128).transpose(1, 0, 2).astype(np.float32)
    return placement_tables() + (
        exact(down),
        exact(down.T),
        exact(down_z),
        exact(down_z.T),
        two_parts(enter).transpose(1, 0, 2, 3),
        two_parts(enter.transpose(0, 2, 1)).transpose(1, 0, 2, 3),
        two_parts(enter_z),
        two_parts(leave_z),
        two_parts(mode_x.reshape(4 * slabs, slabs * 16)),
        two_parts(back_x),
        spectrum,
        two_parts(ring_tables(GZ, 1.0)),
        two_parts(ring_tables(GZ // 2, 0.5)),
    )


PER_SUB = (6, 7, 12)


def dot(a, b):
    return jnp.dot(a, b, preferred_element_type=jnp.float32)


def dot_right(values, table):
    high, low = halves(values)
    if len(table.shape) == 2:
        return dot(high, table[...]) + dot(low, table[...])
    return dot(high, table[0]) + dot(low, table[0]) + dot(high, table[1])


def dot_left(table, values):
    high, low = halves(values)
    count = values.shape[1]
    both = jnp.concatenate([high, low], axis=1)
    if len(table.shape) == 2:
        sums = dot(table[...], both)
        return sums[:, :count] + sums[:, count:]
    sums = dot(table[0], both)
    return sums[:, :count] + sums[:, count:] + dot(table[1], high)


def fold_columns(lattice, columns, planes, rows):
    columns[0] = lattice[:, 3 : 3 + rows, :]
    for b in range(1, 4):
        columns[b] = lattice[:, 3 - b : 3 - b + rows, :] + lattice[:, 3 + b : 3 + b + rows, :]


def short_range(columns, table, planes, rows):
    def sides(a, b):
        if a == 0:
            return columns[b, 3 : 3 + planes]
        return columns[b, 3 - a : 3 - a + planes] + columns[b, 3 + a : 3 + a + planes]

    total = None
    for n in range(0, len(RINGS), 2):
        parts = []
        for a, b in RINGS[n : n + 2]:
            part = sides(a, b) if a == b else sides(a, b) + sides(b, a)
            parts.append(halves(part.reshape(planes * rows, GZ)))
        high, low = (jnp.concatenate([part[m] for part in parts], axis=1) for m in range(2))
        span = pl.ds(n * GZ, 2 * GZ)
        here = dot(high, table[0, span, :]) + dot(low, table[0, span, :]) + dot(high, table[1, span, :])
        total = here if total is None else total + here
    return total


SIDES = [(1, 0), (-1, 0), (0, 1), (0, -1), (1, 1), (1, -1), (-1, 1), (-1, -1)]


def whole_kernel(slabs, subs, chosen, counts, cells, atoms, *refs):
    tables = refs[:15]
    potentials_out, grid_out = refs[15:17]
    rest = list(refs[17:])
    take = lambda count: [rest.pop(0) for _ in range(count)]
    held = take(15)
    atoms_held, outgoing, incoming, cells_out, cells_in, cell_block, cell_scalars = take(7)
    across, along, patches, cell_sums, partial, table, potentials, grid_part = take(8)
    fine_in, middle_in = take(8), take(8)
    edge, middle, fine, middle_wide, columns, middle_columns, rim_x, rim_y, rim_corner = take(9)
    modes_out, modes_in, line_out, line_in, back_out, back_in = take(6)
    out_sem, ready, load_sem, atoms_sem, sent, got, cell_sent, cell_got, scalar_sem = take(9)
    fine_sent, fine_got, middle_sent, middle_got, in_sent, in_got, line_sent, line_got, back_sent, back_got = rest
    devices = slabs * subs
    slab = lax.axis_index("slab")
    sub = lax.axis_index("sub")
    me = slab * subs + sub

    def beside(dx, dy):
        return (lax.rem(slab + dx + slabs, slabs), lax.rem(sub + dy + subs, subs))

    def send(source, target_ref, sent, got, target):
        copy = pltpu.make_async_remote_copy(source, target_ref, sent, got, device_id=target, device_id_type=MESH)
        copy.start()
        return copy

    atoms_load = pltpu.make_async_copy(atoms, atoms_held, atoms_sem)
    atoms_load.start()
    barrier = pltpu.get_barrier_semaphore()

    def peer_of(step):
        peer = lax.rem(me + step * STRIDE, devices)
        return peer, (peer // subs, lax.rem(peer, subs))

    def in_groups(act):
        def several(group, carry):
            for n in range(ISSUE):
                act(group * ISSUE + n)
            return carry

        for step in range(1, ISSUE):
            act(step)
        lax.fori_loop(1, devices // ISSUE, several, 0)

    lines = [beside(r, 0) for r in range(1, slabs)] + [beside(0, r) for r in range(1, subs)]
    for target in lines:
        pl.semaphore_signal(barrier, inc=1, device_id=target, device_id_type=MESH)
    loads = [
        pltpu.make_async_copy(table_ref.at[sub] if n in PER_SUB else table_ref, held[n], load_sem.at[n])
        for n, table_ref in enumerate(tables)
    ]
    for load in loads:
        load.start()
    place_in, place_back = held[:2]
    loads_of_levels = loads[2:]

    atoms_load.wait()
    lane = lax.broadcasted_iota(jnp.int32, (1, BLOCK), 1)

    def pick(row, carry):
        for n in range(subs):
            peer = row * subs + n
            line = jnp.full((1, BLOCK), 512, jnp.int32)
            for j in range(4):
                index = chosen[j, peer]
                outgoing[peer, pl.ds(4 * j, 4), :] = atoms_held[index]
                cell = cells[index]
                local = ((cell >> 10) & 3) * 128 + ((cell >> 5) & 3) * 32 + (cell & 31)
                line = jnp.where(lane == j, jnp.where(counts[0, peer] > j, local, 512), line)
            cells_out[peer] = line
        return carry

    pl.semaphore_wait(barrier, len(lines))
    for r in range(1, subs):
        pl.semaphore_signal(ready, inc=1, device_id=beside(0, r), device_id_type=MESH)
    lax.fori_loop(0, slabs, pick, 0)
    pl.semaphore_wait(ready, subs - 1)

    def start(step):
        peer, target = peer_of(step)
        send(outgoing.at[peer], incoming.at[step], sent, got.at[step], target)
        send(cells_out.at[peer], cells_in.at[step], cell_sent, cell_got, target)

    in_groups(start)
    own = pltpu.make_async_copy(outgoing.at[me], incoming.at[0], got.at[0])
    own.start()
    cells_in[0] = cells_out[me]

    offsets = lax.broadcasted_iota(jnp.int32, (8, BLOCK), 0).astype(jnp.float32) - 1.0

    def spread(group, carry):
        for n in range(SENDERS):
            step = group * SENDERS + n
            pltpu.make_async_copy(incoming.at[step], incoming.at[step], got.at[step]).wait()
        parts = []
        for n in range(SENDERS):
            step = group * SENDERS + n
            for j in range(4):
                wx, wy, wz = (spline_rows(incoming[step, pl.ds(4 * j + d, 1), :], offsets) for d in range(3))
                charge = incoming[step, pl.ds(4 * j + 3, 1), :]
                high, low = halves(cross(wx, wy))
                slot = step * 4 + j
                across[slot, 0:64, :] = high
                across[slot, 64:128, :] = low
                along[slot] = wz
                both = jnp.concatenate(halves(wz * charge), axis=0)
                product = lax.dot_general(
                    jnp.concatenate([both, both], axis=1),
                    jnp.concatenate([high, low], axis=1),
                    (((1,), (1,)), ((), ())),
                    preferred_element_type=jnp.float32,
                )
                parts.append((step, j, product[0:8] + product[8:16]))
        for step, j, part in parts:
            patches[pl.ds(pl.multiple_of((j * devices + step) * 8, 8), 8), 0:64] = part
        return carry

    groups = devices // SENDERS
    lax.fori_loop(0, groups, spread, 0)
    others = pl.ds(1, devices - 1)
    pltpu.make_async_copy(cells_in.at[others], cells_in.at[others], cell_got).wait()
    cell_block[...] = cells_in[:, 0, :]
    scalars = pltpu.make_async_copy(cell_block, cell_scalars, scalar_sem)
    scalars.start()

    slots_across = cell_block[...].T
    cell_number = lax.broadcasted_iota(jnp.int32, (512, devices), 0)
    member = jnp.concatenate(
        [(cell_number == slots_across[j : j + 1, :]).astype(jnp.float32).astype(jnp.bfloat16) for j in range(4)], axis=1
    )
    for k in range(8):
        sums = dot(member, jnp.concatenate(halves(patches[pl.ds(k, devices * 4, stride=8), :]), axis=1))
        cell_sums[k] = sums[:, :128] + sums[:, 128:]
    partial[...] = jnp.zeros_like(partial)
    loads[0].wait()
    loads[1].wait()
    for a in range(4):
        for b in range(4):
            first = (a * 4 + b) * 32
            column = cell_sums[:, first : first + 32, :].reshape(256, 128)
            planes = dot_left(place_in, column).T
            for i in range(7):
                partial[4 * a + i, 4 * b : 4 * b + 8, :] += planes[8 * i : 8 * i + 8]

    loads = loads_of_levels
    down, up, down_z, up_z, enter, leave, enter_z, leave_z, mode_x, back_x, spectrum, near, near_middle = held[2:]

    for n in (4, 6):
        loads[n].wait()
    rows = 16 * subs
    spread_modes = dot_left(enter, dot_right(partial[...].reshape(19 * 24, GZ), enter_z))
    group_of_lane = lax.broadcasted_iota(jnp.int32, (rows, GZ), 1) // 32
    packed = spread_modes[0:rows]
    for j in range(1, 4):
        packed = jnp.where(group_of_lane == j, spread_modes[j * rows : (j + 1) * rows], packed)
    modes_out[...] = packed.reshape(subs, 16, GZ)
    mode_copies = [
        send(modes_out.at[r], modes_in.at[subs - r], in_sent.at[r], in_got.at[subs - r], beside(0, r))
        for r in range(1, subs)
    ]

    edge[...] = partial[:, 13:21, :]

    low, high = pl.ds(0, 6), pl.ds(13, 6)
    near_rows = pl.ds(0, 8)
    sources = [
        partial.at[high], partial.at[low], edge, partial.at[:, near_rows, :],
        edge.at[high], partial.at[high, near_rows, :], edge.at[low], partial.at[low, near_rows, :],
    ]
    fine_copies = [
        send(source, fine_in[n], fine_sent.at[n], fine_got.at[n], beside(*SIDES[n])) for n, source in enumerate(sources)
    ]

    for n in (0, 2):
        loads[n].wait()
    middle[...] = dot_left(down, dot_right(partial[...].reshape(19 * 24, GZ), down_z)).reshape(13, 16, GZ)

    def pair_planes(values, count):
        return values[:count] + pltpu.roll(values[count:], 64, 2)

    high_x = pair_planes(middle[5:13], 4)
    low_x = pair_planes(middle[0:8], 4)
    rim_x[0] = high_x
    rim_x[1] = low_x
    rim_y[0, 0:7] = middle[0:7, 5:13, :]
    rim_y[0, 0:6] += pltpu.roll(middle[7:13, 5:13, :], 64, 2)
    rim_y[1, 0:7] = middle[0:7, 0:8, :]
    rim_y[1, 0:6] += pltpu.roll(middle[7:13, 0:8, :], 64, 2)
    rim_corner[0] = high_x[:, 5:13, :]
    rim_corner[1] = low_x[:, 5:13, :]
    sources = [
        rim_x.at[0], rim_x.at[1], rim_y.at[0], rim_y.at[1],
        rim_corner.at[0], rim_x.at[0, :, near_rows, :], rim_corner.at[1], rim_x.at[1, :, near_rows, :],
    ]
    middle_copies = [
        send(source, middle_in[n], middle_sent.at[n], middle_got.at[n], beside(*SIDES[n]))
        for n, source in enumerate(sources)
    ]

    for copy in mode_copies:
        copy.wait_recv()
    total = modes_out[0]
    for r in range(1, subs):
        total = total + modes_in[r]
    line_out[...] = total
    line_copies = [
        send(line_out, line_in.at[slabs - r], line_sent.at[r], line_got.at[slabs - r], beside(r, 0))
        for r in range(1, slabs)
    ]
    line_in[0] = total

    fine[...] = jnp.zeros_like(fine)
    fine[3:22, 3:27, :] = partial[...]
    for n, (dx, dy) in enumerate(SIDES):
        fine_copies[n].wait_recv()
        first = {1: 0, -1: 19, 0: 3}
        size = fine_in[n].shape
        x, y = first[dx], first[dy]
        fine[x : x + size[0], y : y + size[1], :] += fine_in[n][...]

    fold_columns(fine, columns, 19, 24)
    loads[11].wait()
    fine_short = short_range(columns, near, 19, 24)

    for n in (8, 9, 10):
        loads[n].wait()
    for copy in line_copies:
        copy.wait_recv()
    in_modes = dot_left(mode_x, line_in[...].reshape(slabs * 16, GZ)) * spectrum[...]
    back_out[...] = dot_left(back_x, in_modes)
    back_copies = [
        send(back_out, back_in.at[subs - r], back_sent.at[r], back_got.at[subs - r], beside(0, r))
        for r in range(1, subs)
    ]
    back_in[0] = back_out[...]

    middle_wide[...] = jnp.zeros_like(middle_wide)
    middle_wide[3:16, 3:19, :] = middle[...]
    for n, (dx, dy) in enumerate(SIDES):
        middle_copies[n].wait_recv()
        first = {1: 0, -1: 11, 0: 3}
        size = middle_in[n].shape
        x, y, span = first[dx], first[dy], size[0] if dx else 6
        middle_wide[x : x + size[0], y : y + size[1], :] += middle_in[n][...]
        x = x + size[0]
        middle_wide[x : x + span, y : y + size[1], :] += pltpu.roll(middle_in[n][0:span], 64, 2)
    fold_columns(middle_wide, middle_columns, 13, 16)
    loads[12].wait()
    middle_short = short_range(middle_columns, near_middle, 13, 16)

    for n in (1, 3):
        loads[n].wait()
    grid = fine_short + dot_right(dot_left(up, middle_short), up_z)
    for n in (5, 7):
        loads[n].wait()
    for copy in back_copies:
        copy.wait_recv()
    wide = dot_right(back_in[...].reshape(rows, GZ), leave_z)
    grid = grid + dot_left(leave, jnp.concatenate([wide[:, j * GZ : (j + 1) * GZ] for j in range(4)], axis=0))
    for copy in fine_copies:
        copy.wait_send()
    lattice = partial
    lattice[...] = grid.reshape(19, 24, GZ)
    grid_part[...] = lattice[1:17, 1:17, :]
    grid_copy = pltpu.make_async_copy(grid_part, grid_out, out_sem.at[0])
    grid_copy.start()

    scalars.wait()
    forms = (((1,), (1,)), ((), ()))
    for a in range(4):
        for b in range(4):
            rows_of = [lattice[4 * a + i, 4 * b : 4 * b + 8, :] for i in range(7)] + [jnp.zeros((8, 128), jnp.float32)]
            high, low = halves(jnp.concatenate(rows_of, axis=0))
            column = lax.dot_general(place_back[...], high, forms, preferred_element_type=jnp.float32)
            column = column + lax.dot_general(place_back[...], low, forms, preferred_element_type=jnp.float32)
            first = (a * 4 + b) * 32
            pair = jnp.concatenate(halves(column.reshape(32, 8, 64)), axis=1)
            table[first : first + 32] = jnp.concatenate([pair, pair], axis=2)
    table[512] = jnp.zeros((16, 128), jnp.bfloat16)

    def interpolate(group, carry):
        for n in range(SENDERS):
            step = group * SENDERS + n
            sender = lax.rem(me + devices - lax.rem(step * STRIDE, devices), devices)
            for j in range(0, 4, 2):
                slot = step * 4 + j
                first, second = (table[cell_scalars[step, j + m]] for m in range(2))
                none = jnp.zeros_like(first)
                product = dot(
                    jnp.concatenate(
                        [jnp.concatenate([first, none], axis=1), jnp.concatenate([none, second], axis=1)], axis=0
                    ),
                    across[pl.ds(slot, 2)].reshape(256, BLOCK),
                )
                for m in range(2):
                    part = (product[16 * m : 16 * m + 8] + product[16 * m + 8 : 16 * m + 16]) * along[slot + m]
                    potentials[pl.ds(sender * 4 + j + m, 1), :] = jnp.sum(part, axis=0, keepdims=True)
        return carry

    lax.fori_loop(0, groups, interpolate, 0)
    potentials_copy = pltpu.make_async_copy(potentials, potentials_out, out_sem.at[1])
    potentials_copy.start()
    pltpu.make_async_copy(outgoing.at[others], outgoing.at[others], sent).wait()
    pltpu.make_async_copy(cells_out.at[others], cells_out.at[others], cell_sent).wait()
    for copy in middle_copies + mode_copies + line_copies + back_copies:
        copy.wait_send()
    grid_copy.wait()
    potentials_copy.wait()


def whole(chosen, counts, cells, atoms, slabs, subs):
    tables = [jnp.asarray(table) for table in level_tables(slabs, subs)]
    devices = slabs * subs
    held = [
        pltpu.VMEM(table.shape[1:] if n in PER_SUB else table.shape, table.dtype) for n, table in enumerate(tables)
    ]
    f32 = lambda *shape: pltpu.VMEM(shape, jnp.float32)
    i32 = lambda *shape: pltpu.VMEM(shape, jnp.int32)
    fine_in = [(6, 24), (6, 24), (19, 8), (19, 8)] + [(6, 8)] * 4
    middle_in = [(4, 16), (4, 16), (7, 8), (7, 8)] + [(4, 8)] * 4
    dma = lambda count: pltpu.SemaphoreType.DMA((count,))
    return pl.pallas_call(
        functools.partial(whole_kernel, slabs, subs),
        out_shape=(
            jax.ShapeDtypeStruct((devices * 4, BLOCK), jnp.float32),
            jax.ShapeDtypeStruct((GX, GY, GZ), jnp.float32),
        ),
        in_specs=[SMEM, SMEM, SMEM] + [ANY] * (1 + len(tables)),
        out_specs=(ANY, ANY),
        scratch_shapes=held
        + [
            f32(*atoms.shape),
            f32(devices, 16, BLOCK),
            f32(devices, 16, BLOCK),
            i32(devices, 1, BLOCK),
            i32(devices, 1, BLOCK),
            i32(devices, BLOCK),
            pltpu.SMEM((devices, BLOCK), jnp.int32),
            pltpu.VMEM((devices * 4, 128, BLOCK), jnp.bfloat16),
            f32(devices * 4, 8, BLOCK),
            f32(devices * 4 * 8, 128),
            f32(8, 512, 128),
            f32(19, 24, GZ),
            pltpu.VMEM((513, 16, 128), jnp.bfloat16),
            f32(devices * 4, BLOCK),
            f32(GX, GY, GZ),
        ]
        + [f32(*shape, GZ) for shape in fine_in + middle_in]
        + [
            f32(19, 8, GZ),
            f32(13, 16, GZ),
            f32(25, 32, GZ),
            f32(19, 24, GZ),
            f32(4, 25, 24, GZ),
            f32(4, 19, 16, GZ),
            f32(2, 4, 16, GZ),
            f32(2, 7, 8, GZ),
            f32(2, 4, 8, GZ),
            f32(subs, 16, GZ),
            f32(subs, 16, GZ),
            f32(16, GZ),
            f32(slabs, 16, GZ),
            f32(16, GZ),
            f32(subs, 16, GZ),
        ]
        + [dma(2), pltpu.SemaphoreType.REGULAR, dma(len(tables)), pltpu.SemaphoreType.DMA, pltpu.SemaphoreType.DMA, dma(devices)]
        + [pltpu.SemaphoreType.DMA] * 3
        + [dma(8), dma(8), dma(8), dma(8)]
        + [dma(subs), dma(subs), dma(slabs), dma(slabs), dma(subs), dma(subs)],
        compiler_params=pltpu.CompilerParams(collective_id=0, has_side_effects=True, vmem_limit_bytes=60 << 20),
        name="multilevel",
    )(chosen, counts, cells, atoms, *tables)


def finish_kernel(potentials, grid, potentials_out, grid_out, *rest):
    values, sems = rest[:2], rest[2]
    loads = [pltpu.make_async_copy(ref, values[n], sems.at[n]) for n, ref in enumerate((potentials, grid))]
    stores = [pltpu.make_async_copy(values[n], ref, sems.at[n]) for n, ref in enumerate((potentials_out, grid_out))]
    for load in loads:
        load.start()
    for load, store in zip(loads, stores):
        load.wait()
        store.start()
    for store in stores:
        store.wait()


def finish(potentials, grid):
    return pl.pallas_call(
        finish_kernel,
        out_shape=tuple(jax.ShapeDtypeStruct(value.shape, value.dtype) for value in (potentials, grid)),
        in_specs=[ANY, ANY],
        out_specs=(ANY, ANY),
        scratch_shapes=[pltpu.VMEM(value.shape, value.dtype) for value in (potentials, grid)]
        + [pltpu.SemaphoreType.DMA((2,))],
        compiler_params=pltpu.CompilerParams(vmem_limit_bytes=60 << 20),
        name="finish",
    )(potentials, grid)


def body(atom_data, block_cell, send_list, send_count):
    slabs, subs = lax.axis_size("slab"), lax.axis_size("sub")
    return finish(*whole(send_list[0].T, send_count, block_cell, atom_data, slabs, subs))


def solution(mesh):
    placed = (
        P(("slab", "sub"), None, None),
        P(("slab", "sub")),
        P(("slab", "sub"), None, None),
        P(("slab", "sub"), None),
    )
    return jax.shard_map(
        body,
        mesh=mesh,
        in_specs=placed,
        out_specs=(P(("slab", "sub"), None), P("slab", "sub", None)),
        check_vma=False,
    )
```

```python
import functools
import ml_dtypes
import numpy as np
import jax
import jax.numpy as jnp
from jax import lax
from jax.experimental import pallas as pl
from jax.experimental.pallas import tpu as pltpu
from jax.sharding import PartitionSpec as P

BLOCK = 128
SENDERS = 16
ISSUE = 8
STRIDE = 77

GX = 16
GY = 16
GZ = 128
SMEM = pl.BlockSpec(memory_space=pltpu.SMEM)
VMEM = pl.BlockSpec(memory_space=pltpu.VMEM)
ANY = pl.BlockSpec(memory_space=pl.ANY)
MESH = pl.DeviceIdType.MESH


def spline_rows(row, offsets):
    left = jnp.maximum(1.0 - jnp.abs(row - offsets), -1.0)
    inner = left > 0.0
    return left * (0.5 + left * (jnp.where(inner, 2.0, 1.0) + left * jnp.where(inner, -1.5, 0.5)))


def halves(values):
    high = values.astype(jnp.bfloat16)
    low = (values - high.astype(jnp.float32)).astype(jnp.bfloat16)
    return high, low


def cross(first, second):
    rows = [first[i : i + 1, :] * second for i in range(7)]
    return jnp.concatenate(rows + [jnp.zeros_like(second)], axis=0)


def placement_tables():
    table = np.zeros((32, 8, GZ))
    for c in range(32):
        for k in range(7):
            table[c, k, (4 * c + k - 1) % GZ] = 1.0
    exact = table.astype(ml_dtypes.bfloat16)
    return exact.transpose(1, 0, 2).reshape(256, GZ).T, exact.reshape(256, GZ)


def two_parts(table):
    high = table.astype(ml_dtypes.bfloat16)
    low = (table - high.astype(np.float64)).astype(ml_dtypes.bfloat16)
    return np.stack([high, low])


def stencil(offset):
    size = np.abs(offset)
    return np.where(size == 0, 1.0, np.where(size == 1, 0.5625, np.where(size == 3, -0.0625, 0.0)))


def wrapped(offset, length):
    return (offset + length // 2) % length - length // 2


def halve(coarse, fine, coarse_first, fine_first, coarse_rows, fine_rows):
    table = np.zeros((coarse_rows, fine_rows))
    k = coarse_first + np.arange(coarse)[:, None]
    table[:coarse, :fine] = stencil(fine_first + np.arange(fine)[None, :] - 2 * k)
    return table


def halve_ring(coarse):
    return stencil(wrapped(np.arange(2 * coarse)[None, :] - 2 * np.arange(coarse)[:, None], 2 * coarse))


def soften(scaled):
    square = scaled * scaled
    return np.where(scaled < 1.0, (15.0 - 10.0 * square + 3.0 * square * square) / 8.0, 1.0 / np.maximum(scaled, 1.0))


def split_kernel(distance):
    return soften(distance / 2.0) / 2.0 - soften(distance / 4.0) / 4.0


def modes(length):
    angle = 2.0 * np.pi / length * (np.arange(length)[:, None] * np.arange(length)[None, :] % length)
    return (np.cos(angle) + np.sin(angle)) / np.sqrt(length)


RINGS = [(a, b) for a in range(4) for b in range(a, 4)]


def ring_tables(length, scale):
    shift = wrapped(np.arange(length)[:, None] - np.arange(length)[None, :], length)
    out = np.zeros((len(RINGS), GZ, GZ))
    for n, (a, b) in enumerate(RINGS):
        values = scale * split_kernel(np.sqrt(a * a + b * b + shift * shift))
        out[n, :length, :length] = np.where(np.abs(shift) <= 3, values, 0.0)
    return out.reshape(len(RINGS) * GZ, GZ)


def level_tables(slabs, subs):
    exact = lambda table: table.astype(ml_dtypes.bfloat16)
    down = np.kron(halve(13, 19, -2, -1, 13, 19), halve(13, 19, -2, -1, 16, 24))
    down_z = np.zeros((GZ, GZ))
    down_z[:, :64] = halve_ring(64).T
    top_x = halve(9, 13, -2, -2, 16, 13) @ halve(13, 19, -2, -1, 13, 19)
    top_y = halve(9, 13, -2, -2, 9, 16) @ halve(13, 19, -2, -1, 16, 24)
    top_z = halve_ring(32) @ halve_ring(64)
    wave_x, wave_y, wave_z = modes(4 * slabs), modes(4 * subs), modes(32)
    reach = np.arange(9) - 2
    enter = []
    for sub in range(subs):
        rows = 4 * ((sub + np.arange(subs)[None, :]) % subs) + np.arange(4)[:, None]
        along = wave_y[rows][:, :, (4 * sub + reach) % (4 * subs)] @ top_y
        enter.append(np.einsum("jrm,xn->jrxnm", along, top_x).reshape(4 * subs * 16, 19 * 24))
    enter = np.stack(enter)
    enter_z = np.tile((wave_z @ top_z).T, (1, 4))
    leave_z = np.kron(np.eye(4), wave_z @ top_z)
    mode_x = np.zeros((4 * slabs, slabs, 16))
    for r in range(slabs):
        mode_x[:, r, :9] = wave_x[:, (4 * r + reach) % (4 * slabs)]
    back_x = np.zeros((16, 4 * slabs))
    back_x[:9] = wave_x[:, reach % (4 * slabs)].T
    squared = 0.0
    for dimension, length in enumerate((4 * slabs, 4 * subs, 32)):
        shape = [1, 1, 1]
        shape[dimension] = length
        squared = squared + (wrapped(np.arange(length), length) ** 2).reshape(shape)
    spectrum = np.fft.fftn(soften(np.sqrt(squared) / 2.0) / 8.0).real
    spectrum = spectrum.reshape(4 * slabs, subs, 128).transpose(1, 0, 2).astype(np.float32)
    return placement_tables() + (
        exact(down),
        exact(down.T),
        exact(down_z),
        exact(down_z.T),
        two_parts(enter).transpose(1, 0, 2, 3),
        two_parts(enter.transpose(0, 2, 1)).transpose(1, 0, 2, 3),
        two_parts(enter_z),
        two_parts(leave_z),
        two_parts(mode_x.reshape(4 * slabs, slabs * 16)),
        two_parts(back_x),
        spectrum,
        two_parts(ring_tables(GZ, 1.0)),
        two_parts(ring_tables(GZ // 2, 0.5)),
    )


PER_SUB = (6, 7, 12)


def dot(a, b):
    return jnp.dot(a, b, preferred_element_type=jnp.float32)


def dot_right(values, table):
    high, low = halves(values)
    if len(table.shape) == 2:
        return dot(high, table[...]) + dot(low, table[...])
    return dot(high, table[0]) + dot(low, table[0]) + dot(high, table[1])


def dot_left(table, values):
    high, low = halves(values)
    count = values.shape[1]
    both = jnp.concatenate([high, low], axis=1)
    if len(table.shape) == 2:
        sums = dot(table[...], both)
        return sums[:, :count] + sums[:, count:]
    sums = dot(table[0], both)
    return sums[:, :count] + sums[:, count:] + dot(table[1], high)


def fold_columns(lattice, columns, planes, rows):
    columns[0] = lattice[:, 3 : 3 + rows, :]
    for b in range(1, 4):
        columns[b] = lattice[:, 3 - b : 3 - b + rows, :] + lattice[:, 3 + b : 3 + b + rows, :]


def short_range(columns, table, planes, rows):
    def sides(a, b):
        if a == 0:
            return columns[b, 3 : 3 + planes]
        return columns[b, 3 - a : 3 - a + planes] + columns[b, 3 + a : 3 + a + planes]

    total = None
    for n in range(0, len(RINGS), 2):
        parts = []
        for a, b in RINGS[n : n + 2]:
            part = sides(a, b) if a == b else sides(a, b) + sides(b, a)
            parts.append(halves(part.reshape(planes * rows, GZ)))
        high, low = (jnp.concatenate([part[m] for part in parts], axis=1) for m in range(2))
        span = pl.ds(n * GZ, 2 * GZ)
        here = dot(high, table[0, span, :]) + dot(low, table[0, span, :]) + dot(high, table[1, span, :])
        total = here if total is None else total + here
    return total


SIDES = [(1, 0), (-1, 0), (0, 1), (0, -1), (1, 1), (1, -1), (-1, 1), (-1, -1)]


def whole_kernel(slabs, subs, chosen, counts, cells, atoms, *refs):
    tables = refs[:15]
    potentials_out, grid_out = refs[15:17]
    rest = list(refs[17:])
    take = lambda count: [rest.pop(0) for _ in range(count)]
    held = take(15)
    atoms_held, outgoing, incoming, cells_out, cells_in, cell_block, cell_scalars = take(7)
    across, along, patches, cell_sums, partial, table, potentials, grid_part = take(8)
    fine_in, middle_in = take(8), take(8)
    edge, middle, fine, middle_wide, columns, middle_columns, rim_x, rim_y, rim_corner = take(9)
    modes_out, modes_in, line_out, line_in, back_out, back_in = take(6)
    out_sem, ready, load_sem, atoms_sem, sent, got, cell_sent, cell_got, scalar_sem = take(9)
    fine_sent, fine_got, middle_sent, middle_got, in_sent, in_got, line_sent, line_got, back_sent, back_got = rest
    devices = slabs * subs
    slab = lax.axis_index("slab")
    sub = lax.axis_index("sub")
    me = slab * subs + sub

    def beside(dx, dy):
        return (lax.rem(slab + dx + slabs, slabs), lax.rem(sub + dy + subs, subs))

    def send(source, target_ref, sent, got, target):
        copy = pltpu.make_async_remote_copy(source, target_ref, sent, got, device_id=target, device_id_type=MESH)
        copy.start()
        return copy

    atoms_load = pltpu.make_async_copy(atoms, atoms_held, atoms_sem)
    atoms_load.start()
    barrier = pltpu.get_barrier_semaphore()

    def peer_of(step):
        peer = lax.rem(me + step * STRIDE, devices)
        return peer, (peer // subs, lax.rem(peer, subs))

    def in_groups(act):
        def several(group, carry):
            for n in range(ISSUE):
                act(group * ISSUE + n)
            return carry

        for step in range(1, ISSUE):
            act(step)
        lax.fori_loop(1, devices // ISSUE, several, 0)

    lines = [beside(r, 0) for r in range(1, slabs)] + [beside(0, r) for r in range(1, subs)]
    for target in lines:
        pl.semaphore_signal(barrier, inc=1, device_id=target, device_id_type=MESH)
    loads = [
        pltpu.make_async_copy(table_ref.at[sub] if n in PER_SUB else table_ref, held[n], load_sem.at[n])
        for n, table_ref in enumerate(tables)
    ]
    for load in loads:
        load.start()
    place_in, place_back = held[:2]
    loads_of_levels = loads[2:]

    atoms_load.wait()
    lane = lax.broadcasted_iota(jnp.int32, (1, BLOCK), 1)

    def pick(row, carry):
        for n in range(subs):
            peer = row * subs + n
            line = jnp.full((1, BLOCK), 512, jnp.int32)
            for j in range(4):
                index = chosen[j, peer]
                outgoing[peer, pl.ds(4 * j, 4), :] = atoms_held[index]
                cell = cells[index]
                local = ((cell >> 10) & 3) * 128 + ((cell >> 5) & 3) * 32 + (cell & 31)
                line = jnp.where(lane == j, jnp.where(counts[0, peer] > j, local, 512), line)
            cells_out[peer] = line
        return carry

    pl.semaphore_wait(barrier, len(lines))
    for r in range(1, subs):
        pl.semaphore_signal(ready, inc=1, device_id=beside(0, r), device_id_type=MESH)
    lax.fori_loop(0, slabs, pick, 0)
    pl.semaphore_wait(ready, subs - 1)

    def start(step):
        peer, target = peer_of(step)
        send(outgoing.at[peer], incoming.at[step], sent, got.at[step], target)
        send(cells_out.at[peer], cells_in.at[step], cell_sent, cell_got, target)

    in_groups(start)
    own = pltpu.make_async_copy(outgoing.at[me], incoming.at[0], got.at[0])
    own.start()
    cells_in[0] = cells_out[me]

    offsets = lax.broadcasted_iota(jnp.int32, (8, BLOCK), 0).astype(jnp.float32) - 1.0

    def spread(group, carry):
        for n in range(SENDERS):
            step = group * SENDERS + n
            pltpu.make_async_copy(incoming.at[step], incoming.at[step], got.at[step]).wait()
        parts = []
        for n in range(SENDERS):
            step = group * SENDERS + n
            for j in range(4):
                wx, wy, wz = (spline_rows(incoming[step, pl.ds(4 * j + d, 1), :], offsets) for d in range(3))
                charge = incoming[step, pl.ds(4 * j + 3, 1), :]
                high, low = halves(cross(wx, wy))
                slot = step * 4 + j
                across[slot, 0:64, :] = high
                across[slot, 64:128, :] = low
                along[slot] = wz
                both = jnp.concatenate(halves(wz * charge), axis=0)
                product = lax.dot_general(
                    jnp.concatenate([both, both], axis=1),
                    jnp.concatenate([high, low], axis=1),
                    (((1,), (1,)), ((), ())),
                    preferred_element_type=jnp.float32,
                )
                parts.append((step, j, product[0:8] + product[8:16]))
        for step, j, part in parts:
            patches[pl.ds(pl.multiple_of((j * devices + step) * 8, 8), 8), 0:64] = part
        return carry

    groups = devices // SENDERS
    lax.fori_loop(0, groups, spread, 0)
    others = pl.ds(1, devices - 1)
    pltpu.make_async_copy(cells_in.at[others], cells_in.at[others], cell_got).wait()
    cell_block[...] = cells_in[:, 0, :]
    scalars = pltpu.make_async_copy(cell_block, cell_scalars, scalar_sem)
    scalars.start()

    slots_across = cell_block[...].T
    cell_number = lax.broadcasted_iota(jnp.int32, (512, devices), 0)
    member = jnp.concatenate(
        [(cell_number == slots_across[j : j + 1, :]).astype(jnp.float32).astype(jnp.bfloat16) for j in range(4)], axis=1
    )
    for k in range(8):
        sums = dot(member, jnp.concatenate(halves(patches[pl.ds(k, devices * 4, stride=8), :]), axis=1))
        cell_sums[k] = sums[:, :128] + sums[:, 128:]
    partial[...] = jnp.zeros_like(partial)
    loads[0].wait()
    loads[1].wait()
    for a in range(4):
        for b in range(4):
            first = (a * 4 + b) * 32
            column = cell_sums[:, first : first + 32, :].reshape(256, 128)
            planes = dot_left(place_in, column).T
            for i in range(7):
                partial[4 * a + i, 4 * b : 4 * b + 8, :] += planes[8 * i : 8 * i + 8]

    loads = loads_of_levels
    down, up, down_z, up_z, enter, leave, enter_z, leave_z, mode_x, back_x, spectrum, near, near_middle = held[2:]

    for n in (4, 6):
        loads[n].wait()
    rows = 16 * subs
    spread_modes = dot_left(enter, dot_right(partial[...].reshape(19 * 24, GZ), enter_z))
    group_of_lane = lax.broadcasted_iota(jnp.int32, (rows, GZ), 1) // 32
    packed = spread_modes[0:rows]
    for j in range(1, 4):
        packed = jnp.where(group_of_lane == j, spread_modes[j * rows : (j + 1) * rows], packed)
    modes_out[...] = packed.reshape(subs, 16, GZ)
    mode_copies = [
        send(modes_out.at[r], modes_in.at[subs - r], in_sent.at[r], in_got.at[subs - r], beside(0, r))
        for r in range(1, subs)
    ]

    edge[...] = partial[:, 13:21, :]

    low, high = pl.ds(0, 6), pl.ds(13, 6)
    near_rows = pl.ds(0, 8)
    sources = [
        partial.at[high], partial.at[low], edge, partial.at[:, near_rows, :],
        edge.at[high], partial.at[high, near_rows, :], edge.at[low], partial.at[low, near_rows, :],
    ]
    fine_copies = [
        send(source, fine_in[n], fine_sent.at[n], fine_got.at[n], beside(*SIDES[n])) for n, source in enumerate(sources)
    ]

    for n in (0, 2):
        loads[n].wait()
    middle[...] = dot_left(down, dot_right(partial[...].reshape(19 * 24, GZ), down_z)).reshape(13, 16, GZ)

    def pair_planes(values, count):
        return values[:count] + pltpu.roll(values[count:], 64, 2)

    high_x = pair_planes(middle[5:13], 4)
    low_x = pair_planes(middle[0:8], 4)
    rim_x[0] = high_x
    rim_x[1] = low_x
    rim_y[0, 0:7] = middle[0:7, 5:13, :]
    rim_y[0, 0:6] += pltpu.roll(middle[7:13, 5:13, :], 64, 2)
    rim_y[1, 0:7] = middle[0:7, 0:8, :]
    rim_y[1, 0:6] += pltpu.roll(middle[7:13, 0:8, :], 64, 2)
    rim_corner[0] = high_x[:, 5:13, :]
    rim_corner[1] = low_x[:, 5:13, :]
    sources = [
        rim_x.at[0], rim_x.at[1], rim_y.at[0], rim_y.at[1],
        rim_corner.at[0], rim_x.at[0, :, near_rows, :], rim_corner.at[1], rim_x.at[1, :, near_rows, :],
    ]
    middle_copies = [
        send(source, middle_in[n], middle_sent.at[n], middle_got.at[n], beside(*SIDES[n]))
        for n, source in enumerate(sources)
    ]

    for copy in mode_copies:
        copy.wait_recv()
    total = modes_out[0]
    for r in range(1, subs):
        total = total + modes_in[r]
    line_out[...] = total
    line_copies = [
        send(line_out, line_in.at[slabs - r], line_sent.at[r], line_got.at[slabs - r], beside(r, 0))
        for r in range(1, slabs)
    ]
    line_in[0] = total

    fine[...] = jnp.zeros_like(fine)
    fine[3:22, 3:27, :] = partial[...]
    for n, (dx, dy) in enumerate(SIDES):
        fine_copies[n].wait_recv()
        first = {1: 0, -1: 19, 0: 3}
        size = fine_in[n].shape
        x, y = first[dx], first[dy]
        fine[x : x + size[0], y : y + size[1], :] += fine_in[n][...]

    fold_columns(fine, columns, 19, 24)
    loads[11].wait()
    fine_short = short_range(columns, near, 19, 24)

    for n in (8, 9, 10):
        loads[n].wait()
    for copy in line_copies:
        copy.wait_recv()
    in_modes = dot_left(mode_x, line_in[...].reshape(slabs * 16, GZ)) * spectrum[...]
    back_out[...] = dot_left(back_x, in_modes)
    back_copies = [
        send(back_out, back_in.at[subs - r], back_sent.at[r], back_got.at[subs - r], beside(0, r))
        for r in range(1, subs)
    ]
    back_in[0] = back_out[...]

    middle_wide[...] = jnp.zeros_like(middle_wide)
    middle_wide[3:16, 3:19, :] = middle[...]
    for n, (dx, dy) in enumerate(SIDES):
        middle_copies[n].wait_recv()
        first = {1: 0, -1: 11, 0: 3}
        size = middle_in[n].shape
        x, y, span = first[dx], first[dy], size[0] if dx else 6
        middle_wide[x : x + size[0], y : y + size[1], :] += middle_in[n][...]
        x = x + size[0]
        middle_wide[x : x + span, y : y + size[1], :] += pltpu.roll(middle_in[n][0:span], 64, 2)
    fold_columns(middle_wide, middle_columns, 13, 16)
    loads[12].wait()
    middle_short = short_range(middle_columns, near_middle, 13, 16)

    for n in (1, 3):
        loads[n].wait()
    grid = fine_short + dot_right(dot_left(up, middle_short), up_z)
    for n in (5, 7):
        loads[n].wait()
    for copy in back_copies:
        copy.wait_recv()
    wide = dot_right(back_in[...].reshape(rows, GZ), leave_z)
    grid = grid + dot_left(leave, jnp.concatenate([wide[:, j * GZ : (j + 1) * GZ] for j in range(4)], axis=0))
    for copy in fine_copies:
        copy.wait_send()
    lattice = partial
    lattice[...] = grid.reshape(19, 24, GZ)
    grid_part[...] = lattice[1:17, 1:17, :]
    grid_copy = pltpu.make_async_copy(grid_part, grid_out, out_sem.at[0])
    grid_copy.start()

    scalars.wait()
    forms = (((1,), (1,)), ((), ()))
    for a in range(4):
        for b in range(4):
            rows_of = [lattice[4 * a + i, 4 * b : 4 * b + 8, :] for i in range(7)] + [jnp.zeros((8, 128), jnp.float32)]
            high, low = halves(jnp.concatenate(rows_of, axis=0))
            column = lax.dot_general(place_back[...], high, forms, preferred_element_type=jnp.float32)
            column = column + lax.dot_general(place_back[...], low, forms, preferred_element_type=jnp.float32)
            first = (a * 4 + b) * 32
            pair = jnp.concatenate(halves(column.reshape(32, 8, 64)), axis=1)
            table[first : first + 32] = jnp.concatenate([pair, pair], axis=2)
    table[512] = jnp.zeros((16, 128), jnp.bfloat16)

    def interpolate(group, carry):
        for n in range(2 * SENDERS):
            step = group * 2 * SENDERS + n
            sender = lax.rem(me + devices - lax.rem(step * STRIDE, devices), devices)
            for j in range(0, 4, 2):
                slot = step * 4 + j
                first, second = (table[cell_scalars[step, j + m]] for m in range(2))
                none = jnp.zeros_like(first)
                product = dot(
                    jnp.concatenate(
                        [jnp.concatenate([first, none], axis=1), jnp.concatenate([none, second], axis=1)], axis=0
                    ),
                    across[pl.ds(slot, 2)].reshape(256, BLOCK),
                )
                for m in range(2):
                    part = (product[16 * m : 16 * m + 8] + product[16 * m + 8 : 16 * m + 16]) * along[slot + m]
                    potentials[pl.ds(sender * 4 + j + m, 1), :] = jnp.sum(part, axis=0, keepdims=True)
        return carry

    lax.fori_loop(0, groups // 2, interpolate, 0)
    potentials_copy = pltpu.make_async_copy(potentials, potentials_out, out_sem.at[1])
    potentials_copy.start()
    pltpu.make_async_copy(outgoing.at[others], outgoing.at[others], sent).wait()
    pltpu.make_async_copy(cells_out.at[others], cells_out.at[others], cell_sent).wait()
    for copy in middle_copies + mode_copies + line_copies + back_copies:
        copy.wait_send()
    grid_copy.wait()
    potentials_copy.wait()


def whole(chosen, counts, cells, atoms, slabs, subs):
    tables = [jnp.asarray(table) for table in level_tables(slabs, subs)]
    devices = slabs * subs
    held = [
        pltpu.VMEM(table.shape[1:] if n in PER_SUB else table.shape, table.dtype) for n, table in enumerate(tables)
    ]
    f32 = lambda *shape: pltpu.VMEM(shape, jnp.float32)
    i32 = lambda *shape: pltpu.VMEM(shape, jnp.int32)
    fine_in = [(6, 24), (6, 24), (19, 8), (19, 8)] + [(6, 8)] * 4
    middle_in = [(4, 16), (4, 16), (7, 8), (7, 8)] + [(4, 8)] * 4
    dma = lambda count: pltpu.SemaphoreType.DMA((count,))
    return pl.pallas_call(
        functools.partial(whole_kernel, slabs, subs),
        out_shape=(
            jax.ShapeDtypeStruct((devices * 4, BLOCK), jnp.float32),
            jax.ShapeDtypeStruct((GX, GY, GZ), jnp.float32),
        ),
        in_specs=[SMEM, SMEM, SMEM] + [ANY] * (1 + len(tables)),
        out_specs=(ANY, ANY),
        scratch_shapes=held
        + [
            f32(*atoms.shape),
            f32(devices, 16, BLOCK),
            f32(devices, 16, BLOCK),
            i32(devices, 1, BLOCK),
            i32(devices, 1, BLOCK),
            i32(devices, BLOCK),
            pltpu.SMEM((devices, BLOCK), jnp.int32),
            pltpu.VMEM((devices * 4, 128, BLOCK), jnp.bfloat16),
            f32(devices * 4, 8, BLOCK),
            f32(devices * 4 * 8, 128),
            f32(8, 512, 128),
            f32(19, 24, GZ),
            pltpu.VMEM((513, 16, 128), jnp.bfloat16),
            f32(devices * 4, BLOCK),
            f32(GX, GY, GZ),
        ]
        + [f32(*shape, GZ) for shape in fine_in + middle_in]
        + [
            f32(19, 8, GZ),
            f32(13, 16, GZ),
            f32(25, 32, GZ),
            f32(19, 24, GZ),
            f32(4, 25, 24, GZ),
            f32(4, 19, 16, GZ),
            f32(2, 4, 16, GZ),
            f32(2, 7, 8, GZ),
            f32(2, 4, 8, GZ),
            f32(subs, 16, GZ),
            f32(subs, 16, GZ),
            f32(16, GZ),
            f32(slabs, 16, GZ),
            f32(16, GZ),
            f32(subs, 16, GZ),
        ]
        + [dma(2), pltpu.SemaphoreType.REGULAR, dma(len(tables)), pltpu.SemaphoreType.DMA, pltpu.SemaphoreType.DMA, dma(devices)]
        + [pltpu.SemaphoreType.DMA] * 3
        + [dma(8), dma(8), dma(8), dma(8)]
        + [dma(subs), dma(subs), dma(slabs), dma(slabs), dma(subs), dma(subs)],
        compiler_params=pltpu.CompilerParams(collective_id=0, has_side_effects=True, vmem_limit_bytes=60 << 20),
        name="multilevel",
    )(chosen, counts, cells, atoms, *tables)


def finish_kernel(potentials, grid, potentials_out, grid_out, *rest):
    values, sems = rest[:2], rest[2]
    loads = [pltpu.make_async_copy(ref, values[n], sems.at[n]) for n, ref in enumerate((potentials, grid))]
    stores = [pltpu.make_async_copy(values[n], ref, sems.at[n]) for n, ref in enumerate((potentials_out, grid_out))]
    for load in loads:
        load.start()
    for load, store in zip(loads, stores):
        load.wait()
        store.start()
    for store in stores:
        store.wait()


def finish(potentials, grid):
    return pl.pallas_call(
        finish_kernel,
        out_shape=tuple(jax.ShapeDtypeStruct(value.shape, value.dtype) for value in (potentials, grid)),
        in_specs=[ANY, ANY],
        out_specs=(ANY, ANY),
        scratch_shapes=[pltpu.VMEM(value.shape, value.dtype) for value in (potentials, grid)]
        + [pltpu.SemaphoreType.DMA((2,))],
        compiler_params=pltpu.CompilerParams(vmem_limit_bytes=60 << 20),
        name="finish",
    )(potentials, grid)


def body(atom_data, block_cell, send_list, send_count):
    slabs, subs = lax.axis_size("slab"), lax.axis_size("sub")
    return finish(*whole(send_list[0].T, send_count, block_cell, atom_data, slabs, subs))


def solution(mesh):
    placed = (
        P(("slab", "sub"), None, None),
        P(("slab", "sub")),
        P(("slab", "sub"), None, None),
        P(("slab", "sub"), None),
    )
    return jax.shard_map(
        body,
        mesh=mesh,
        in_specs=placed,
        out_specs=(P(("slab", "sub"), None), P("slab", "sub", None)),
        check_vma=False,
    )
```
